128 devices in a mesh: gx: 32 (over y, z, core), gy: 4 (over x).
Axes of the slice: x: 4, y: 4, z: 4, core: 2. Of those that a mesh axis runs over, the one named last changes fastest.
Arguments:
- block_input: bfloat16 [16384, 768], P('gx', 'gy'), may hold values from -6 to 6
- cotangent: bfloat16 [16384, 768], P('gx', 'gy'), may hold values from -6 to 6
- doc_ids: int32 [16384], P('gx'), may hold values from 0 to 127, never falling along the last dimension, each value on 1 to 256 neighbouring positions
- routes: int32 [16384, 2], P('gx'), may hold values from 0 to 63, all different within a row; in each aligned block of 512 rows (0 to 511, 512 to 1023, ...) at most 18 rows name the same one
- qkv_weight: bfloat16 [2, 768, 3, 768], P(None, 'gx', None, 'gy'), may hold values from -0.21875 to 0.21875
- out_weight: bfloat16 [2, 768, 768], P(None, 'gx', 'gy'), may hold values from -0.625 to 0.625
- rel_bias: float32 [2, 12, 32], P(None, 'gy'), may hold values from -3 to 3
- norm_gain: float32 [2, 2, 768], P(None, None, 'gy'), may hold values from 0.5 to 1.5
- ff_in: bfloat16 [768, 3072], P('gx', 'gy'), may hold values from -0.21875 to 0.21875
- ff_out: bfloat16 [768, 3072], P('gx', 'gy'), may hold values from -0.109375 to 0.109375
- router: bfloat16 [768, 64], P('gx'), may hold values from -0.15625 to 0.15625
- expert_in: bfloat16 [64, 768, 3072], P('gx', None, 'gy'), may hold values from -0.21875 to 0.21875
- expert_out: bfloat16 [64, 3072, 768], P('gx', 'gy'), may hold values from -0.109375 to 0.109375
Outputs:
- block_output: bfloat16 [16384, 768], P('gx', 'gy')
- input_grad: bfloat16 [16384, 768], P('gx', 'gy')
- qkv_grad: float32 [2, 768, 3, 768], P(None, 'gx', None, 'gy')
- out_grad: float32 [2, 768, 768], P(None, 'gx', 'gy')
- bias_grad: float32 [2, 12, 32], P(None, 'gy')
- gain_grad: float32 [2, 2, 768], P(None, None, 'gy')
- ff_in_grad: float32 [768, 3072], P('gx', 'gy')
- ff_out_grad: float32 [768, 3072], P('gx', 'gy')
- router_grad: float32 [768, 64], P('gx')
- expert_in_grad: float32 [64, 768, 3072], P('gx', None, 'gy')
- expert_out_grad: float32 [64, 3072, 768], P('gx', 'gy')
The draws below stay inside these ranges and needn't reach their ends.
Inputs may be any that keep to these rules, and one draw needn't show every extreme that they name: `routes`: each row names 2 different experts. Within the rows of one sequence (aligned blocks of 512 rows) no expert is named more than 18 times, a bound that some block reaches. `doc_ids`: document numbers never fall along the tokens; a document has at most 256 tokens and one has exactly that many.
All inputs are finite; a program needn't handle non-finite values.
Results may differ from the reference program's by a relative error of at most 0.025.
Values may be sent and summed in bfloat16 or wider, within the bound.
A program may use at most 192 MiB of HBM per device.

```python
import math
import jax
import jax.numpy as jnp
import numpy as np
from jax import lax

D = 768
H = 12
HD = 64
FF = 3072
EXPERTS = 64
TOP = 2
NB = 32
LAYERS = 2
TOK_GRP = 512
TOKENS = 16384
CAP = 18
N_GX = 32


def block_levels(rng, extent, cuts, least, top_value):
    level, own = 1.0, jax.random.fold_in(rng, 6)
    for position, parts in cuts:
        heights = jnp.exp(jax.random.uniform(jax.random.fold_in(own, position), (parts,), jnp.float32, least / len(cuts), top_value / len(cuts)))
        level = level * jnp.repeat(heights, extent[position] // parts).reshape([-1 if axis == position else 1 for axis in range(len(extent))])
    return level


def length_profile(number_of, total, bound, skew):
    portions = [(1 << 20) // math.isqrt(grade ** skew) + 1 for grade in range(2, number_of + 1)]
    spare, given = total - bound - (number_of - 1), [1] * (number_of - 1)
    while spare > 0:
        free = [i for i in range(number_of - 1) if given[i] < bound]
        whole, left = sum([portions[i] for i in free]), spare
        for i in free:
            extra = min(bound - given[i], max(1, left * portions[i] // whole), spare)
            given[i] = given[i] + extra
            spare = spare - extra
    return np.array([bound] + given)


def ragged(own_key, count, total, most, lean):
    if count == 2:
        one = jax.random.randint(own_key, (), max(1, total - most), min(most, total - 1) + 1)
        return jnp.stack([one, total - one])
    lengths = jnp.asarray(length_profile(count, total, most, lean), jnp.int32)
    couples = (count - 1) // 2
    giver, taker = lengths[1:1 + 2 * couples:2], lengths[2:2 + 2 * couples:2]
    margin = jnp.minimum(giver - 1, most - taker)
    moved = jax.random.randint(jax.random.fold_in(own_key, 1), (couples,), 0, 1 << 20) % (margin + 1)
    lengths = lengths.at[1:1 + 2 * couples:2].set(giver - moved).at[2:2 + 2 * couples:2].set(taker + moved)
    return lengths[jax.random.permutation(jax.random.fold_in(own_key, 2), count)]


def shared_out(own_key, own, number, rows, amount, top, reach, slope):
    order = jax.random.permutation(own_key, amount)
    crowded, common = portions_of(amount, rows * top, reach, slope, True), portions_of(amount, rows * top, reach, slope, False)
    places = jnp.arange(amount)

    def named(sizes, turn):
        used = int((sizes > 0).sum())
        fixed = max(1, used // 4)
        shifted = fixed + (places - fixed + turn * (used - fixed)) % max(1, amount - fixed)
        return jnp.zeros((amount,), jnp.int32).at[order[jnp.where(places < fixed, places, shifted)]].set(jnp.asarray(sizes, jnp.int32))

    sizes = jnp.where(number % 4 == 0, named(crowded, number // 4), named(common, number - number // 4 - 1))
    mixed = jax.random.permutation(jax.random.fold_in(own, 3), amount)
    source_of, sink = mixed[0:amount // 2 * 2:2], mixed[1:amount // 2 * 2:2]
    room = jnp.minimum(sizes[source_of] - 1, reach - sizes[sink]) // 2
    room = jnp.where((source_of == order[0]) | (sink == order[0]) | (sizes[sink] == 0), 0, jnp.maximum(room, 0))
    shifted = jax.random.randint(jax.random.fold_in(own, 4), (amount // 2,), 0, 1 << 20) % (room + 1)
    sizes = sizes.at[source_of].add(-shifted).at[sink].add(shifted)
    items = jnp.searchsorted(jnp.cumsum(sizes), jnp.arange(rows * top), side="right").astype(jnp.int32)
    listing = items.reshape(top, rows).T
    listing = listing[jax.random.permutation(jax.random.fold_in(own, 1), rows)]
    turn = jax.random.randint(jax.random.fold_in(own, 2), (rows, 1), 0, top)
    return jnp.take_along_axis(listing, (jnp.arange(top)[None, :] + turn) % top, axis=1)


def portions_of(amount, total, reach, skew, full):
    portions = [(1 << 20) // math.isqrt(rank ** skew) + 1 for rank in range(1, amount + 1)]
    largest = reach if full else min(reach, max(-(-total // amount), total * portions[0] // sum(portions)))
    least = 1 if total - largest >= amount - 1 else 0
    holding, rest = [largest] + [least] * (amount - 1), total - largest - least * (amount - 1)
    while rest > 0:
        free = [i for i in range(1, amount) if holding[i] < largest] or [i for i in range(1, amount) if holding[i] < reach]
        mass, remaining = sum([portions[i] for i in free]), rest
        for i in free:
            more = min(reach - holding[i], max(1, remaining * portions[i] // mass), rest)
            holding[i] = holding[i] + more
            rest = rest - more
    return np.array(holding)


def scatter_about(key, extent, spread, most, cuts=(), kind=jnp.bfloat16):
    level = block_levels(key, extent, cuts, -0.22, 0.18) if cuts else 1.0
    drawn = jax.random.normal(key, extent, jnp.float32) * spread * level
    return jnp.minimum(jnp.maximum(drawn, -most), most).astype(kind)


def setup_inputs(seed: int = 0) -> dict:
    streams_of = jax.random.split(jax.random.key(seed), 14)
    block_input = scatter_about(streams_of[0], (TOKENS, D), 1.0, 6.0, ((0, 32), (1, 4)))
    cotangent = scatter_about(streams_of[1], (TOKENS, D), 1.0, 6.0, ((0, 32), (1, 4)))
    doc_ids = jnp.searchsorted(jnp.cumsum(ragged(streams_of[2], 4 * N_GX, TOKENS, TOK_GRP // 2, 1)), jnp.arange(TOKENS), side="right").astype(jnp.int32)
    routes_keys = jax.random.split(jax.random.fold_in(streams_of[3], 1), TOKENS // TOK_GRP)
    routes_turns = jax.random.permutation(jax.random.fold_in(streams_of[3], 3), TOKENS // TOK_GRP)
    routes = jax.vmap(lambda own, number: shared_out(jax.random.fold_in(streams_of[3], 2), own, number, TOK_GRP, EXPERTS, TOP, CAP, 1))(routes_keys, routes_turns).reshape((TOKENS, TOP))
    qkv_weight = scatter_about(streams_of[4], (LAYERS, D, 3, D), D ** -0.5, 0.21875, ((1, 32), (3, 4)))
    out_weight = scatter_about(streams_of[5], (LAYERS, D, D), (D // 8) ** -0.5, 0.625, ((1, 32), (2, 4)))
    rel_bias = scatter_about(streams_of[6], (LAYERS, H, NB), 1.0, 3.0, ((1, 4),), jnp.float32)
    norm_gain = jnp.clip(1.0 + 0.1 * jax.random.normal(streams_of[7], (LAYERS, 2, D), jnp.float32), 0.5, 1.5)
    ff_in = scatter_about(streams_of[8], (D, FF), D ** -0.5, 0.21875, ((0, 32), (1, 4)))
    ff_out = scatter_about(streams_of[9], (D, FF), FF ** -0.5, 0.109375, ((0, 32), (1, 4)))
    router = scatter_about(streams_of[10], (D, EXPERTS), (2 * D) ** -0.5, 0.15625, ((0, 32),))
    expert_in = scatter_about(streams_of[11], (EXPERTS, D, FF), D ** -0.5, 0.21875, ((0, 32), (2, 4)))
    expert_out = scatter_about(streams_of[12], (EXPERTS, FF, D), FF ** -0.5, 0.109375, ((0, 32), (1, 4)))
    return {"block_input": block_input, "cotangent": cotangent, "doc_ids": doc_ids, "routes": routes, "qkv_weight": qkv_weight, "out_weight": out_weight, "rel_bias": rel_bias, "norm_gain": norm_gain, "ff_in": ff_in, "ff_out": ff_out, "router": router, "expert_in": expert_in, "expert_out": expert_out}


@jax.custom_vjp
def low(v):
    return lax.optimization_barrier(v.astype(jnp.bfloat16)).astype(jnp.float32)

@jax.custom_vjp
def low_back(v):
    return v

def low_keep(v):
    return (low(v), None)

def low_pass(kept, grad):
    return (grad,)

def back_keep(v):
    return (v, None)

def back_low(kept, grad):
    return (low(grad),)
low.defvjp(low_keep, low_pass)
low_back.defvjp(back_keep, back_low)
epsilon = 1e-06
highest = lax.Precision.HIGHEST
bucket_edges = [int(math.ceil(16.0 * 8.0 ** (step / 16.0))) for step in range(1, 16)]

def bucket_of(distance):
    nearby = jnp.clip(distance, 0, 16)
    beyond = jnp.zeros_like(distance)
    for edge in bucket_edges:
        beyond = beyond + (distance >= edge).astype(jnp.int32)
    return nearby + beyond

def gelu(value):
    return jax.nn.gelu(value, approximate=True)

def rms_norm(state, gain):
    scale = lax.rsqrt(lax.optimization_barrier(jnp.mean(state * state, axis=-1, keepdims=True)) + epsilon)
    return low(state * scale * gain)

def attention(normed, weight_qkv, weight_out, table, doc_ids):
    mixed = jnp.einsum('td,dsc->tsc', normed, weight_qkv, precision=highest)
    mixed = low(low_back(mixed))
    groups = TOKENS // TOK_GRP
    mixed = mixed.reshape(groups, TOK_GRP, 3, H, HD)
    documents = doc_ids.reshape(groups, TOK_GRP)
    places = jnp.arange(TOK_GRP, dtype=jnp.int32)
    distance = places[:, None] - places[None, :]
    bias = jnp.take(table, bucket_of(distance), axis=1)

    @jax.checkpoint
    def one_sequence(pieces):
        block, doc_row = pieces
        queries, keys, values = (block[:, 0], block[:, 1], block[:, 2])
        scores = jnp.einsum('qhd,khd->hqk', queries, keys, precision=highest) * 0.125 + bias
        allowed = (distance >= 0) & (doc_row[:, None] == doc_row[None, :])
        scores = low_back(jnp.where(allowed[None], scores, -1000000000.0))
        peak = lax.optimization_barrier(jnp.max(scores, axis=-1, keepdims=True))
        weights = jnp.exp(scores - peak)
        probs = weights / lax.optimization_barrier(jnp.sum(weights, axis=-1, keepdims=True))
        return jnp.einsum('hqk,khd->qhd', low(probs), values, precision=highest)
    context = lax.map(one_sequence, (mixed, documents)).reshape(TOKENS, D)
    context = low(low_back(context))
    return low_back(jnp.dot(context, weight_out.T, precision=highest))

def dense(normed, weight_in, weight_out):
    hidden = low_back(jnp.dot(normed, weight_in, precision=highest))
    return low_back(jnp.dot(low(gelu(hidden)), weight_out.T, precision=highest))

def experts(normed, router, expert_in, expert_out, routes):
    groups = TOKENS // TOK_GRP
    logits = jnp.dot(normed, router, precision=highest)
    picked = low_back(jnp.take_along_axis(logits, routes, axis=1))
    gates = jax.nn.softmax(picked, axis=-1)
    chosen = routes.reshape(groups, TOK_GRP * TOP)
    marks = (chosen[:, :, None] == jnp.arange(EXPERTS, dtype=jnp.int32)[None, None, :]).astype(jnp.int32)
    places = lax.optimization_barrier(jnp.sum(jnp.cumsum(marks, axis=1) * marks, axis=2)) - 1
    group_ids = jnp.arange(groups, dtype=jnp.int32)[:, None]
    slots = ((chosen * groups + group_ids) * CAP + places).reshape(-1).astype(jnp.int32)
    owners = jnp.arange(TOKENS * TOP, dtype=jnp.int32) // TOP
    rows_all = EXPERTS * groups * CAP
    source = jnp.full((rows_all,), TOKENS, jnp.int32).at[slots].set(owners)
    padded = jnp.concatenate([normed, jnp.zeros((1, D), normed.dtype)], axis=0)
    inputs = padded[source].reshape(EXPERTS, groups * CAP, D)

    @jax.checkpoint
    def one_expert(pieces):
        rows, weight_in, weight_out = pieces
        hidden = low_back(jnp.dot(rows, weight_in, precision=highest))
        return jnp.dot(low(gelu(hidden)), weight_out, precision=highest)
    results = lax.map(one_expert, (inputs, expert_in, expert_out)).reshape(rows_all, D)
    routed = low_back(results[slots].reshape(TOKENS, TOP, D))
    return lax.optimization_barrier(jnp.sum(gates[:, :, None] * routed, axis=1))

def reference(block_input, cotangent, doc_ids, routes, qkv_weight, out_weight, rel_bias, norm_gain, ff_in, ff_out, router, expert_in, expert_out):
    floats = tuple((item.astype(jnp.float32) for item in (block_input, qkv_weight, out_weight, rel_bias, norm_gain, ff_in, ff_out, router, expert_in, expert_out)))

    def forward(state, w_qkv, w_out, table, gains, f_in, f_out, w_router, e_in, e_out):
        state = state + attention(rms_norm(state, gains[0, 0]), w_qkv[0], w_out[0], table[0], doc_ids)
        state = state + dense(rms_norm(state, gains[0, 1]), f_in, f_out)
        state = state + attention(rms_norm(state, gains[1, 0]), w_qkv[1], w_out[1], table[1], doc_ids)
        state = state + experts(rms_norm(state, gains[1, 1]), w_router, e_in, e_out, routes)
        return state
    result, pull = jax.vjp(forward, *floats)
    grads = pull(cotangent.astype(jnp.float32))
    return (result.astype(jnp.bfloat16), grads[0].astype(jnp.bfloat16), grads[1], grads[2], grads[3], grads[4], grads[5], grads[6], grads[7], grads[8], grads[9])
```

```python
import functools
import math

import numpy as np

import jax
import jax.numpy as jnp
from jax import lax
from jax.experimental import pallas as pl
from jax.experimental.pallas import tpu as pltpu
from jax.sharding import PartitionSpec as P

NB = 32
D = 768
LOCAL = 192
SEQ = 512
HALF = 256
PACK = 384
ROWS = 24
HEADS = 3
HD = 64
SLOT = 24
SLOTS = 64 * SLOT
BF = jnp.bfloat16
F32 = jnp.float32
MESH = pl.DeviceIdType.MESH
VM = pl.BlockSpec(memory_space=pltpu.VMEM)
HB = pl.BlockSpec(memory_space=pl.ANY)
epsilon = 1e-06
highest = lax.Precision.HIGHEST
bucket_edges = [int(math.ceil(16.0 * 8.0 ** (step / 16.0))) for step in range(1, 16)]


def bucket_picks():
    distance = (SEQ - np.arange(SEQ)) % SEQ
    bucket = np.minimum(distance, 16)
    for edge in bucket_edges:
        bucket = bucket + (distance >= edge)
    return (bucket[None, :] == np.arange(NB)[:, None]).astype(np.float32)


def dot(a, b, ca, cb):
    return lax.dot_general(a, b, (((ca,), (cb,)), ((), ())), preferred_element_type=F32)


def unpack(p):
    return jnp.concatenate([p[:, :LOCAL], p[:, LOCAL:]], axis=0)


def pack(a):
    half = a.shape[0] // 2
    return jnp.concatenate([a[:half], a[half:]], axis=1)


def join(ref):
    return jnp.concatenate([unpack(ref[j]) for j in range(4)], axis=1)


def split_store(ref, a):
    for j in range(4):
        ref[j] = pack(a[:, LOCAL * j : LOCAL * (j + 1)])


def gain_row(ref, k):
    return jnp.concatenate([ref[j, k : k + 1, :LOCAL] for j in range(4)], axis=1)


def normalise(whole, gain):
    scale = lax.rsqrt(jnp.mean(whole * whole, axis=-1, keepdims=True) + epsilon)
    return (whole * scale * gain).astype(BF), scale


def norm_back(normed_grad, whole, scale, gain):
    weighted = normed_grad * gain
    inner = jnp.mean(weighted * whole, axis=-1, keepdims=True)
    state_grad = weighted * scale - whole * (scale * scale * scale * inner)
    gain_part = jnp.sum(normed_grad * whole * scale, axis=0, keepdims=True)
    return state_grad, gain_part


def gelu_both(v):
    c = math.sqrt(2.0 / math.pi)
    t = jnp.tanh(c * (v + 0.044715 * (v * v * v)))
    value = 0.5 * v * (1.0 + t)
    slope = 0.5 * (1.0 + t) + 0.5 * v * (1.0 - t * t) * (c * (1.0 + 3.0 * 0.044715 * (v * v)))
    return value, slope


def local_call(body, out, args, specs=None, vmem=48, **kw):
    return pl.pallas_call(
        body,
        out_shape=out,
        in_specs=[VM] * len(args) if specs is None else specs,
        out_specs=jax.tree.map(lambda _: VM, out),
        compiler_params=pltpu.CompilerParams(vmem_limit_bytes=vmem * 2**20),
        **kw,
    )(*args)


def shape(*dims, dtype=BF):
    return jax.ShapeDtypeStruct(dims, dtype)


def attn_fwd_body(layer, wp, gains, w, lines, doc_c, doc_r, pp, mixed_o, ctx_o, probs_o):
    whole = join(wp).astype(F32)
    normed, _ = normalise(whole, gain_row(gains, 2 * layer))
    mixed = dot(normed, w[:, :576], 1, 0).astype(BF)
    mixed_o[...] = mixed
    row = lax.broadcasted_iota(jnp.int32, (SEQ, SEQ), 0)
    col = lax.broadcasted_iota(jnp.int32, (SEQ, SEQ), 1)
    allowed = (col <= row) & (doc_c[...] == doc_r[...])
    context = []
    for h in range(HEADS):
        q = mixed[:, HD * h : HD * (h + 1)]
        k = mixed[:, LOCAL + HD * h : LOCAL + HD * (h + 1)]
        v = mixed[:, 2 * LOCAL + HD * h : 2 * LOCAL + HD * (h + 1)]
        line = jnp.broadcast_to(lines[layer, h : h + 1, :], (SEQ, SEQ))
        bias = pltpu.roll(line, 0, 1, stride=1, stride_axis=0)
        s = jnp.where(allowed, dot(q, k, 1, 1) * 0.125 + bias, -1000000000.0)
        e = jnp.exp(s - jnp.max(s, axis=-1, keepdims=True))
        p = (e * (1.0 / jnp.sum(e, axis=-1, keepdims=True))).astype(BF)
        probs_o[h] = p
        context.append(dot(p, v, 1, 0))
    ctx = jnp.concatenate(context, axis=1).astype(BF)
    ctx_o[...] = ctx
    split_store(pp, dot(ctx, w[:, 576:], 1, 1).astype(BF))


def attn_fwd(layer, wp, gains, w, lines, doc_c, doc_r):
    out = (
        shape(4, HALF, PACK),
        shape(SEQ, 576),
        shape(SEQ, LOCAL),
        shape(HEADS, SEQ, SEQ),
    )
    return local_call(
        functools.partial(attn_fwd_body, layer), out, (wp, gains, w, lines, doc_c, doc_r)
    )


def attn_bwd_body(layer, gp, wp, gains, w, mixed, ctx, probs, pp, dw, gain_o, cols_o):
    whole = join(wp).astype(F32)
    gain = gain_row(gains, 2 * layer)
    normed, scale = normalise(whole, gain)
    rows = join(gp)
    cg = dot(rows, w[:, 576:], 1, 0).astype(BF)
    dw[:, 576:] = dot(rows, ctx[...], 0, 0).astype(BF)
    row = lax.broadcasted_iota(jnp.int32, (SEQ, SEQ), 0)
    col = lax.broadcasted_iota(jnp.int32, (SEQ, SEQ), 1)
    flip = jnp.where(row + col == SEQ - 1, 1.0, 0.0).astype(BF)
    dq, dk, dv = [], [], []
    cols_o[...] = jnp.zeros_like(cols_o)
    for h in range(HEADS):
        q = mixed[:, HD * h : HD * (h + 1)]
        k = mixed[:, LOCAL + HD * h : LOCAL + HD * (h + 1)]
        v = mixed[:, 2 * LOCAL + HD * h : 2 * LOCAL + HD * (h + 1)]
        c = cg[:, HD * h : HD * (h + 1)]
        p = probs[h]
        pf = p.astype(F32)
        pg = dot(c, v, 1, 1)
        sg = (pf * (pg - jnp.sum(pf * pg, axis=-1, keepdims=True))).astype(BF)
        dq.append(dot(sg, k, 1, 0) * 0.125)
        dk.append(dot(sg, q, 0, 0) * 0.125)
        dv.append(dot(p, c, 0, 0))
        rolled = pltpu.roll(dot(flip, sg, 1, 0), 1, 1, stride=1, stride_axis=0)
        cols_o[h : h + 1, :] = jnp.sum(rolled, axis=0, keepdims=True)
    dmixed = jnp.concatenate(dq + dk + dv, axis=1).astype(BF)
    dw[:, :576] = dot(normed, dmixed, 0, 0).astype(BF)
    ng = dot(dmixed, w[:, :576], 1, 1)
    state_grad, gain_part = norm_back(ng, whole, scale, gain)
    split_store(pp, state_grad.astype(BF))
    gain_o[...] = gain_part


def attn_bwd(layer, gp, wp, gains, w, mixed, ctx, probs):
    out = (
        shape(4, HALF, PACK),
        shape(D, D),
        shape(1, D, dtype=F32),
        shape(8, SEQ, dtype=F32),
    )
    return local_call(
        functools.partial(attn_bwd_body, layer), out, (gp, wp, gains, w, mixed, ctx, probs)
    )


def ff_fwd_body(wp, gains, w_in, w_out, pp, pre_o):
    whole = join(wp).astype(F32)
    normed, _ = normalise(whole, gain_row(gains, 1))
    pre = dot(normed, w_in[...], 1, 0)
    pre_o[...] = pre
    active = gelu_both(pre)[0].astype(BF)
    split_store(pp, dot(active, w_out[...], 1, 1).astype(BF))


def ff_fwd(wp, gains, w_in, w_out):
    out = (shape(4, HALF, PACK), shape(SEQ, D, dtype=F32))
    return local_call(ff_fwd_body, out, (wp, gains, w_in, w_out))


def ff_bwd_body(gp, wp, gains, w_in, w_out, pre, pp, dw_in, dw_out, gain_o):
    whole = join(wp).astype(F32)
    gain = gain_row(gains, 1)
    normed, scale = normalise(whole, gain)
    rows = join(gp)
    value, slope = gelu_both(pre[...])
    dw_out[...] = dot(rows, value.astype(BF), 0, 0).astype(BF)
    hg = (slope * dot(rows, w_out[...], 1, 0)).astype(BF)
    dw_in[...] = dot(normed, hg, 0, 0).astype(BF)
    ng = dot(hg, w_in[...], 1, 1)
    state_grad, gain_part = norm_back(ng, whole, scale, gain)
    split_store(pp, state_grad.astype(BF))
    gain_o[...] = gain_part


def ff_bwd(gp, wp, gains, w_in, w_out, pre):
    out = (shape(4, HALF, PACK), shape(D, D), shape(D, D), shape(1, D, dtype=F32))
    return local_call(ff_bwd_body, out, (gp, wp, gains, w_in, w_out, pre))


def marks_of(routes, r):
    lane = lax.broadcasted_iota(jnp.int32, (SEQ, 128), 1)
    return lane == routes[:, r : r + 1]


def dispatch_body(wp, state, cot, gains, own_gain, router, routes, out, meta_o):
    whole = join(wp).astype(F32)
    normed, scale = normalise(whole, gain_row(gains, 3))
    logits = dot(normed, router[...], 1, 0)
    marks = [marks_of(routes, r) for r in range(2)]
    picked = [jnp.sum(jnp.where(m, logits, 0.0), axis=1, keepdims=True) for m in marks]
    top = jnp.maximum(picked[0], picked[1])
    weights = [jnp.exp(v - top) for v in picked]
    total = weights[0] + weights[1]
    gates = [v / total for v in weights]
    ones = (jnp.where(marks[0], 1.0, 0.0) + jnp.where(marks[1], 1.0, 0.0)).astype(BF)
    row = lax.broadcasted_iota(jnp.int32, (SEQ, SEQ), 0)
    col = lax.broadcasted_iota(jnp.int32, (SEQ, SEQ), 1)
    before = dot(jnp.where(col < row, 1.0, 0.0).astype(BF), ones, 1, 0)
    places = [jnp.sum(jnp.where(m, before, 0.0), axis=1, keepdims=True) for m in marks]
    slots = [
        places[r] + SLOT * routes[:, r : r + 1].astype(F32) for r in range(2)
    ]
    lane = lax.broadcasted_iota(jnp.int32, (SEQ, 128), 1)
    meta = jnp.zeros((SEQ, 128), F32)
    for index, value in enumerate(gates + slots):
        meta = jnp.where(lane == index, value, meta)
    meta_o[...] = meta
    turned = jnp.transpose(meta)
    own = (unpack(state[...]) * scale * own_gain[...]).astype(BF)
    cotangent = unpack(cot[...].astype(F32))
    sent = jnp.zeros((SLOTS, PACK), F32)
    place = lax.broadcasted_iota(jnp.int32, (SLOTS, SEQ), 0)
    for r in range(2):
        chosen = place == turned[2 + r : 3 + r, :].astype(jnp.int32)
        rows = jnp.concatenate([own, (gates[r] * cotangent).astype(BF)], axis=1)
        sent = sent + dot(jnp.where(chosen, 1.0, 0.0).astype(BF), rows, 1, 0)
    out[...] = sent.reshape(32, 2, SLOT, PACK).astype(BF)


def dispatch(wp, state, cot, gains, own_gain, router, routes):
    out = (shape(32, 2, SLOT, PACK), shape(SEQ, 128, dtype=F32))
    return local_call(dispatch_body, out, (wp, state, cot, gains, own_gain, router, routes))


def expert_body(arrived, w_in, w_out, back, dw_in, dw_out):
    halves = [arrived[j, :, 0].astype(F32).reshape(32 * SLOT, PACK).astype(BF) for j in range(4)]
    x = jnp.concatenate([a[:, :LOCAL] for a in halves], axis=1)
    g = jnp.concatenate([a[:, LOCAL:] for a in halves], axis=1)
    value, slope = gelu_both(dot(x, w_in[0], 1, 0))
    active = value.astype(BF)
    hg = (slope * dot(g, w_out[0], 1, 1)).astype(BF)
    result = dot(active, w_out[0], 1, 0)
    sent = dot(hg, w_in[0], 1, 1)
    for j in range(4):
        span = slice(LOCAL * j, LOCAL * (j + 1))
        both = jnp.concatenate([result[:, span], sent[:, span]], axis=1)
        back[j, :, 0] = both.reshape(32, SLOT, PACK).astype(BF)
    dw_out[0] = dot(active, g, 0, 0)
    dw_in[0] = dot(x, hg, 0, 0)


def expert(arrived, w_in, w_out):
    rows = pl.BlockSpec((4, 32, 1, SLOT, PACK), lambda e: (0, 0, e, 0, 0))
    weight = pl.BlockSpec((1, D, D), lambda e: (e, 0, 0))
    return pl.pallas_call(
        expert_body,
        grid=(2,),
        out_shape=(
            shape(4, 32, 2, SLOT, PACK),
            shape(2, D, D, dtype=F32),
            shape(2, D, D, dtype=F32),
        ),
        in_specs=[rows, weight, weight],
        out_specs=(rows, weight, weight),
        compiler_params=pltpu.CompilerParams(vmem_limit_bytes=56 * 2**20),
    )(arrived, w_in, w_out)


def combine_body(returned, meta, state, cot, out, tg_o, gate_o):
    values = returned[...].astype(F32).reshape(SLOTS, PACK).astype(BF)
    lane = lax.broadcasted_iota(jnp.int32, (SEQ, SLOTS), 1)
    total = unpack(state[...])
    cotangent = unpack(cot[...].astype(F32))
    token_grad = jnp.zeros((SEQ, LOCAL), F32)
    spread = jnp.zeros((SEQ, 128), F32)
    place = lax.broadcasted_iota(jnp.int32, (SEQ, 128), 1)
    for r in range(2):
        chosen = lane == meta[:, 2 + r : 3 + r].astype(jnp.int32)
        found = dot(jnp.where(chosen, 1.0, 0.0).astype(BF), values, 1, 0)
        routed = found[:, :LOCAL]
        token_grad = token_grad + found[:, LOCAL:]
        total = total + meta[:, r : r + 1] * routed
        spread = jnp.where(
            place == r, jnp.sum(cotangent * routed, axis=1, keepdims=True), spread
        )
    out[...] = total.astype(BF)
    tg_o[...] = pack(token_grad).astype(BF)
    gate_o[...] = jnp.transpose(spread)[:8]


def combine(returned, meta, state, cot):
    out = (shape(SEQ, LOCAL), shape(HALF, PACK), shape(8, SEQ, dtype=F32))
    return local_call(combine_body, out, (returned, meta, state, cot))


def router_body(tg, gate, meta, routes, wp, cp, gains, router, gp_o, grad_o, dr_o, gain_o):
    whole = join(wp).astype(F32)
    gain = gain_row(gains, 3)
    normed, scale = normalise(whole, gain)
    summed = gate[0] + gate[1] + gate[2] + gate[3]
    wide = jnp.concatenate([summed, jnp.zeros((120, SEQ), F32)], axis=0)
    turned = jnp.transpose(wide)
    gates = [meta[:, r : r + 1] for r in range(2)]
    gate_grad = [turned[:, r : r + 1] for r in range(2)]
    inner = gates[0] * gate_grad[0] + gates[1] * gate_grad[1]
    logit_grad = jnp.zeros((SEQ, 128), F32)
    for r in range(2):
        picked_grad = gates[r] * (gate_grad[r] - inner)
        logit_grad = logit_grad + jnp.where(marks_of(routes, r), picked_grad, 0.0)
    logit_grad = logit_grad.astype(BF)
    dr_o[...] = dot(normed, logit_grad, 0, 0).astype(BF)
    ng = join(tg).astype(F32) + dot(logit_grad, router[...], 1, 1)
    state_grad, gain_part = norm_back(ng, whole, scale, gain)
    gain_o[...] = gain_part * 0.25
    grad = join(cp).astype(F32) + state_grad
    split_store(grad_o, grad)
    split_store(gp_o, grad.astype(BF))


def router_bwd(tg, gate, meta, routes, wp, cp, gains, router):
    out = (
        shape(4, HALF, PACK),
        shape(4, HALF, PACK, dtype=F32),
        shape(D, 128),
        shape(1, D, dtype=F32),
    )
    return local_call(router_body, out, (tg, gate, meta, routes, wp, cp, gains, router))


def places_of():
    gx, gy = lax.axis_index("gx"), lax.axis_index("gy")
    return gx, gy, gx // 8, (gx // 2) % 4, gx % 2


def at(y, z, core):
    return (y * 4 + z) * 2 + core


def greet(peers):
    barrier = pltpu.get_barrier_semaphore()
    for peer in peers:
        pl.semaphore_signal(barrier, inc=1, device_id=peer, device_id_type=MESH)
    pl.semaphore_wait(barrier, len(peers))


def remote(src, dst, send, recv, peer):
    return pltpu.make_async_remote_copy(
        src_ref=src, dst_ref=dst, send_sem=send, recv_sem=recv, device_id=peer, device_id_type=MESH
    )


def gy_peers(gx, gy):
    return [(gx, (gy + d) % 4) for d in (1, 2, 3)]


def grid_peers(gx, gy, y, z, core):
    return (
        [(at((y + d) % 4, z, core), gy) for d in (1, 2, 3)]
        + [(at(y, (z + d) % 4, core), gy) for d in (1, 2, 3)]
        + [(at(y, z, 1 - core), gy)]
    )


def comm_call(body, out, args, scratch, collective_id, specs, out_specs, vmem=32):
    return pl.pallas_call(
        body,
        out_shape=out,
        in_specs=specs,
        out_specs=out_specs,
        scratch_shapes=scratch,
        compiler_params=pltpu.CompilerParams(
            collective_id=collective_id, has_side_effects=True, vmem_limit_bytes=vmem * 2**20
        ),
    )(*args)


DMA = pltpu.SemaphoreType.DMA
N_W = 5


def start_body(*refs):
    weights, (x, cot, gain) = refs[:N_W], refs[N_W : N_W + 3]
    outs = refs[N_W + 3 : 2 * N_W + 3]
    xw, cw, gw = refs[2 * N_W + 3 : 2 * N_W + 6]
    own, s1, r1, s2, r2, s3, r3, sx, rx = refs[2 * N_W + 6 :]
    gx, gy, y, z, core = places_of()
    greet(grid_peers(gx, gy, y, z, core) + gy_peers(gx, gy))

    rows_first, along = [], []
    for i in range(N_W):
        z_first = i % 2 == 0
        for d in (1, 2, 3):
            peer = (at(y, (z + d) % 4, core) if z_first else at((y + d) % 4, z, core), gy)
            copy = remote(
                weights[i], outs[i].at[y, z, core], s1.at[i, d - 1], r1.at[i, d - 1], peer
            )
            copy.start()
            rows_first.append(copy)
    kept = []
    for i in range(N_W):
        copy = pltpu.make_async_copy(weights[i], outs[i].at[y, z, core], own.at[i])
        copy.start()
        kept.append(copy)
    for k, (src, dst) in enumerate(((x, xw), (cot, cw), (gain, gw))):
        for d in (2, 1, 3):
            copy = remote(
                src, dst.at[gy], sx.at[k, d - 1], rx.at[k, d - 1], (gx, (gy + d) % 4)
            )
            copy.start()
            along.append(copy)
        dst[gy] = src[...]
    partner = (at(y, z, 1 - core), gy)
    second, third = [], []
    for i in range(N_W):
        z_first = i % 2 == 0
        kept[i].wait()
        for d in range(3):
            rows_first[3 * i + d].wait_recv()
        line = outs[i].at[y, :, core] if z_first else outs[i].at[:, z, core]
        for d in (1, 2, 3):
            peer = (at((y + d) % 4, z, core) if z_first else at(y, (z + d) % 4, core), gy)
            copy = remote(line, line, s2.at[i, d - 1], r2.at[i, d - 1], peer)
            copy.start()
            second.append(copy)
        copy = remote(line, line, s3.at[i, 0], r3.at[i, 0], partner)
        copy.start()
        third.append(copy)
    for i in range(N_W):
        z_first = i % 2 == 0
        for d in (1, 2, 3):
            second[3 * i + d - 1].wait_recv()
            line = (
                outs[i].at[(y + 4 - d) % 4, :, core]
                if z_first
                else outs[i].at[:, (z + 4 - d) % 4, core]
            )
            copy = remote(line, line, s3.at[i, d], r3.at[i, d], partner)
            copy.start()
            third.append(copy)
    for copy in rows_first + second:
        copy.wait_send()
    for copy in third + along:
        copy.wait()


def start_gather(weights, x, cot, gain):
    out = tuple(shape(4, 4, 2, *w.shape) for w in weights) + (
        shape(4, HALF, PACK),
        shape(4, HALF, PACK),
        shape(4, 8, 256, dtype=F32),
    )
    scratch = [
        DMA((N_W,)),
        DMA((N_W, 3)),
        DMA((N_W, 3)),
        DMA((N_W, 3)),
        DMA((N_W, 3)),
        DMA((N_W, 4)),
        DMA((N_W, 4)),
        DMA((3, 3)),
        DMA((3, 3)),
    ]
    return comm_call(
        start_body,
        out,
        (*weights, x, cot, gain),
        scratch,
        0,
        [HB] * N_W + [VM] * 3,
        tuple([HB] * N_W + [VM] * 3),
    )


CHUNKS = 2


def turn_body(pick, pp, local, new, out, recv, s1, r1, s2, r2):
    gx, gy = lax.axis_index("gx"), lax.axis_index("gy")
    greet(gy_peers(gx, gy))
    size = HALF // CHUNKS
    first, second = [], []
    for c in range(CHUNKS):
        rows = pl.ds(c * size, size)
        for d in (2, 1, 3):
            peer = (gy + d) % 4
            copy = remote(
                pp.at[peer, rows],
                recv.at[d - 1, rows],
                s1.at[d - 1, c],
                r1.at[d - 1, c],
                (gx, peer),
            )
            copy.start()
            first.append(copy)
    for c in range(CHUNKS):
        rows = pl.ds(c * size, size)
        for copy in first[3 * c : 3 * c + 3]:
            copy.wait_recv()
        base = local[gy, rows] if pick else local[rows]
        total = base + pp[gy, rows].astype(F32)
        for d in range(3):
            total = total + recv[d, rows].astype(F32)
        new[rows] = total
        out[gy, rows] = total.astype(BF)
        for d in (2, 1, 3):
            copy = remote(
                out.at[gy, rows],
                out.at[gy, rows],
                s2.at[d - 1, c],
                r2.at[d - 1, c],
                (gx, (gy + d) % 4),
            )
            copy.start()
            second.append(copy)
    for copy in first:
        copy.wait_send()
    for copy in second:
        copy.wait()


def turn(pp, local):
    pick = local.ndim == 3
    return comm_call(
        functools.partial(turn_body, pick),
        (shape(HALF, PACK, dtype=F32), shape(4, HALF, PACK)),
        (pp, local),
        [
            pltpu.VMEM((3, HALF, PACK), BF),
            DMA((3, CHUNKS)),
            DMA((3, CHUNKS)),
            DMA((3, CHUNKS)),
            DMA((3, CHUNKS)),
        ],
        2 if pick else 1,
        [VM, VM],
        (VM, VM),
    )


def gather_body(tg, gate, tw, gw, sx, rx):
    gx, gy = lax.axis_index("gx"), lax.axis_index("gy")
    greet(gy_peers(gx, gy))
    copies = []
    for k, (src, dst) in enumerate(((gate, gw), (tg, tw))):
        for d in (2, 1, 3):
            copy = remote(src, dst.at[gy], sx.at[k, d - 1], rx.at[k, d - 1], (gx, (gy + d) % 4))
            copy.start()
            copies.append(copy)
        dst[gy] = src[...]
    for copy in copies:
        copy.wait()


def gather_tokens(tg, gate):
    return comm_call(
        gather_body,
        (shape(4, HALF, PACK), shape(4, 8, SEQ, dtype=F32)),
        (tg, gate),
        [DMA((2, 3)), DMA((2, 3))],
        3,
        [VM, VM],
        (VM, VM),
    )


def to_experts_body(sent, out, own, sa, ra, sg, rg):
    gx, gy = lax.axis_index("gx"), lax.axis_index("gy")
    greet(gy_peers(gx, gy) + [((gx + k) % 32, gy) for k in range(1, 32)])
    keep = pltpu.make_async_copy(sent.at[gx], out.at[gy, gx], own)
    keep.start()

    def push(k, carry):
        peer = (gx + k) % 32
        remote(sent.at[peer], out.at[gy, gx], sa, ra.at[k], (peer, gy)).start()
        return carry

    lax.fori_loop(1, 32, push, 0)
    keep.wait()

    def forward(source):
        for d in (2, 1, 3):
            remote(
                out.at[gy, source],
                out.at[gy, source],
                sg.at[d - 1],
                rg.at[d - 1],
                (gx, (gy + d) % 4),
            ).start()

    forward(gx)

    def relay(k, carry):
        source = (gx + 32 - k) % 32
        remote(sent.at[0], out.at[gy, source], sa, ra.at[k], (gx, gy)).wait_recv()
        forward(source)
        return carry

    lax.fori_loop(1, 32, relay, 0)
    many = sent.at[pl.ds(0, 31)]
    remote(many, many, sa, ra.at[0], (gx, gy)).wait_send()
    for d in (1, 2, 3):
        remote(out.at[gy], out.at[(gy + 4 - d) % 4], sg.at[d - 1], rg.at[d - 1], (gx, gy)).wait()


def to_experts(sent):
    return comm_call(
        to_experts_body,
        shape(4, 32, 2, SLOT, PACK),
        (sent,),
        [DMA(()), DMA(()), DMA((32,)), DMA((3,)), DMA((3,))],
        4,
        [HB],
        HB,
    )


GROUP = 4
GROUPS = 32 // GROUP


def from_experts_body(back, out, recv, total, s1, r1, s2, r2):
    gx, gy = lax.axis_index("gx"), lax.axis_index("gy")
    greet(gy_peers(gx, gy) + [((gx + k) % 32, gy) for k in range(1, 32)])

    def group(c):
        return pl.ds(((c + gx // GROUP) % GROUPS) * GROUP, GROUP)

    def push(c, carry):
        for d in (2, 1, 3):
            peer = (gy + d) % 4
            remote(
                back.at[peer, group(c)],
                recv.at[d - 1, group(c)],
                s1.at[d - 1],
                r1.at[d - 1, c],
                (gx, peer),
            ).start()
        return carry

    lax.fori_loop(0, GROUPS, push, 0)

    def reduce(c, carry):
        rows = group(c)
        for d in (1, 2, 3):
            remote(
                back.at[0, rows], recv.at[d - 1, rows], s1.at[d - 1], r1.at[d - 1, c], (gx, gy)
            ).wait_recv()
        value = back[gy, rows].astype(F32)
        for d in range(3):
            value = value + recv[d, rows].astype(F32)
        total[rows] = value.astype(BF)

        def send(i, inner):
            peer = ((c + gx // GROUP) % GROUPS) * GROUP + i

            @pl.when(peer != gx)
            def _():
                remote(total.at[peer], out.at[gx], s2, r2.at[gx], (peer, gy)).start()

            @pl.when(peer == gx)
            def _():
                out[gx] = total[gx]

            return inner

        return lax.fori_loop(0, GROUP, send, carry)

    lax.fori_loop(0, GROUPS, reduce, 0)
    for d in (1, 2, 3):
        remote(back.at[0], recv.at[d - 1], s1.at[d - 1], r1.at[0, 0], (gx, gy)).wait_send()
    many = total.at[pl.ds(0, 31)]
    remote(many, many, s2, r2.at[0], (gx, gy)).wait_send()

    def finish(k, carry):
        source = (gx + k) % 32
        remote(total.at[0], out.at[source], s2, r2.at[source], (gx, gy)).wait_recv()
        return carry

    lax.fori_loop(1, 32, finish, 0)


def from_experts(back):
    return comm_call(
        from_experts_body,
        shape(32, 2, SLOT, PACK),
        (back,),
        [
            pltpu.VMEM((3, 32, 2, SLOT, PACK), BF),
            pltpu.VMEM((32, 2, SLOT, PACK), BF),
            DMA((3,)),
            DMA((3, GROUPS)),
            DMA(()),
            DMA((32,)),
        ],
        5,
        [VM],
        VM,
        vmem=48,
    )


def last_body(*refs):
    parts, (pp, local, small) = refs[:N_W], refs[N_W : N_W + 3]
    outs = refs[N_W + 3 : 2 * N_W + 3]
    grad_o, small_o = refs[2 * N_W + 3 : 2 * N_W + 5]
    scratch = refs[2 * N_W + 5 :]
    got1, sum1 = scratch[:N_W], scratch[N_W : 2 * N_W]
    got2, sum2 = scratch[2 * N_W : 3 * N_W], scratch[3 * N_W : 4 * N_W]
    got3 = scratch[4 * N_W : 5 * N_W]
    rest = scratch[5 * N_W :]
    recv, small_got, small_sum, s1, r1, s2, r2, s3, r3, sx, rx, ss, rs = rest
    gx, gy, y, z, core = places_of()
    greet(grid_peers(gx, gy, y, z, core) + gy_peers(gx, gy))
    partner = (at(y, z, 1 - core), gy)
    first, along, second, third, little = [], [], [], [], []
    for d in (2, 1, 3):
        peer = (gy + d) % 4
        copy = remote(pp.at[peer], recv.at[d - 1], sx.at[d - 1], rx.at[d - 1], (gx, peer))
        copy.start()
        along.append(copy)
    small_sum[0] = small[...]

    def small_send(stage, peers):
        for k, peer in enumerate(peers):
            copy = remote(
                small_sum.at[stage],
                small_got.at[3 * stage + k],
                ss.at[3 * stage + k],
                rs.at[3 * stage + k],
                peer,
            )
            copy.start()
            little.append(copy)

    def small_add(stage, count):
        value = small_sum[stage]
        for copy in little[len(little) - count :]:
            copy.wait_recv()
        for k in range(count):
            value = value + small_got[3 * stage + k]
        return value

    small_send(0, [partner])
    for i in range(N_W):
        copy = remote(parts[i].at[:, :, 1 - core], got1[i], s1.at[i], r1.at[i], partner)
        copy.start()
        first.append(copy)
    small_sum[1] = small_add(0, 1)
    small_send(1, [(at((y + d) % 4, z, core), gy) for d in (1, 2, 3)])
    for i in range(N_W):
        y_first = i % 2 == 0
        first[i].wait_recv()
        sum1[i][...] = (parts[i][:, :, core].astype(F32) + got1[i][...].astype(F32)).astype(BF)
        for d in (1, 2, 3):
            if y_first:
                there = (y + d) % 4
                src, peer = sum1[i].at[there], (at(there, z, core), gy)
            else:
                there = (z + d) % 4
                src, peer = sum1[i].at[:, there], (at(y, there, core), gy)
            copy = remote(src, got2[i].at[d - 1], s2.at[i, d - 1], r2.at[i, d - 1], peer)
            copy.start()
            second.append(copy)
    small_sum[2] = small_add(1, 3)
    small_send(2, [(at(y, (z + d) % 4, core), gy) for d in (1, 2, 3)])
    for copy in along:
        copy.wait_recv()
    total = local[...] + pp[gy].astype(F32)
    for d in range(3):
        total = total + recv[d].astype(F32)
    grad_o[...] = total.astype(BF)
    small_sum[3] = small_add(2, 3)
    small_send(3, gy_peers(gx, gy))
    for i in range(N_W):
        y_first = i % 2 == 0
        for copy in second[3 * i : 3 * i + 3]:
            copy.wait_recv()
        value = (sum1[i][y] if y_first else sum1[i][:, z]).astype(F32)
        for d in range(3):
            value = value + got2[i][d].astype(F32)
        sum2[i][...] = value.astype(BF)
        for d in (1, 2, 3):
            if y_first:
                there = (z + d) % 4
                peer = (at(y, there, core), gy)
            else:
                there = (y + d) % 4
                peer = (at(there, z, core), gy)
            copy = remote(
                sum2[i].at[there], got3[i].at[d - 1], s3.at[i, d - 1], r3.at[i, d - 1], peer
            )
            copy.start()
            third.append(copy)
    over_all = small_add(3, 3)
    small_o[0] = small_sum[3]
    small_o[1] = over_all
    for i in range(N_W):
        y_first = i % 2 == 0
        for copy in third[3 * i : 3 * i + 3]:
            copy.wait_recv()
        value = (sum2[i][z] if y_first else sum2[i][y]).astype(F32)
        for d in range(3):
            value = value + got3[i][d].astype(F32)
        outs[i][...] = value
    for copy in first + along + second + third + little:
        copy.wait_send()


def last_sums(parts, pp, local, small):
    widths = [p.shape[-1] for p in parts]
    out = tuple(shape(ROWS, w, dtype=F32) for w in widths) + (
        shape(HALF, PACK),
        shape(2, 16, D, dtype=F32),
    )
    scratch = (
        [pltpu.VMEM((4, 4, ROWS, w), BF) for w in widths]
        + [pltpu.VMEM((4, 4, ROWS, w), BF) for w in widths]
        + [pltpu.VMEM((3, 4, ROWS, w), BF) for w in widths]
        + [pltpu.VMEM((4, ROWS, w), BF) for w in widths]
        + [pltpu.VMEM((3, ROWS, w), BF) for w in widths]
        + [
            pltpu.VMEM((3, HALF, PACK), BF),
            pltpu.VMEM((12, 16, D), F32),
            pltpu.VMEM((4, 16, D), F32),
            DMA((N_W,)),
            DMA((N_W,)),
            DMA((N_W, 3)),
            DMA((N_W, 3)),
            DMA((N_W, 3)),
            DMA((N_W, 3)),
            DMA((3,)),
            DMA((3,)),
            DMA((12,)),
            DMA((12,)),
        ]
    )
    return comm_call(
        last_body,
        out,
        (*parts, pp, local, small),
        scratch,
        6,
        [VM] * (N_W + 3),
        tuple([VM] * len(out)),
        vmem=48,
    )


def shards(
    block_input,
    cotangent,
    doc_ids,
    routes,
    qkv_weight,
    out_weight,
    rel_bias,
    norm_gain,
    ff_in,
    ff_out,
    router,
    expert_in,
    expert_out,
):
    picks = bucket_picks()
    doc_c, doc_r = doc_ids.reshape(SEQ, 1), doc_ids.reshape(1, SEQ)
    lines = jnp.einsum("lhb,bn->lhn", rel_bias, picks, precision=highest)
    lines = jnp.pad(lines, ((0, 0), (0, 8 - HEADS), (0, 0)))
    layers = [
        jnp.concatenate([qkv_weight[l].reshape(ROWS, 576), out_weight[l]], axis=1)
        for l in range(2)
    ]
    router_wide = jnp.pad(router, ((0, 0), (0, 64)))
    gain_wide = jnp.pad(norm_gain.reshape(4, LOCAL), ((0, 4), (0, 64)))
    x, cot = pack(block_input), pack(cotangent)
    *gathered, xw, cw, gains = start_gather(
        (layers[0], ff_in, ff_out, layers[1], router_wide), x, cot, gain_wide
    )
    w0, w_in, w_out, w1, w_router = [g.reshape(D, g.shape[-1]) for g in gathered]
    state = x.astype(F32)
    pp, *kept0 = attn_fwd(0, xw, gains, w0, lines, doc_c, doc_r)
    state, sw1 = turn(pp, state)
    pp, pre = ff_fwd(sw1, gains, w_in, w_out)
    state, sw2 = turn(pp, state)
    pp, *kept1 = attn_fwd(1, sw2, gains, w1, lines, doc_c, doc_r)
    state, sw3 = turn(pp, state)
    own_gain = norm_gain[1, 1].reshape(1, LOCAL)
    sent, meta = dispatch(sw3, state, cot, gains, own_gain, w_router, routes)
    arrived = to_experts(sent)
    back, expert_in_grad, expert_out_grad = expert(arrived, expert_in, expert_out)
    returned = from_experts(back)
    block_output, tg, gate = combine(returned, meta, state, cot)
    tw, gate_all = gather_tokens(tg, gate)
    gp, grad_all, d_router, gain3 = router_bwd(
        tw, gate_all, meta, routes, sw3, cw, gains, w_router
    )
    pp, d_w1, gain2, cols1 = attn_bwd(1, gp, sw2, gains, w1, *kept1)
    grad, gp = turn(pp, grad_all)
    pp, d_in, d_out, gain1 = ff_bwd(gp, sw1, gains, w_in, w_out, pre)
    grad, gp = turn(pp, grad)
    pp, d_w0, gain0, cols0 = attn_bwd(0, gp, xw, gains, w0, *kept0)
    cols = jnp.stack([cols0[:HEADS], cols1[:HEADS]])
    bias = jnp.einsum("lhn,bn->lhb", cols, picks, precision=highest)
    bias = jnp.pad(bias.reshape(6, NB), ((0, 6), (0, D - NB)))
    small = jnp.concatenate([gain0, gain1, gain2, gain3, bias], axis=0)
    parts = [g.reshape(4, 4, 2, ROWS, g.shape[-1]) for g in (d_w0, d_in, d_out, d_w1, d_router)]
    g0, ff_in_grad, ff_out_grad, g1, router_sum, input_grad, totals = last_sums(
        parts, pp, grad, small
    )
    input_grad = unpack(input_grad)
    both = jnp.stack([g0, g1])
    qkv_grad = both[:, :, :576].reshape(2, ROWS, 3, LOCAL)
    out_grad = both[:, :, 576:]
    router_grad = router_sum[:, :64]
    bias_grad = totals[0, 4:10, :NB].reshape(2, HEADS, NB)
    start = lax.axis_index("gy") * LOCAL
    gain_grad = lax.dynamic_slice(totals[1, :4], (0, start), (4, LOCAL)).reshape(2, 2, LOCAL)
    return (
        block_output,
        input_grad,
        qkv_grad,
        out_grad,
        bias_grad,
        gain_grad,
        ff_in_grad,
        ff_out_grad,
        router_grad,
        expert_in_grad,
        expert_out_grad,
    )


def solution(mesh):
    in_specs = (
        P("gx", "gy"),
        P("gx", "gy"),
        P("gx"),
        P("gx", None),
        P(None, "gx", None, "gy"),
        P(None, "gx", "gy"),
        P(None, "gy", None),
        P(None, None, "gy"),
        P("gx", "gy"),
        P("gx", "gy"),
        P("gx", None),
        P("gx", None, "gy"),
        P("gx", "gy", None),
    )
    out_specs = (
        P("gx", "gy"),
        P("gx", "gy"),
        P(None, "gx", None, "gy"),
        P(None, "gx", "gy"),
        P(None, "gy", None),
        P(None, None, "gy"),
        P("gx", "gy"),
        P("gx", "gy"),
        P("gx", None),
        P("gx", None, "gy"),
        P("gx", "gy", None),
    )
    return jax.shard_map(shards, mesh=mesh, in_specs=in_specs, out_specs=out_specs, check_vma=False)
```

```python
import functools
import math

import numpy as np

import jax
import jax.numpy as jnp
from jax import lax
from jax.experimental import pallas as pl
from jax.experimental.pallas import tpu as pltpu
from jax.sharding import PartitionSpec as P

NB = 32
D = 768
LOCAL = 192
SEQ = 512
HALF = 256
PACK = 384
ROWS = 24
HEADS = 3
HD = 64
SLOT = 24
SLOTS = 64 * SLOT
BF = jnp.bfloat16
F32 = jnp.float32
MESH = pl.DeviceIdType.MESH
VM = pl.BlockSpec(memory_space=pltpu.VMEM)
HB = pl.BlockSpec(memory_space=pltpu.HBM)
epsilon = 1e-06
highest = lax.Precision.HIGHEST
bucket_edges = [int(math.ceil(16.0 * 8.0 ** (step / 16.0))) for step in range(1, 16)]


def bucket_picks():
    distance = (SEQ - np.arange(SEQ)) % SEQ
    bucket = np.minimum(distance, 16)
    for edge in bucket_edges:
        bucket = bucket + (distance >= edge)
    return (bucket[None, :] == np.arange(NB)[:, None]).astype(np.float32)


def dot(a, b, ca, cb):
    return lax.dot_general(a, b, (((ca,), (cb,)), ((), ())), preferred_element_type=F32)


def unpack(p):
    return jnp.concatenate([p[:, :LOCAL], p[:, LOCAL:]], axis=0)


def pack(a):
    half = a.shape[0] // 2
    return jnp.concatenate([a[:half], a[half:]], axis=1)


def join(ref):
    return jnp.concatenate([unpack(ref[j]) for j in range(4)], axis=1)


def split_store(ref, a):
    for j in range(4):
        ref[j] = pack(a[:, LOCAL * j : LOCAL * (j + 1)])


def gain_row(ref, k):
    return jnp.concatenate([ref[j, k : k + 1, :LOCAL] for j in range(4)], axis=1)


def normalise(whole, gain):
    scale = lax.rsqrt(jnp.mean(whole * whole, axis=-1, keepdims=True) + epsilon)
    return (whole * scale * gain).astype(BF), scale


def norm_back(normed_grad, whole, scale, gain):
    weighted = normed_grad * gain
    inner = jnp.mean(weighted * whole, axis=-1, keepdims=True)
    state_grad = weighted * scale - whole * (scale * scale * scale * inner)
    gain_part = jnp.sum(normed_grad * whole * scale, axis=0, keepdims=True)
    return state_grad, gain_part


def gelu_both(v):
    c = math.sqrt(2.0 / math.pi)
    t = jnp.tanh(c * (v + 0.044715 * (v * v * v)))
    value = 0.5 * v * (1.0 + t)
    slope = 0.5 * (1.0 + t) + 0.5 * v * (1.0 - t * t) * (c * (1.0 + 3.0 * 0.044715 * (v * v)))
    return value, slope


def whole_block(a):
    nd = len(a.shape)
    return pl.BlockSpec(a.shape, lambda i: (0,) * nd)


def local_call(body, kinds, args, out_kinds, out, vmem=52):
    return pl.pallas_call(
        body,
        grid=(1,),
        out_shape=out,
        in_specs=[VM if k == "V" else whole_block(a) for k, a in zip(kinds, args)],
        out_specs=tuple(VM if k == "V" else whole_block(o) for k, o in zip(out_kinds, out)),
        compiler_params=pltpu.CompilerParams(vmem_limit_bytes=vmem * 2**20),
    )(*args)


def shape(*dims, dtype=BF):
    return jax.ShapeDtypeStruct(dims, dtype)


def attn_fwd_body(layer, wp, gains, w, table, picks, doc, pp, mixed_o, ctx_o, probs_o):
    whole = join(wp).astype(F32)
    normed, _ = normalise(whole, gain_row(gains, 2 * layer))
    mixed = dot(normed, w[:, :576], 1, 0).astype(BF)
    mixed_o[...] = mixed
    row = lax.broadcasted_iota(jnp.int32, (SEQ, SEQ), 0)
    col = lax.broadcasted_iota(jnp.int32, (SEQ, SEQ), 1)
    doc_r = doc[...].astype(F32)
    doc_c = jnp.transpose(jnp.broadcast_to(doc_r, (128, SEQ)))[:, :1]
    allowed = (col <= row) & (doc_c == doc_r)
    few = jnp.concatenate([table[layer], jnp.zeros((8 - HEADS, NB), F32)], axis=0)
    lines = lax.dot_general(
        few, picks[...], (((1,), (0,)), ((), ())), precision=highest, preferred_element_type=F32
    )
    context = []
    for h in range(HEADS):
        q = mixed[:, HD * h : HD * (h + 1)]
        k = mixed[:, LOCAL + HD * h : LOCAL + HD * (h + 1)]
        v = mixed[:, 2 * LOCAL + HD * h : 2 * LOCAL + HD * (h + 1)]
        line = jnp.broadcast_to(lines[h : h + 1, :], (SEQ, SEQ))
        bias = pltpu.roll(line, 0, 1, stride=1, stride_axis=0)
        s = jnp.where(allowed, dot(q, k, 1, 1) * 0.125 + bias, -1000000000.0)
        e = jnp.exp(s - jnp.max(s, axis=-1, keepdims=True))
        p = (e * (1.0 / jnp.sum(e, axis=-1, keepdims=True))).astype(BF)
        probs_o[h] = p
        context.append(dot(p, v, 1, 0))
    ctx = jnp.concatenate(context, axis=1).astype(BF)
    ctx_o[...] = ctx
    split_store(pp, dot(ctx, w[:, 576:], 1, 1).astype(BF))


def attn_fwd(layer, wp, kind, gains, w, table, picks, doc):
    out = (
        shape(4, HALF, PACK),
        shape(SEQ, 576),
        shape(SEQ, LOCAL),
        shape(HEADS, SEQ, SEQ),
    )
    return local_call(
        functools.partial(attn_fwd_body, layer),
        kind + "BBBBB",
        (wp, gains, w, table, picks, doc),
        "VBBB",
        out,
    )


def attn_bwd_body(layer, gp, wp, gains, w, mixed, ctx, probs, picks, pp, dw, small_o):
    whole = join(wp).astype(F32)
    gain = gain_row(gains, 2 * layer)
    normed, scale = normalise(whole, gain)
    rows = join(gp)
    cg = dot(rows, w[:, 576:], 1, 0).astype(BF)
    dw[:, 576:] = dot(rows, ctx[...], 0, 0).astype(BF)
    row = lax.broadcasted_iota(jnp.int32, (SEQ, SEQ), 0)
    col = lax.broadcasted_iota(jnp.int32, (SEQ, SEQ), 1)
    flip = jnp.where(row + col == SEQ - 1, 1.0, 0.0).astype(BF)
    dq, dk, dv = [], [], []
    cols = []
    for h in range(HEADS):
        q = mixed[:, HD * h : HD * (h + 1)]
        k = mixed[:, LOCAL + HD * h : LOCAL + HD * (h + 1)]
        v = mixed[:, 2 * LOCAL + HD * h : 2 * LOCAL + HD * (h + 1)]
        c = cg[:, HD * h : HD * (h + 1)]
        p = probs[h]
        pf = p.astype(F32)
        pg = dot(c, v, 1, 1)
        sg = (pf * (pg - jnp.sum(pf * pg, axis=-1, keepdims=True))).astype(BF)
        dq.append(dot(sg, k, 1, 0) * 0.125)
        dk.append(dot(sg, q, 0, 0) * 0.125)
        dv.append(dot(p, c, 0, 0))
        rolled = pltpu.roll(dot(flip, sg, 1, 0), 1, 1, stride=1, stride_axis=0)
        cols.append(jnp.sum(rolled, axis=0, keepdims=True))
    dmixed = jnp.concatenate(dq + dk + dv, axis=1).astype(BF)
    dw[:, :576] = dot(normed, dmixed, 0, 0).astype(BF)
    ng = dot(dmixed, w[:, :576], 1, 1)
    state_grad, gain_part = norm_back(ng, whole, scale, gain)
    split_store(pp, state_grad.astype(BF))
    few = jnp.concatenate(cols + [jnp.zeros((8 - HEADS, SEQ), F32)], axis=0)
    table = lax.dot_general(
        few, picks[...], (((1,), (1,)), ((), ())), precision=highest, preferred_element_type=F32
    )
    small_o[...] = jnp.zeros_like(small_o)
    small_o[4 * layer : 4 * layer + 1, :] = gain_part
    small_o[4 * layer + 1 : 4 * layer + 4, :NB] = table[:HEADS]


def attn_bwd(layer, gp, wp, gains, w, mixed, ctx, probs, picks):
    out = (shape(4, HALF, PACK), shape(D, D), shape(8, D, dtype=F32))
    return local_call(
        functools.partial(attn_bwd_body, layer),
        "VBBBBBBB",
        (gp, wp, gains, w, mixed, ctx, probs, picks),
        "VBB",
        out,
    )


def ff_fwd_body(wp, gains, w_in, w_out, pp, pre_o):
    whole = join(wp).astype(F32)
    normed, _ = normalise(whole, gain_row(gains, 1))
    pre = dot(normed, w_in[...], 1, 0)
    pre_o[...] = pre
    active = gelu_both(pre)[0].astype(BF)
    split_store(pp, dot(active, w_out[...], 1, 1).astype(BF))


def ff_fwd(wp, gains, w_in, w_out):
    out = (shape(4, HALF, PACK), shape(SEQ, D, dtype=F32))
    return local_call(ff_fwd_body, "VBBB", (wp, gains, w_in, w_out), "VB", out)


def ff_bwd_body(gp, wp, gains, w_in, w_out, pre, pp, dw_in, dw_out, small_o):
    whole = join(wp).astype(F32)
    gain = gain_row(gains, 1)
    normed, scale = normalise(whole, gain)
    rows = join(gp)
    value, slope = gelu_both(pre[...])
    dw_out[...] = dot(rows, value.astype(BF), 0, 0).astype(BF)
    hg = (slope * dot(rows, w_out[...], 1, 0)).astype(BF)
    dw_in[...] = dot(normed, hg, 0, 0).astype(BF)
    ng = dot(hg, w_in[...], 1, 1)
    state_grad, gain_part = norm_back(ng, whole, scale, gain)
    split_store(pp, state_grad.astype(BF))
    small_o[...] = jnp.zeros_like(small_o)
    small_o[0:1, :] = gain_part


def ff_bwd(gp, wp, gains, w_in, w_out, pre):
    out = (shape(4, HALF, PACK), shape(D, D), shape(D, D), shape(8, D, dtype=F32))
    return local_call(ff_bwd_body, "VBBBBB", (gp, wp, gains, w_in, w_out, pre), "VBBB", out)


def marks_of(routes, r):
    lane = lax.broadcasted_iota(jnp.int32, (SEQ, 128), 1)
    return lane == routes[:, r : r + 1]


def dispatch_body(wp, state, cot, gains, own_gain, router, routes, out, meta_o):
    whole = join(wp).astype(F32)
    normed, scale = normalise(whole, gain_row(gains, 3))
    logits = dot(normed, router[...], 1, 0)
    marks = [marks_of(routes, r) for r in range(2)]
    picked = [jnp.sum(jnp.where(m, logits, 0.0), axis=1, keepdims=True) for m in marks]
    top = jnp.maximum(picked[0], picked[1])
    weights = [jnp.exp(v - top) for v in picked]
    total = weights[0] + weights[1]
    gates = [v / total for v in weights]
    ones = (jnp.where(marks[0], 1.0, 0.0) + jnp.where(marks[1], 1.0, 0.0)).astype(BF)
    row = lax.broadcasted_iota(jnp.int32, (SEQ, SEQ), 0)
    col = lax.broadcasted_iota(jnp.int32, (SEQ, SEQ), 1)
    before = dot(jnp.where(col < row, 1.0, 0.0).astype(BF), ones, 1, 0)
    places = [jnp.sum(jnp.where(m, before, 0.0), axis=1, keepdims=True) for m in marks]
    slots = [
        places[r] + SLOT * routes[:, r : r + 1].astype(F32) for r in range(2)
    ]
    lane = lax.broadcasted_iota(jnp.int32, (SEQ, 128), 1)
    meta = jnp.zeros((SEQ, 128), F32)
    for index, value in enumerate(gates + slots):
        meta = jnp.where(lane == index, value, meta)
    meta_o[...] = meta
    turned = jnp.transpose(meta)
    own = (unpack(state[...]) * scale * own_gain[...]).astype(BF)
    cotangent = cot[...].astype(F32)
    sent = jnp.zeros((SLOTS, PACK), F32)
    place = lax.broadcasted_iota(jnp.int32, (SLOTS, SEQ), 0)
    for r in range(2):
        chosen = place == turned[2 + r : 3 + r, :].astype(jnp.int32)
        rows = jnp.concatenate([own, (gates[r] * cotangent).astype(BF)], axis=1)
        sent = sent + dot(jnp.where(chosen, 1.0, 0.0).astype(BF), rows, 1, 0)
    out[...] = sent.reshape(32, 2, SLOT, PACK).astype(BF)


def dispatch(wp, state, cot, gains, own_gain, router, routes):
    out = (shape(32, 2, SLOT, PACK), shape(SEQ, 128, dtype=F32))
    return local_call(
        dispatch_body, "VVBBBBB", (wp, state, cot, gains, own_gain, router, routes), "BB", out
    )


def expert_body(arrived, w_in, w_out, back, dw_in, dw_out):
    halves = [arrived[j, :, 0].astype(F32).reshape(32 * SLOT, PACK).astype(BF) for j in range(4)]
    x = jnp.concatenate([a[:, :LOCAL] for a in halves], axis=1)
    g = jnp.concatenate([a[:, LOCAL:] for a in halves], axis=1)
    value, slope = gelu_both(dot(x, w_in[0], 1, 0))
    active = value.astype(BF)
    hg = (slope * dot(g, w_out[0], 1, 1)).astype(BF)
    result = dot(active, w_out[0], 1, 0)
    sent = dot(hg, w_in[0], 1, 1)
    for j in range(4):
        span = slice(LOCAL * j, LOCAL * (j + 1))
        both = jnp.concatenate([result[:, span], sent[:, span]], axis=1)
        back[j, :, 0] = both.reshape(32, SLOT, PACK).astype(BF)
    dw_out[0] = dot(active, g, 0, 0)
    dw_in[0] = dot(x, hg, 0, 0)


def expert(arrived, w_in, w_out):
    rows = pl.BlockSpec((4, 32, 1, SLOT, PACK), lambda e: (0, 0, e, 0, 0))
    weight = pl.BlockSpec((1, D, D), lambda e: (e, 0, 0))
    return pl.pallas_call(
        expert_body,
        grid=(2,),
        out_shape=(
            shape(4, 32, 2, SLOT, PACK),
            shape(2, D, D, dtype=F32),
            shape(2, D, D, dtype=F32),
        ),
        in_specs=[rows, weight, weight],
        out_specs=(rows, weight, weight),
        compiler_params=pltpu.CompilerParams(vmem_limit_bytes=60 * 2**20),
    )(arrived, w_in, w_out)


def combine_body(returned, meta, state, cot, out, tg_o, gate_o):
    values = returned[...].astype(F32).reshape(SLOTS, PACK).astype(BF)
    lane = lax.broadcasted_iota(jnp.int32, (SEQ, SLOTS), 1)
    total = unpack(state[...])
    cotangent = cot[...].astype(F32)
    token_grad = jnp.zeros((SEQ, LOCAL), F32)
    spread = jnp.zeros((SEQ, 128), F32)
    place = lax.broadcasted_iota(jnp.int32, (SEQ, 128), 1)
    for r in range(2):
        chosen = lane == meta[:, 2 + r : 3 + r].astype(jnp.int32)
        found = dot(jnp.where(chosen, 1.0, 0.0).astype(BF), values, 1, 0)
        routed = found[:, :LOCAL]
        token_grad = token_grad + found[:, LOCAL:]
        total = total + meta[:, r : r + 1] * routed
        spread = jnp.where(
            place == r, jnp.sum(cotangent * routed, axis=1, keepdims=True), spread
        )
    out[...] = total.astype(BF)
    tg_o[...] = pack(token_grad).astype(BF)
    gate_o[...] = jnp.transpose(spread)[:8]


def combine(returned, meta, state, cot):
    out = (shape(SEQ, LOCAL), shape(HALF, PACK), shape(8, SEQ, dtype=F32))
    return local_call(combine_body, "VBVB", (returned, meta, state, cot), "BVV", out)


def router_body(tg, gate, meta, routes, wp, cp, gains, router, gp_o, grad_o, dr_o, small_o):
    whole = join(wp).astype(F32)
    gain = gain_row(gains, 3)
    normed, scale = normalise(whole, gain)
    summed = gate[0] + gate[1] + gate[2] + gate[3]
    wide = jnp.concatenate([summed, jnp.zeros((120, SEQ), F32)], axis=0)
    turned = jnp.transpose(wide)
    gates = [meta[:, r : r + 1] for r in range(2)]
    gate_grad = [turned[:, r : r + 1] for r in range(2)]
    inner = gates[0] * gate_grad[0] + gates[1] * gate_grad[1]
    logit_grad = jnp.zeros((SEQ, 128), F32)
    for r in range(2):
        picked_grad = gates[r] * (gate_grad[r] - inner)
        logit_grad = logit_grad + jnp.where(marks_of(routes, r), picked_grad, 0.0)
    logit_grad = logit_grad.astype(BF)
    dr_o[...] = dot(normed, logit_grad, 0, 0).astype(BF)
    ng = join(tg).astype(F32) + dot(logit_grad, router[...], 1, 1)
    state_grad, gain_part = norm_back(ng, whole, scale, gain)
    small_o[...] = jnp.zeros_like(small_o)
    small_o[4:5, :] = gain_part * 0.25
    grad = join(cp).astype(F32) + state_grad
    split_store(grad_o, grad)
    split_store(gp_o, grad.astype(BF))


def router_bwd(tg, gate, meta, routes, wp, cp, gains, router):
    out = (
        shape(4, HALF, PACK),
        shape(4, HALF, PACK, dtype=F32),
        shape(D, 128),
        shape(8, D, dtype=F32),
    )
    return local_call(
        router_body, "VVBBBBBB", (tg, gate, meta, routes, wp, cp, gains, router), "VVBB", out
    )


def places_of():
    gx, gy = lax.axis_index("gx"), lax.axis_index("gy")
    return gx, gy, gx // 8, (gx // 2) % 4, gx % 2


def at(y, z, core):
    return (y * 4 + z) * 2 + core


def greet(peers):
    barrier = pltpu.get_barrier_semaphore()
    for peer in peers:
        pl.semaphore_signal(barrier, inc=1, device_id=peer, device_id_type=MESH)
    pl.semaphore_wait(barrier, len(peers))


def remote(src, dst, send, recv, peer):
    return pltpu.make_async_remote_copy(
        src_ref=src, dst_ref=dst, send_sem=send, recv_sem=recv, device_id=peer, device_id_type=MESH
    )


def gy_peers(gx, gy):
    return [(gx, (gy + d) % 4) for d in (1, 2, 3)]


def grid_peers(gx, gy, y, z, core):
    return (
        [(at((y + d) % 4, z, core), gy) for d in (1, 2, 3)]
        + [(at(y, (z + d) % 4, core), gy) for d in (1, 2, 3)]
        + [(at(y, z, 1 - core), gy)]
    )


def comm_call(body, out, args, scratch, collective_id, specs, out_specs, vmem=32):
    return pl.pallas_call(
        body,
        out_shape=out,
        in_specs=specs,
        out_specs=out_specs,
        scratch_shapes=scratch,
        compiler_params=pltpu.CompilerParams(
            collective_id=collective_id, has_side_effects=True, vmem_limit_bytes=vmem * 2**20
        ),
    )(*args)


DMA = pltpu.SemaphoreType.DMA
N_W = 5


def start_body(*refs):
    weights, (x, cot, gain) = refs[:N_W], refs[N_W : N_W + 3]
    outs = refs[N_W + 3 : 2 * N_W + 3]
    xw, cw, gw, state = refs[2 * N_W + 3 : 2 * N_W + 7]
    raw, packed, load, own, s1, r1, s2, r2, s3, r3, sx, rx = refs[2 * N_W + 7 :]
    gx, gy, y, z, core = places_of()
    loads = [pltpu.make_async_copy(src, raw.at[k], load.at[k]) for k, src in enumerate((x, cot))]
    for copy in loads:
        copy.start()
    greet(grid_peers(gx, gy, y, z, core) + gy_peers(gx, gy))

    rows_first, along = [], []
    for i in range(N_W):
        z_first = i % 2 == 0
        for d in (1, 2, 3):
            peer = (at(y, (z + d) % 4, core) if z_first else at((y + d) % 4, z, core), gy)
            copy = remote(
                weights[i], outs[i].at[y, z, core], s1.at[i, d - 1], r1.at[i, d - 1], peer
            )
            copy.start()
            rows_first.append(copy)
    kept = []
    for i in range(N_W):
        copy = pltpu.make_async_copy(weights[i], outs[i].at[y, z, core], own.at[i])
        copy.start()
        kept.append(copy)
    for k in range(2):
        loads[k].wait()
        packed[k] = pack(raw[k])
    state[...] = packed[0].astype(F32)
    for k, (src, dst) in enumerate(((packed.at[0], xw), (packed.at[1], cw), (gain, gw))):
        for d in (2, 1, 3):
            copy = remote(
                src, dst.at[gy], sx.at[k, d - 1], rx.at[k, d - 1], (gx, (gy + d) % 4)
            )
            copy.start()
            along.append(copy)
        copy = pltpu.make_async_copy(src, dst.at[gy], load.at[k])
        copy.start()
        loads.append(copy)
    partner = (at(y, z, 1 - core), gy)
    second, third = [], []
    for i in range(N_W):
        z_first = i % 2 == 0
        kept[i].wait()
        for d in range(3):
            rows_first[3 * i + d].wait_recv()
        line = outs[i].at[y, :, core] if z_first else outs[i].at[:, z, core]
        for d in (1, 2, 3):
            peer = (at((y + d) % 4, z, core) if z_first else at(y, (z + d) % 4, core), gy)
            copy = remote(line, line, s2.at[i, d - 1], r2.at[i, d - 1], peer)
            copy.start()
            second.append(copy)
        copy = remote(line, line, s3.at[i, 0], r3.at[i, 0], partner)
        copy.start()
        third.append(copy)
    for i in range(N_W):
        z_first = i % 2 == 0
        for d in (1, 2, 3):
            second[3 * i + d - 1].wait_recv()
            line = (
                outs[i].at[(y + 4 - d) % 4, :, core]
                if z_first
                else outs[i].at[:, (z + 4 - d) % 4, core]
            )
            copy = remote(line, line, s3.at[i, d], r3.at[i, d], partner)
            copy.start()
            third.append(copy)
    for copy in rows_first + second:
        copy.wait_send()
    for copy in third + along + loads[2:]:
        copy.wait()


def start_gather(weights, x, cot, gain):
    out = tuple(shape(4, 4, 2, *w.shape) for w in weights) + (
        shape(4, HALF, PACK),
        shape(4, HALF, PACK),
        shape(4, 8, 256, dtype=F32),
        shape(HALF, PACK, dtype=F32),
    )
    scratch = [
        pltpu.VMEM((2, SEQ, LOCAL), BF),
        pltpu.VMEM((2, HALF, PACK), BF),
        DMA((3,)),
        DMA((N_W,)),
        DMA((N_W, 3)),
        DMA((N_W, 3)),
        DMA((N_W, 3)),
        DMA((N_W, 3)),
        DMA((N_W, 4)),
        DMA((N_W, 4)),
        DMA((3, 3)),
        DMA((3, 3)),
    ]
    return comm_call(
        start_body,
        out,
        (*weights, x, cot, gain),
        scratch,
        0,
        [HB] * (N_W + 3),
        tuple([HB] * (N_W + 3) + [VM]),
    )


def turn_body(pick, pp, local, new, out, via, recv, s1, r1, s2, r2, s3, r3, s4, r4):
    gx, gy = lax.axis_index("gx"), lax.axis_index("gy")
    right, left, far = (gy + 1) % 4, (gy + 3) % 4, (gy + 2) % 4
    beside = [(gx, right), (gx, left)]
    greet(beside)
    size = HALF // 2
    rows = [pl.ds(0, size), pl.ds(size, size)]
    there = [right, left]
    copies, passed, direct = [], [], []
    for k in range(2):
        copy = remote(pp.at[far, rows[k]], via.at[k], s1.at[k], r1.at[k], beside[k])
        copy.start()
        passed.append(copy)
    for k in range(2):
        half = rows[1 - k]
        copy = remote(pp.at[there[k], half], recv.at[k, half], s2.at[k], r2.at[k], beside[k])
        copy.start()
        direct.append(copy)
    for k in range(2):
        half = rows[k]
        passed[k].wait_recv()
        via[k] = (via[k].astype(F32) + pp[there[k], half].astype(F32)).astype(BF)
        copy = remote(via.at[k], recv.at[k, half], s2.at[2 + k], r2.at[2 + k], beside[k])
        copy.start()
        direct.append(copy)
    sends = [None] * 4
    for k in range(2):
        half = rows[k]
        direct[1 - k].wait_recv()
        direct[2 + k].wait_recv()
        base = local[gy, half] if pick else local[half]
        total = base + pp[gy, half].astype(F32)
        total = total + recv[0, half].astype(F32) + recv[1, half].astype(F32)
        new[half] = total
        out[gy, half] = total.astype(BF)
        for to in (k, 1 - k):
            block = out.at[gy, half]
            copy = remote(block, block, s3.at[to, k], r3.at[to, k], beside[to])
            copy.start()
            sends[2 * to + k] = copy
    onward = []
    for k in range(2):
        sends[2 * k + k].wait_recv()
        block = out.at[there[1 - k], rows[k]]
        copy = remote(block, block, s4.at[k], r4.at[k], beside[k])
        copy.start()
        onward.append(copy)
    for k in range(2):
        sends[2 * k + 1 - k].wait_recv()
    for copy in onward:
        copy.wait()
    for copy in passed + direct + sends:
        copy.wait_send()


def turn(pp, local):
    pick = local.ndim == 3
    return comm_call(
        functools.partial(turn_body, pick),
        (shape(HALF, PACK, dtype=F32), shape(4, HALF, PACK)),
        (pp, local),
        [
            pltpu.VMEM((2, HALF // 2, PACK), BF),
            pltpu.VMEM((2, HALF, PACK), BF),
            DMA((2,)),
            DMA((2,)),
            DMA((4,)),
            DMA((4,)),
            DMA((2, 2)),
            DMA((2, 2)),
            DMA((2,)),
            DMA((2,)),
        ],
        2 if pick else 1,
        [VM, VM],
        (VM, VM),
    )


def gather_body(tg, gate, tw, gw, sx, rx):
    gx, gy = lax.axis_index("gx"), lax.axis_index("gy")
    greet(gy_peers(gx, gy))
    copies = []
    for k, (src, dst) in enumerate(((gate, gw), (tg, tw))):
        for d in (2, 1, 3):
            copy = remote(src, dst.at[gy], sx.at[k, d - 1], rx.at[k, d - 1], (gx, (gy + d) % 4))
            copy.start()
            copies.append(copy)
        dst[gy] = src[...]
    for copy in copies:
        copy.wait()


def gather_tokens(tg, gate):
    return comm_call(
        gather_body,
        (shape(4, HALF, PACK), shape(4, 8, SEQ, dtype=F32)),
        (tg, gate),
        [DMA((2, 3)), DMA((2, 3))],
        3,
        [VM, VM],
        (VM, VM),
    )


def to_experts_body(sent, out, own, sa, ra, sg, rg, sf, rf):
    gx, gy = lax.axis_index("gx"), lax.axis_index("gy")
    there = [(gy + 1) % 4, (gy + 3) % 4]
    beside = [(gx, there[0]), (gx, there[1])]
    greet(beside + [((gx + k) % 32, gy) for k in range(1, 32)])
    keep = pltpu.make_async_copy(sent.at[gx], out.at[gy, gx], own)
    keep.start()

    def push(k, carry):
        peer = (gx + k) % 32
        remote(sent.at[peer], out.at[gy, gx], sa, ra.at[k], (peer, gy)).start()
        return carry

    lax.fori_loop(1, 32, push, 0)

    def spread(k):
        block = out.at[gy, (gx + 32 - k) % 32]
        for to in range(2):
            remote(block, block, sg.at[to], rg.at[to, k], beside[to]).start()

    def relay(k):
        source = (gx + 32 - k) % 32
        for to in range(2):
            block = out.at[there[1 - to], source]
            remote(block, block, sg.at[to], rg.at[to, k], beside[to]).wait_recv()
            block = out.at[there[1 - to], source, to]
            remote(block, block, sf.at[to], rf.at[to], beside[to]).start()

    def arrive(k):
        source = (gx + 32 - k) % 32
        remote(sent.at[0], out.at[gy, source], sa, ra.at[k], beside[0]).wait_recv()
        spread(k)

    keep.wait()
    spread(0)
    arrive(1)
    arrive(2)

    def step(k, carry):
        arrive(k)
        relay(k - 3)
        return carry

    lax.fori_loop(3, 32, step, 0)
    for k in (29, 30, 31):
        relay(k)
    many = sent.at[pl.ds(0, 31)]
    remote(many, many, sa, ra.at[0], beside[0]).wait_send()
    far = (gy + 2) % 4
    for to in range(2):
        block = out.at[far, :, to]
        remote(block, block, sf.at[to], rf.at[to], beside[to]).wait()
        remote(out.at[gy], out.at[gy], sg.at[to], rg.at[to, 0], beside[to]).wait_send()


def to_experts(sent):
    return comm_call(
        to_experts_body,
        shape(4, 32, 2, SLOT, PACK),
        (sent,),
        [
            DMA(()),
            DMA(()),
            DMA((32,)),
            DMA((2,)),
            DMA((2, 32)),
            DMA((2,)),
            DMA((2,)),
        ],
        4,
        [HB],
        HB,
    )


GROUPS = 8
AHEAD = 3


def from_experts_body(back, out, mine, via, part, recv, total, sl, rl, s1, r1, s2, r2, s3, r3, s4, r4):
    gx, gy = lax.axis_index("gx"), lax.axis_index("gy")
    there = [(gy + 1) % 4, (gy + 3) % 4]
    far = (gy + 2) % 4
    beside = [(gx, there[0]), (gx, there[1])]
    loads = [pltpu.make_async_copy(back.at[gy], mine, sl)]
    for to in range(2):
        loads.append(pltpu.make_async_copy(back.at[there[to], :, :, to], part.at[to], rl.at[to]))
    for copy in loads:
        copy.start()
    greet(beside + [((gx + k) % 32, gy) for k in range(1, 32)])

    def place(c):
        return (c + gx) % GROUPS

    def passing(c, to):
        return remote(
            back.at[far, :, place(c), to], via.at[to, c], s1.at[to], r1.at[to, c], beside[to]
        )

    def directly(c, to):
        return remote(
            back.at[there[to], :, place(c), 1 - to],
            recv.at[to, c, 1 - to],
            s2.at[to],
            r2.at[to, c],
            beside[to],
        )

    def summed(c, to):
        return remote(
            part.at[to, :, place(c)], recv.at[to, c, to], s3.at[to], r3.at[to, c], beside[to]
        )

    def begin(c):
        for to in range(2):
            passing(c, to).start()
        for to in range(2):
            directly(c, to).start()

    def middle(c):
        for to in range(2):
            passing(c, to).wait_recv()
            value = part[to, :, place(c)].astype(F32) + via[to, c].astype(F32)
            part[to, :, place(c)] = value.astype(BF)
            summed(c, to).start()

    def end(c):
        for to in range(2):
            directly(c, to).wait_recv()
            summed(c, to).wait_recv()
        for e in range(2):
            value = mine[:, place(c), e].astype(F32)
            value = value + recv[0, c, e].astype(F32) + recv[1, c, e].astype(F32)
            total[:, place(c), e] = value.astype(BF)
        for i in range(4):
            peer = i * GROUPS + place(c)

            @pl.when(peer != gx)
            def _():
                remote(
                    total.at[i, place(c)],
                    out.at[gx // GROUPS, gx % GROUPS],
                    s4.at[peer],
                    r4.at[gx],
                    (peer, gy),
                ).start()

            @pl.when(peer == gx)
            def _():
                out[gx // GROUPS, gx % GROUPS] = total[i, place(c)]

    for c in range(AHEAD):
        begin(c)
    for copy in loads:
        copy.wait()
    middle(0)
    middle(1)

    def step(c, carry):
        @pl.when(c + AHEAD < GROUPS)
        def _():
            begin(c + AHEAD)

        @pl.when(c + 2 < GROUPS)
        def _():
            middle(c + 2)

        end(c)
        return carry

    lax.fori_loop(0, GROUPS, step, 0)
    for to in range(2):
        half = back.at[far, :, :, to]
        for sem in (s1, s2, s3):
            remote(half, half, sem.at[to], r1.at[to, 0], beside[to]).wait_send()

    def finish(k, carry):
        source = (gx + k) % 32
        remote(
            total.at[0, 0],
            out.at[source // GROUPS, source % GROUPS],
            s4.at[source],
            r4.at[source],
            beside[0],
        ).wait()
        return carry

    lax.fori_loop(1, 32, finish, 0)


def from_experts(back):
    half = (4, GROUPS, SLOT, PACK)
    full = (4, GROUPS, 2, SLOT, PACK)
    return comm_call(
        from_experts_body,
        shape(*full),
        (back.reshape(4, *full),),
        [
            pltpu.VMEM(full, BF),
            pltpu.VMEM((2, GROUPS, 4, SLOT, PACK), BF),
            pltpu.VMEM((2, *half), BF),
            pltpu.VMEM((2, GROUPS, 2, 4, SLOT, PACK), BF),
            pltpu.VMEM(full, BF),
            DMA(()),
            DMA((2,)),
            DMA((2,)),
            DMA((2, GROUPS)),
            DMA((2,)),
            DMA((2, GROUPS)),
            DMA((2,)),
            DMA((2, GROUPS)),
            DMA((32,)),
            DMA((32,)),
        ],
        5,
        [HB],
        VM,
        vmem=40,
    ).reshape(32, 2, SLOT, PACK)


def last_body(*refs):
    parts, (pp, local), smalls = refs[:N_W], refs[N_W : N_W + 2], refs[N_W + 2 : N_W + 6]
    outs = refs[N_W + 6 : 2 * N_W + 6]
    grad_o, bias_o, gain_o = refs[2 * N_W + 6 : 2 * N_W + 9]
    scratch = refs[2 * N_W + 9 :]
    got1, sum1 = scratch[:N_W], scratch[N_W : 2 * N_W]
    got2, sum2 = scratch[2 * N_W : 3 * N_W], scratch[3 * N_W : 4 * N_W]
    got3 = scratch[4 * N_W : 5 * N_W]
    rest = scratch[5 * N_W :]
    small_raw, sl, recv, small_got, small_sum, s1, r1, s2, r2, s3, r3, sx, rx, ss, rs = rest
    gx, gy, y, z, core = places_of()
    loads = [
        pltpu.make_async_copy(src, small_raw.at[k], sl.at[N_W + k]) for k, src in enumerate(smalls)
    ] + [pltpu.make_async_copy(parts[i].at[:, :, core], sum1[i], sl.at[i]) for i in range(N_W)]
    for copy in loads:
        copy.start()
    greet(grid_peers(gx, gy, y, z, core) + gy_peers(gx, gy))
    partner = (at(y, z, 1 - core), gy)
    first, along, second, third, little = [], [], [], [], []
    for d in (2, 1, 3):
        peer = (gy + d) % 4
        copy = remote(pp.at[peer], recv.at[d - 1], sx.at[d - 1], rx.at[d - 1], (gx, peer))
        copy.start()
        along.append(copy)
    for copy in loads[:4]:
        copy.wait()
    small_sum[0, 0:8] = small_raw[0] + small_raw[1]
    small_sum[0, 8:16] = small_raw[2] + small_raw[3]

    def small_send(stage, peers):
        for k, peer in enumerate(peers):
            copy = remote(
                small_sum.at[stage],
                small_got.at[3 * stage + k],
                ss.at[3 * stage + k],
                rs.at[3 * stage + k],
                peer,
            )
            copy.start()
            little.append(copy)

    def small_add(stage, count):
        value = small_sum[stage]
        for copy in little[len(little) - count :]:
            copy.wait_recv()
        for k in range(count):
            value = value + small_got[3 * stage + k]
        return value

    small_send(0, [partner])
    for i in range(N_W):
        copy = remote(parts[i].at[:, :, 1 - core], got1[i], s1.at[i], r1.at[i], partner)
        copy.start()
        first.append(copy)
    small_sum[1] = small_add(0, 1)
    small_send(1, [(at((y + d) % 4, z, core), gy) for d in (1, 2, 3)])
    for i in range(N_W):
        y_first = i % 2 == 0
        loads[4 + i].wait()
        first[i].wait_recv()
        sum1[i][...] = (sum1[i][...].astype(F32) + got1[i][...].astype(F32)).astype(BF)
        for d in (1, 2, 3):
            if y_first:
                there = (y + d) % 4
                src, peer = sum1[i].at[there], (at(there, z, core), gy)
            else:
                there = (z + d) % 4
                src, peer = sum1[i].at[:, there], (at(y, there, core), gy)
            copy = remote(src, got2[i].at[d - 1], s2.at[i, d - 1], r2.at[i, d - 1], peer)
            copy.start()
            second.append(copy)
    small_sum[2] = small_add(1, 3)
    small_send(2, [(at(y, (z + d) % 4, core), gy) for d in (1, 2, 3)])
    for copy in along:
        copy.wait_recv()
    total = local[...] + pp[gy].astype(F32)
    for d in range(3):
        total = total + recv[d].astype(F32)
    grad_o[...] = unpack(total).astype(BF)
    small_sum[3] = small_add(2, 3)
    small_send(3, gy_peers(gx, gy))
    for i in range(N_W):
        y_first = i % 2 == 0
        for copy in second[3 * i : 3 * i + 3]:
            copy.wait_recv()
        value = (sum1[i][y] if y_first else sum1[i][:, z]).astype(F32)
        for d in range(3):
            value = value + got2[i][d].astype(F32)
        sum2[i][...] = value.astype(BF)
        for d in (1, 2, 3):
            if y_first:
                there = (z + d) % 4
                peer = (at(y, there, core), gy)
            else:
                there = (y + d) % 4
                peer = (at(there, z, core), gy)
            copy = remote(
                sum2[i].at[there], got3[i].at[d - 1], s3.at[i, d - 1], r3.at[i, d - 1], peer
            )
            copy.start()
            third.append(copy)
    over_all = small_add(3, 3)
    bias_o[...] = small_sum[3, 0:8, :128]
    for j in range(4):

        @pl.when(gy == j)
        def _():
            for k, row in enumerate((0, 8, 4, 12)):
                gain_o[k : k + 1, :] = over_all[row : row + 1, LOCAL * j : LOCAL * (j + 1)]

    for i in range(N_W):
        y_first = i % 2 == 0
        for copy in third[3 * i : 3 * i + 3]:
            copy.wait_recv()
        value = (sum2[i][z] if y_first else sum2[i][y]).astype(F32)
        for d in range(3):
            value = value + got3[i][d].astype(F32)
        outs[i][...] = value
    for copy in first + along + second + third + little:
        copy.wait_send()


def last_sums(parts, pp, local, smalls):
    widths = [p.shape[-1] for p in parts]
    out = tuple(shape(ROWS, w, dtype=F32) for w in widths) + (
        shape(SEQ, LOCAL),
        shape(8, 128, dtype=F32),
        shape(4, LOCAL, dtype=F32),
    )
    scratch = (
        [pltpu.VMEM((4, 4, ROWS, w), BF) for w in widths]
        + [pltpu.VMEM((4, 4, ROWS, w), BF) for w in widths]
        + [pltpu.VMEM((3, 4, ROWS, w), BF) for w in widths]
        + [pltpu.VMEM((4, ROWS, w), BF) for w in widths]
        + [pltpu.VMEM((3, ROWS, w), BF) for w in widths]
        + [
            pltpu.VMEM((4, 8, D), F32),
            DMA((N_W + 4,)),
            pltpu.VMEM((3, HALF, PACK), BF),
            pltpu.VMEM((12, 16, D), F32),
            pltpu.VMEM((4, 16, D), F32),
            DMA((N_W,)),
            DMA((N_W,)),
            DMA((N_W, 3)),
            DMA((N_W, 3)),
            DMA((N_W, 3)),
            DMA((N_W, 3)),
            DMA((3,)),
            DMA((3,)),
            DMA((12,)),
            DMA((12,)),
        ]
    )
    return comm_call(
        last_body,
        out,
        (*parts, pp, local, *smalls),
        scratch,
        6,
        [HB] * N_W + [VM] * 2 + [HB] * 4,
        tuple([VM] * len(out)),
        vmem=48,
    )


def shards(
    block_input,
    cotangent,
    doc_ids,
    routes,
    qkv_weight,
    out_weight,
    rel_bias,
    norm_gain,
    ff_in,
    ff_out,
    router,
    expert_in,
    expert_out,
):
    picks = jnp.asarray(bucket_picks())
    doc = doc_ids.reshape(1, SEQ)
    layers = [
        jnp.concatenate([qkv_weight[l].reshape(ROWS, 576), out_weight[l]], axis=1)
        for l in range(2)
    ]
    router_wide = jnp.pad(router, ((0, 0), (0, 64)))
    gain_wide = jnp.pad(norm_gain.reshape(4, LOCAL), ((0, 4), (0, 64)))
    *gathered, xw, cw, gains, state = start_gather(
        (layers[0], ff_in, ff_out, layers[1], router_wide), block_input, cotangent, gain_wide
    )
    w0, w_in, w_out, w1, w_router = [g.reshape(D, g.shape[-1]) for g in gathered]
    pp, *kept0 = attn_fwd(0, xw, "B", gains, w0, rel_bias, picks, doc)
    state, sw1 = turn(pp, state)
    pp, pre = ff_fwd(sw1, gains, w_in, w_out)
    state, sw2 = turn(pp, state)
    pp, *kept1 = attn_fwd(1, sw2, "V", gains, w1, rel_bias, picks, doc)
    state, sw3 = turn(pp, state)
    own_gain = norm_gain[1, 1].reshape(1, LOCAL)
    sent, meta = dispatch(sw3, state, cotangent, gains, own_gain, w_router, routes)
    arrived = to_experts(sent)
    back, expert_in_grad, expert_out_grad = expert(arrived, expert_in, expert_out)
    returned = from_experts(back)
    block_output, tg, gate = combine(returned, meta, state, cotangent)
    tw, gate_all = gather_tokens(tg, gate)
    gp, grad_all, d_router, small3 = router_bwd(
        tw, gate_all, meta, routes, sw3, cw, gains, w_router
    )
    pp, d_w1, small2 = attn_bwd(1, gp, sw2, gains, w1, *kept1, picks)
    grad, gp = turn(pp, grad_all)
    pp, d_in, d_out, small1 = ff_bwd(gp, sw1, gains, w_in, w_out, pre)
    grad, gp = turn(pp, grad)
    pp, d_w0, small0 = attn_bwd(0, gp, xw, gains, w0, *kept0, picks)
    parts = [g.reshape(4, 4, 2, ROWS, g.shape[-1]) for g in (d_w0, d_in, d_out, d_w1, d_router)]
    g0, ff_in_grad, ff_out_grad, g1, router_sum, input_grad, bias, gain_grad = last_sums(
        parts, pp, grad, (small0, small2, small1, small3)
    )
    both = jnp.stack([g0, g1])
    qkv_grad = both[:, :, :576].reshape(2, ROWS, 3, LOCAL)
    out_grad = both[:, :, 576:]
    router_grad = router_sum[:, :64]
    bias_grad = bias.reshape(2, 4, 128)[:, 1:, :NB]
    gain_grad = gain_grad.reshape(2, 2, LOCAL)
    return (
        block_output,
        input_grad,
        qkv_grad,
        out_grad,
        bias_grad,
        gain_grad,
        ff_in_grad,
        ff_out_grad,
        router_grad,
        expert_in_grad,
        expert_out_grad,
    )


def solution(mesh):
    in_specs = (
        P("gx", "gy"),
        P("gx", "gy"),
        P("gx"),
        P("gx", None),
        P(None, "gx", None, "gy"),
        P(None, "gx", "gy"),
        P(None, "gy", None),
        P(None, None, "gy"),
        P("gx", "gy"),
        P("gx", "gy"),
        P("gx", None),
        P("gx", None, "gy"),
        P("gx", "gy", None),
    )
    out_specs = (
        P("gx", "gy"),
        P("gx", "gy"),
        P(None, "gx", None, "gy"),
        P(None, "gx", "gy"),
        P(None, "gy", None),
        P(None, None, "gy"),
        P("gx", "gy"),
        P("gx", "gy"),
        P("gx", None),
        P("gx", None, "gy"),
        P("gx", "gy", None),
    )
    return jax.shard_map(shards, mesh=mesh, in_specs=in_specs, out_specs=out_specs, check_vma=False)
```

```python
import functools
import math

import numpy as np

import jax
import jax.numpy as jnp
from jax import lax
from jax.experimental import pallas as pl
from jax.experimental.pallas import tpu as pltpu
from jax.sharding import PartitionSpec as P

NB = 32
D = 768
LOCAL = 192
SEQ = 512
HALF = 256
PACK = 384
ROWS = 24
HEADS = 3
HD = 64
MAIN = 16
SLOT = 40
SLOTS = 32 * SLOT
EXPERT_MB = 36
BF = jnp.bfloat16
F32 = jnp.float32
MESH = pl.DeviceIdType.MESH
DMA = pltpu.SemaphoreType.DMA
VM = pl.BlockSpec(memory_space=pltpu.VMEM)
HB = pl.BlockSpec(memory_space=pltpu.HBM)
epsilon = 1e-06
highest = lax.Precision.HIGHEST
bucket_edges = [int(math.ceil(16.0 * 8.0 ** (step / 16.0))) for step in range(1, 16)]


def bucket_picks():
    distance = (SEQ - np.arange(SEQ)) % SEQ
    bucket = np.minimum(distance, 16)
    for edge in bucket_edges:
        bucket = bucket + (distance >= edge)
    return (bucket[None, :] == np.arange(NB)[:, None]).astype(np.float32)


def dot(a, b, ca, cb):
    return lax.dot_general(a, b, (((ca,), (cb,)), ((), ())), preferred_element_type=F32)


def unpack(p):
    return jnp.concatenate([p[:, :LOCAL], p[:, LOCAL:]], axis=0)


def pack(a):
    half = a.shape[0] // 2
    return jnp.concatenate([a[:half], a[half:]], axis=1)


def join(ref):
    return jnp.concatenate([unpack(ref[j]) for j in range(4)], axis=1)


def split_store(ref, a):
    for j in range(4):
        ref[j] = pack(a[:, LOCAL * j : LOCAL * (j + 1)])


def gain_row(ref, k):
    return jnp.concatenate([ref[j, k : k + 1, :LOCAL] for j in range(4)], axis=1)


def normalise(whole, gain):
    scale = lax.rsqrt(jnp.mean(whole * whole, axis=-1, keepdims=True) + epsilon)
    return (whole * scale * gain).astype(BF), scale


def norm_back(normed_grad, whole, scale, gain):
    weighted = normed_grad * gain
    inner = jnp.mean(weighted * whole, axis=-1, keepdims=True)
    state_grad = weighted * scale - whole * (scale * scale * scale * inner)
    gain_part = jnp.sum(normed_grad * whole * scale, axis=0, keepdims=True)
    return state_grad, gain_part


def gelu_both(v):
    c = math.sqrt(2.0 / math.pi)
    t = jnp.tanh(c * (v + 0.044715 * (v * v * v)))
    value = 0.5 * v * (1.0 + t)
    slope = 0.5 * (1.0 + t) + 0.5 * v * (1.0 - t * t) * (c * (1.0 + 3.0 * 0.044715 * (v * v)))
    return value, slope


class Fetched:
    def __init__(self, ref, copy):
        self.ref, self.copy = ref, copy

    def __getitem__(self, index):
        if self.copy is not None:
            self.copy.wait()
            self.copy = None
        return self.ref[index]


class Kept:
    def __init__(self, ref, copy):
        self.ref, self.copy, self.sent = ref, copy, False

    def __setitem__(self, index, value):
        self.ref[index] = value

    def send(self):
        if not self.sent:
            self.copy.start()
            self.sent = True


def staged_body(body, kinds, out_kinds, *refs):
    n, m = len(kinds), len(out_kinds)
    buffers, sems = list(refs[n + m : -1]), refs[-1]
    count, held = 0, []
    for k, ref in zip(kinds, refs[:n]):
        if k == "B":
            copy = pltpu.make_async_copy(ref, buffers[count], sems.at[count])
            copy.start()
            ref, count = Fetched(buffers[count], copy), count + 1
        held.append(ref)
    results = []
    for k, ref in zip(out_kinds, refs[n : n + m]):
        if k == "B":
            copy = pltpu.make_async_copy(buffers[count], ref, sems.at[count])
            ref, count = Kept(buffers[count], copy), count + 1
        results.append(ref)
    body(*held, *results)
    for ref in held:
        if isinstance(ref, Fetched):
            ref[...]
    for ref in results:
        if isinstance(ref, Kept):
            ref.send()
    for ref in results:
        if isinstance(ref, Kept):
            ref.copy.wait()


def local_call(body, kinds, args, out_kinds, out, vmem=28):
    moved = [a for k, a in zip(kinds, args) if k == "B"]
    moved += [o for k, o in zip(out_kinds, out) if k == "B"]
    return pl.pallas_call(
        functools.partial(staged_body, body, kinds, out_kinds),
        out_shape=out,
        in_specs=[VM if k == "V" else HB for k in kinds],
        out_specs=tuple(VM if k == "V" else HB for k in out_kinds),
        scratch_shapes=[pltpu.VMEM(a.shape, a.dtype) for a in moved] + [DMA((len(moved),))],
        compiler_params=pltpu.CompilerParams(vmem_limit_bytes=vmem * 2**20),
    )(*args)


def shape(*dims, dtype=BF):
    return jax.ShapeDtypeStruct(dims, dtype)


def attn_fwd_body(layer, wp, gains, w, table, picks, doc, pp, mixed_o, ctx_o, probs_o):
    whole = join(wp).astype(F32)
    normed, _ = normalise(whole, gain_row(gains, 2 * layer))
    mixed = dot(normed, w[:, :576], 1, 0).astype(BF)
    mixed_o[...] = mixed
    mixed_o.send()
    row = lax.broadcasted_iota(jnp.int32, (SEQ, SEQ), 0)
    col = lax.broadcasted_iota(jnp.int32, (SEQ, SEQ), 1)
    doc_r = doc[...].astype(F32)
    doc_c = jnp.transpose(jnp.broadcast_to(doc_r, (128, SEQ)))[:, :1]
    allowed = (col <= row) & (doc_c == doc_r)
    few = jnp.concatenate([table[layer], jnp.zeros((8 - HEADS, NB), F32)], axis=0)
    lines = lax.dot_general(
        few, picks[...], (((1,), (0,)), ((), ())), precision=highest, preferred_element_type=F32
    )
    context = []
    for h in range(HEADS):
        q = mixed[:, HD * h : HD * (h + 1)]
        k = mixed[:, LOCAL + HD * h : LOCAL + HD * (h + 1)]
        v = mixed[:, 2 * LOCAL + HD * h : 2 * LOCAL + HD * (h + 1)]
        line = jnp.broadcast_to(lines[h : h + 1, :], (SEQ, SEQ))
        bias = pltpu.roll(line, 0, 1, stride=1, stride_axis=0)
        s = jnp.where(allowed, dot(q, k, 1, 1) * 0.125 + bias, -1000000000.0)
        e = jnp.exp(s - jnp.max(s, axis=-1, keepdims=True))
        p = (e * (1.0 / jnp.sum(e, axis=-1, keepdims=True))).astype(BF)
        probs_o[h] = p
        context.append(dot(p, v, 1, 0))
    ctx = jnp.concatenate(context, axis=1).astype(BF)
    ctx_o[...] = ctx
    ctx_o.send()
    probs_o.send()
    split_store(pp, dot(ctx, w[:, 576:], 1, 1).astype(BF))


def attn_fwd(layer, wp, kind, gains, w, table, picks, doc):
    out = (
        shape(4, HALF, PACK),
        shape(SEQ, 576),
        shape(SEQ, LOCAL),
        shape(HEADS, SEQ, SEQ),
    )
    return local_call(
        functools.partial(attn_fwd_body, layer),
        kind + "BBBBB",
        (wp, gains, w, table, picks, doc),
        "VBBB",
        out,
    )


def attn_bwd_body(layer, gp, wp, gains, w, mixed, ctx, probs, picks, pp, dw, small_o):
    whole = join(wp).astype(F32)
    gain = gain_row(gains, 2 * layer)
    normed, scale = normalise(whole, gain)
    rows = join(gp)
    cg = dot(rows, w[:, 576:], 1, 0).astype(BF)
    dw[:, 576:] = dot(rows, ctx[...], 0, 0).astype(BF)
    row = lax.broadcasted_iota(jnp.int32, (SEQ, SEQ), 0)
    col = lax.broadcasted_iota(jnp.int32, (SEQ, SEQ), 1)
    flip = jnp.where(row + col == SEQ - 1, 1.0, 0.0).astype(BF)
    dq, dk, dv = [], [], []
    cols = []
    for h in range(HEADS):
        q = mixed[:, HD * h : HD * (h + 1)]
        k = mixed[:, LOCAL + HD * h : LOCAL + HD * (h + 1)]
        v = mixed[:, 2 * LOCAL + HD * h : 2 * LOCAL + HD * (h + 1)]
        c = cg[:, HD * h : HD * (h + 1)]
        p = probs[h]
        pf = p.astype(F32)
        pg = dot(c, v, 1, 1)
        sg = (pf * (pg - jnp.sum(pf * pg, axis=-1, keepdims=True))).astype(BF)
        dq.append(dot(sg, k, 1, 0) * 0.125)
        dk.append(dot(sg, q, 0, 0) * 0.125)
        dv.append(dot(p, c, 0, 0))
        rolled = pltpu.roll(dot(flip, sg, 1, 0), 1, 1, stride=1, stride_axis=0)
        cols.append(jnp.sum(rolled, axis=0, keepdims=True))
    dmixed = jnp.concatenate(dq + dk + dv, axis=1).astype(BF)
    dw[:, :576] = dot(normed, dmixed, 0, 0).astype(BF)
    dw.send()
    ng = dot(dmixed, w[:, :576], 1, 1)
    state_grad, gain_part = norm_back(ng, whole, scale, gain)
    split_store(pp, state_grad.astype(BF))
    few = jnp.concatenate(cols + [jnp.zeros((8 - HEADS, SEQ), F32)], axis=0)
    table = lax.dot_general(
        few, picks[...], (((1,), (1,)), ((), ())), precision=highest, preferred_element_type=F32
    )
    small_o[...] = jnp.zeros((8, D), F32)
    small_o[4 * layer : 4 * layer + 1, :] = gain_part
    small_o[4 * layer + 1 : 4 * layer + 4, :NB] = table[:HEADS]


def attn_bwd(layer, gp, wp, gains, w, mixed, ctx, probs, picks):
    out = (shape(4, HALF, PACK), shape(D, D), shape(8, D, dtype=F32))
    return local_call(
        functools.partial(attn_bwd_body, layer),
        "VBBBBBBB",
        (gp, wp, gains, w, mixed, ctx, probs, picks),
        "VBB",
        out,
    )


def ff_fwd_body(wp, gains, w_in, w_out, pp, pre_o):
    whole = join(wp).astype(F32)
    normed, _ = normalise(whole, gain_row(gains, 1))
    pre = dot(normed, w_in[...], 1, 0)
    pre_o[...] = pre
    pre_o.send()
    active = gelu_both(pre)[0].astype(BF)
    split_store(pp, dot(active, w_out[...], 1, 1).astype(BF))


def ff_fwd(wp, gains, w_in, w_out):
    out = (shape(4, HALF, PACK), shape(SEQ, D, dtype=F32))
    return local_call(ff_fwd_body, "VBBB", (wp, gains, w_in, w_out), "VB", out)


def ff_bwd_body(gp, wp, gains, w_in, w_out, pre, pp, dw_in, dw_out, small_o):
    whole = join(wp).astype(F32)
    gain = gain_row(gains, 1)
    normed, scale = normalise(whole, gain)
    rows = join(gp)
    value, slope = gelu_both(pre[...])
    dw_out[...] = dot(rows, value.astype(BF), 0, 0).astype(BF)
    dw_out.send()
    hg = (slope * dot(rows, w_out[...], 1, 0)).astype(BF)
    dw_in[...] = dot(normed, hg, 0, 0).astype(BF)
    dw_in.send()
    ng = dot(hg, w_in[...], 1, 1)
    state_grad, gain_part = norm_back(ng, whole, scale, gain)
    split_store(pp, state_grad.astype(BF))
    small_o[...] = jnp.zeros((8, D), F32)
    small_o[0:1, :] = gain_part


def ff_bwd(gp, wp, gains, w_in, w_out, pre):
    out = (shape(4, HALF, PACK), shape(D, D), shape(D, D), shape(8, D, dtype=F32))
    return local_call(ff_bwd_body, "VBBBBB", (gp, wp, gains, w_in, w_out, pre), "VBBB", out)


def marks_of(routes, r):
    lane = lax.broadcasted_iota(jnp.int32, (SEQ, 64), 1)
    return lane == routes[:, r : r + 1]


def dispatch_body(wp, state, cot, gains, own_gain, router, routes, out, meta_o):
    whole = join(wp).astype(F32)
    normed, scale = normalise(whole, gain_row(gains, 3))
    logits = dot(normed, router[...], 1, 0)
    marks = [marks_of(routes, r) for r in range(2)]
    picked = [jnp.sum(jnp.where(m, logits, 0.0), axis=1, keepdims=True) for m in marks]
    top = jnp.maximum(picked[0], picked[1])
    weights = [jnp.exp(v - top) for v in picked]
    total = weights[0] + weights[1]
    gates = [v / total for v in weights]
    ones = (jnp.where(marks[0], 1.0, 0.0) + jnp.where(marks[1], 1.0, 0.0)).astype(BF)
    row = lax.broadcasted_iota(jnp.int32, (SEQ, SEQ), 0)
    col = lax.broadcasted_iota(jnp.int32, (SEQ, SEQ), 1)
    before = dot(jnp.where(col < row, 1.0, 0.0).astype(BF), ones, 1, 0)
    places = [jnp.sum(jnp.where(m, before, 0.0), axis=1, keepdims=True) for m in marks]
    slots = []
    for r in range(2):
        chosen = routes[:, r : r + 1]
        second = (chosen % 2).astype(F32)
        inside = jnp.where(
            places[r] < MAIN, places[r] + MAIN * second, places[r] + MAIN + 2.0 * second
        )
        slots.append(inside + SLOT * (chosen // 2).astype(F32))
    lane = lax.broadcasted_iota(jnp.int32, (SEQ, 128), 1)
    meta = jnp.zeros((SEQ, 128), F32)
    for index, value in enumerate(gates + slots):
        meta = jnp.where(lane == index, value, meta)
    meta_o[...] = meta
    meta_o.send()
    turned = jnp.transpose(meta)
    own = (unpack(state[...]) * scale * own_gain[...]).astype(BF)
    cotangent = cot[...].astype(F32)
    sent = jnp.zeros((SLOTS, PACK), F32)
    place = lax.broadcasted_iota(jnp.int32, (SLOTS, SEQ), 0)
    for r in range(2):
        chosen = place == turned[2 + r : 3 + r, :].astype(jnp.int32)
        rows = jnp.concatenate([own, (gates[r] * cotangent).astype(BF)], axis=1)
        sent = sent + dot(jnp.where(chosen, 1.0, 0.0).astype(BF), rows, 1, 0)
    out[...] = sent.reshape(32, SLOT, PACK).astype(BF)


def dispatch(wp, state, cot, gains, own_gain, router, routes):
    out = (shape(32, SLOT, PACK), shape(SEQ, 128, dtype=F32))
    return local_call(
        dispatch_body, "VVBBBBB", (wp, state, cot, gains, own_gain, router, routes), "VB", out
    )


def expert_body(arrived, w_in, w_out, back, dw_in, dw_out, wi, wo, gi, go, sems):
    loads, stores = [], []
    for e in range(2):
        for k, (src, dst) in enumerate(((w_in.at[e], wi.at[e]), (w_out.at[e], wo.at[e]))):
            copy = pltpu.make_async_copy(src, dst, sems.at[2 * e + k])
            copy.start()
            loads.append(copy)

    def store(src, dst):
        copy = pltpu.make_async_copy(src, dst, sems.at[4 + len(stores)])
        copy.start()
        stores.append(copy)

    halves = [arrived[j].astype(F32) for j in range(4)]
    tails = [a[:, 2 * MAIN :].reshape(256, PACK).astype(BF) for a in halves]
    tail_row = lax.broadcasted_iota(jnp.int32, (256, D), 0) % 8
    held = None
    for e in range(2):
        mains = [
            a[:, MAIN * e : MAIN * (e + 1)].reshape(32 * MAIN, PACK).astype(BF) for a in halves
        ]
        both = [jnp.concatenate([m, t], axis=0) for m, t in zip(mains, tails)]
        x = jnp.concatenate([a[:, :LOCAL] for a in both], axis=1)
        own = tail_row // 2 == e
        g = jnp.concatenate([a[:, LOCAL:] for a in mains], axis=1)
        g_tail = jnp.concatenate([a[:, LOCAL:] for a in tails], axis=1)
        g_tail = jnp.where(own, g_tail.astype(F32), 0.0).astype(BF)
        g = jnp.concatenate([g, g_tail], axis=0)
        loads[2 * e].wait()
        value, slope = gelu_both(dot(x, wi[e], 1, 0))
        active = value.astype(BF)
        loads[2 * e + 1].wait()
        go[e] = dot(active, g, 0, 0)
        store(go.at[e], dw_out.at[e])
        hg = (slope * dot(g, wo[e], 1, 1)).astype(BF)
        gi[e] = dot(x, hg, 0, 0)
        store(gi.at[e], dw_in.at[e])
        result = dot(active, wo[e], 1, 0)
        sent = dot(hg, wi[e], 1, 1)
        tail = (jnp.where(own, result[32 * MAIN :], 0.0), sent[32 * MAIN :])
        if e == 1:
            tail = (tail[0] + held[0], tail[1] + held[1])
        held = tail
        for j in range(4):
            span = slice(LOCAL * j, LOCAL * (j + 1))
            pair = jnp.concatenate([result[: 32 * MAIN, span], sent[: 32 * MAIN, span]], axis=1)
            back[j, :, MAIN * e : MAIN * (e + 1)] = pair.reshape(32, MAIN, PACK).astype(BF)
            if e == 1:
                pair = jnp.concatenate([tail[0][:, span], tail[1][:, span]], axis=1)
                back[j, :, 2 * MAIN :] = pair.reshape(32, 8, PACK).astype(BF)
    for copy in stores:
        copy.wait()


def expert(arrived, w_in, w_out):
    return pl.pallas_call(
        expert_body,
        out_shape=(
            shape(4, 32, SLOT, PACK),
            shape(2, D, D, dtype=F32),
            shape(2, D, D, dtype=F32),
        ),
        in_specs=[VM, HB, HB],
        out_specs=(VM, HB, HB),
        scratch_shapes=[
            pltpu.VMEM((2, D, D), BF),
            pltpu.VMEM((2, D, D), BF),
            pltpu.VMEM((2, D, D), F32),
            pltpu.VMEM((2, D, D), F32),
            DMA((8,)),
        ],
        compiler_params=pltpu.CompilerParams(vmem_limit_bytes=EXPERT_MB * 2**20),
    )(arrived, w_in, w_out)


def combine_body(returned, meta, state, cot, out, tg_o, gate_o):
    values = returned[...].astype(F32).reshape(SLOTS, PACK).astype(BF)
    lane = lax.broadcasted_iota(jnp.int32, (SEQ, SLOTS), 1)
    total = unpack(state[...])
    cotangent = cot[...].astype(F32)
    token_grad = jnp.zeros((SEQ, LOCAL), F32)
    spread = jnp.zeros((SEQ, 128), F32)
    place = lax.broadcasted_iota(jnp.int32, (SEQ, 128), 1)
    for r in range(2):
        chosen = lane == meta[:, 2 + r : 3 + r].astype(jnp.int32)
        found = dot(jnp.where(chosen, 1.0, 0.0).astype(BF), values, 1, 0)
        routed = found[:, :LOCAL]
        token_grad = token_grad + found[:, LOCAL:]
        total = total + meta[:, r : r + 1] * routed
        spread = jnp.where(
            place == r, jnp.sum(cotangent * routed, axis=1, keepdims=True), spread
        )
    out[...] = total.astype(BF)
    out.send()
    tg_o[...] = pack(token_grad).astype(BF)
    gate_o[...] = jnp.transpose(spread)[:8]


def combine(returned, meta, state, cot):
    out = (shape(SEQ, LOCAL), shape(HALF, PACK), shape(8, SEQ, dtype=F32))
    return local_call(combine_body, "VBVB", (returned, meta, state, cot), "BVV", out)


def router_body(tg, gate, meta, routes, wp, cp, gains, router, gp_o, grad_o, dr_o, small_o):
    whole = join(wp).astype(F32)
    gain = gain_row(gains, 3)
    normed, scale = normalise(whole, gain)
    summed = gate[0] + gate[1] + gate[2] + gate[3]
    wide = jnp.concatenate([summed, jnp.zeros((120, SEQ), F32)], axis=0)
    turned = jnp.transpose(wide)
    gates = [meta[:, r : r + 1] for r in range(2)]
    gate_grad = [turned[:, r : r + 1] for r in range(2)]
    inner = gates[0] * gate_grad[0] + gates[1] * gate_grad[1]
    logit_grad = jnp.zeros((SEQ, 64), F32)
    for r in range(2):
        picked_grad = gates[r] * (gate_grad[r] - inner)
        logit_grad = logit_grad + jnp.where(marks_of(routes, r), picked_grad, 0.0)
    logit_grad = logit_grad.astype(BF)
    dr_o[...] = dot(normed, logit_grad, 0, 0).astype(BF)
    ng = join(tg).astype(F32) + dot(logit_grad, router[...], 1, 1)
    state_grad, gain_part = norm_back(ng, whole, scale, gain)
    small_o[...] = jnp.zeros((8, D), F32)
    small_o[4:5, :] = gain_part * 0.25
    grad = join(cp).astype(F32) + state_grad
    split_store(grad_o, grad)
    split_store(gp_o, grad.astype(BF))


def router_bwd(tg, gate, meta, routes, wp, cp, gains, router):
    out = (
        shape(4, HALF, PACK),
        shape(4, HALF, PACK, dtype=F32),
        shape(D, 64),
        shape(8, D, dtype=F32),
    )
    return local_call(
        router_body, "VVBBBBBB", (tg, gate, meta, routes, wp, cp, gains, router), "VVBB", out
    )


def places_of():
    gx, gy = lax.axis_index("gx"), lax.axis_index("gy")
    return gx, gy, gx // 8, (gx // 2) % 4, gx % 2


def at(y, z, core):
    return (y * 4 + z) * 2 + core


def greet(peers):
    barrier = pltpu.get_barrier_semaphore()
    for peer in peers:
        pl.semaphore_signal(barrier, inc=1, device_id=peer, device_id_type=MESH)
    pl.semaphore_wait(barrier, len(peers))


def remote(src, dst, send, recv, peer):
    return pltpu.make_async_remote_copy(
        src_ref=src, dst_ref=dst, send_sem=send, recv_sem=recv, device_id=peer, device_id_type=MESH
    )


def gy_peers(gx, gy):
    return [(gx, (gy + d) % 4) for d in (1, 2, 3)]


def grid_peers(gx, gy, y, z, core):
    return (
        [(at((y + d) % 4, z, core), gy) for d in (1, 2, 3)]
        + [(at(y, (z + d) % 4, core), gy) for d in (1, 2, 3)]
        + [(at(y, z, 1 - core), gy)]
    )


def comm_call(body, out, args, scratch, collective_id, specs, out_specs, vmem=16):
    return pl.pallas_call(
        body,
        out_shape=out,
        in_specs=specs,
        out_specs=out_specs,
        scratch_shapes=scratch,
        compiler_params=pltpu.CompilerParams(
            collective_id=collective_id, has_side_effects=True, vmem_limit_bytes=vmem * 2**20
        ),
    )(*args)


class Pool:
    def __init__(self, sems):
        self.sems, self.count = sems, 0

    def take(self):
        self.count += 1
        return self.sems.at[self.count - 1]

    def send(self, src, dst, peer):
        copy = remote(src, dst, self.take(), self.take(), peer)
        copy.start()
        return copy

    def keep(self, src, dst):
        copy = pltpu.make_async_copy(src, dst, self.take())
        copy.start()
        return copy


def together(pieces):
    pieces = list(pieces)
    while pieces:
        pieces = [p for p in pieces if next(p, False) is None]


def gather_weight(pool, w, out, z_first):
    gx, gy, y, z, core = places_of()
    mine = y if z_first else z
    partner = (at(y, z, 1 - core), gy)

    def line(k):
        return out.at[k, :, core] if z_first else out.at[:, k, core]

    def across(d, along_z):
        return (at(y, (z + d) % 4, core) if along_z else at((y + d) % 4, z, core), gy)

    own = pool.keep(w, out.at[y, z, core])
    first = [pool.send(w, out.at[y, z, core], across(d, z_first)) for d in (1, 2, 3)]
    yield
    own.wait()
    for copy in first:
        copy.wait_recv()
    second = [pool.send(line(mine), line(mine), across(d, not z_first)) for d in (1, 2, 3)]
    third = [pool.send(line(mine), line(mine), partner)]
    yield
    for d in (1, 2, 3):
        second[d - 1].wait_recv()
        block = line((mine + 4 - d) % 4)
        third.append(pool.send(block, block, partner))
    yield
    for copy in first + second:
        copy.wait_send()
    for copy in third:
        copy.wait()


def reduce_weight(pool, part, out, y_first, got1, sum1, got2, sum2, got3):
    gx, gy, y, z, core = places_of()
    own = pool.keep(part.at[:, :, core], sum1)
    first = pool.send(part.at[:, :, 1 - core], got1, (at(y, z, 1 - core), gy))
    yield
    own.wait()
    first.wait_recv()
    sum1[...] = (sum1[...].astype(F32) + got1[...].astype(F32)).astype(BF)
    second, third = [], []
    for d in (1, 2, 3):
        if y_first:
            there = (y + d) % 4
            src, peer = sum1.at[there], (at(there, z, core), gy)
        else:
            there = (z + d) % 4
            src, peer = sum1.at[:, there], (at(y, there, core), gy)
        second.append(pool.send(src, got2.at[d - 1], peer))
    yield
    for copy in second:
        copy.wait_recv()
    value = (sum1[y] if y_first else sum1[:, z]).astype(F32)
    for d in range(3):
        value = value + got2[d].astype(F32)
    sum2[...] = value.astype(BF)
    for d in (1, 2, 3):
        there = (z + d) % 4 if y_first else (y + d) % 4
        peer = (at(y, there, core) if y_first else at(there, z, core), gy)
        third.append(pool.send(sum2.at[there], got3.at[d - 1], peer))
    yield
    for copy in third:
        copy.wait_recv()
    value = (sum2[z] if y_first else sum2[y]).astype(F32)
    for d in range(3):
        value = value + got3[d].astype(F32)
    out[...] = value
    for copy in [first] + second + third:
        copy.wait_send()


def reduce_scratch(w):
    return [
        pltpu.VMEM((4, 4, ROWS, w), BF),
        pltpu.VMEM((4, 4, ROWS, w), BF),
        pltpu.VMEM((3, 4, ROWS, w), BF),
        pltpu.VMEM((4, ROWS, w), BF),
        pltpu.VMEM((3, ROWS, w), BF),
    ]


def start_rows(pool, x, gain, xw, gw, state, raw, packed, load):
    gx, gy = lax.axis_index("gx"), lax.axis_index("gy")
    copies = []

    def spread(src, dst):
        copies.extend(pool.send(src, dst.at[gy], (gx, (gy + d) % 4)) for d in (2, 1, 3))
        copies.append(pool.keep(src, dst.at[gy]))

    load.wait()
    packed[...] = pack(raw[...])
    spread(packed, xw)
    spread(gain, gw)
    state[...] = packed[...].astype(F32)
    yield
    for copy in copies:
        copy.wait()


def start_body(w, x, gain, w_all, xw, gw, state, raw, packed, sems):
    gx, gy, y, z, core = places_of()
    pool = Pool(sems)
    halves = [pl.ds(0, D // 2), pl.ds(D // 2, D // 2)]
    load = pool.keep(x, raw)
    greet(grid_peers(gx, gy, y, z, core) + gy_peers(gx, gy))
    together(
        [
            *[
                gather_weight(
                    pool, w.at[:, half], w_all.at[:, :, :, :, half], half.start == 0
                )
                for half in halves
            ],
            start_rows(pool, x, gain, xw, gw, state, raw, packed, load),
        ]
    )


def start_gather(w, x, gain):
    out = (
        shape(4, 4, 2, *w.shape),
        shape(4, HALF, PACK),
        shape(4, 8, 256, dtype=F32),
        shape(HALF, PACK, dtype=F32),
    )
    scratch = [pltpu.VMEM((SEQ, LOCAL), BF), pltpu.VMEM((HALF, PACK), BF), DMA((96,))]
    return comm_call(start_body, out, (w, x, gain), scratch, 0, [HB] * 3, (HB, HB, HB, VM))


def gather_rows(pool, load, raw, packed, out):
    gx, gy = lax.axis_index("gx"), lax.axis_index("gy")
    yield
    load.wait()
    packed[...] = pack(raw[...])
    yield
    copies = [pool.send(packed, out.at[gy], (gx, (gy + d) % 4)) for d in (2, 1, 3)]
    copies.append(pool.keep(packed, out.at[gy]))
    yield
    yield
    for copy in copies:
        copy.wait()


def turn_rows(pool, pick, pp, local, new, out, via, recv):
    gx, gy = lax.axis_index("gx"), lax.axis_index("gy")
    there, far = [(gy + 1) % 4, (gy + 3) % 4], (gy + 2) % 4
    beside = [(gx, there[0]), (gx, there[1])]
    size = HALF // 2
    rows = [pl.ds(0, size), pl.ds(size, size)]
    passed = [pool.send(pp.at[far, rows[k]], via.at[k], beside[k]) for k in range(2)]
    direct = [
        pool.send(pp.at[there[k], rows[1 - k]], recv.at[k, rows[1 - k]], beside[k])
        for k in range(2)
    ]
    yield
    for k in range(2):
        half = rows[k]
        passed[k].wait_recv()
        via[k] = (via[k].astype(F32) + pp[there[k], half].astype(F32)).astype(BF)
        direct.append(pool.send(via.at[k], recv.at[k, half], beside[k]))
    yield
    sends = [None] * 4
    for k in range(2):
        half = rows[k]
        direct[1 - k].wait_recv()
        direct[2 + k].wait_recv()
        base = local[gy, half] if pick else local[half]
        total = base + pp[gy, half].astype(F32)
        total = total + recv[0, half].astype(F32) + recv[1, half].astype(F32)
        new[half] = total
        out[gy, half] = total.astype(BF)
        for to in (k, 1 - k):
            block = out.at[gy, half]
            sends[2 * to + k] = pool.send(block, block, beside[to])
    yield
    onward = []
    for k in range(2):
        sends[2 * k + k].wait_recv()
        block = out.at[there[1 - k], rows[k]]
        onward.append(pool.send(block, block, beside[k]))
    yield
    for k in range(2):
        sends[2 * k + 1 - k].wait_recv()
    for copy in onward:
        copy.wait()
    for copy in passed + direct + sends:
        copy.wait_send()


def turn_body(pick, n_gather, n_reduce, n_rows, *refs):
    n = 2 + n_gather + n_reduce + n_rows
    pp, local = refs[:2]
    extra, (new, out) = refs[2:n], refs[n : n + 2]
    made = refs[n + 2 : 2 * n]
    via, recv = refs[2 * n : 2 * n + 2]
    scratch, sems = refs[2 * n + 2 : -1], refs[-1]
    gx, gy, y, z, core = places_of()
    pool = Pool(sems)
    if n_rows:
        raw, packed = scratch[-2:]
        load = pool.keep(extra[-1], raw)
    greet(
        [(gx, (gy + 1) % 4), (gx, (gy + 3) % 4)]
        + ([(gx, (gy + 2) % 4)] if n_rows else [])
        + (grid_peers(gx, gy, y, z, core) if n_gather + n_reduce else [])
    )
    pieces = [turn_rows(pool, pick, pp, local, new, out, via, recv)]
    for i in range(n_gather):
        pieces.append(gather_weight(pool, extra[i], made[i], i % 2 == 0))
    if n_rows:
        pieces.append(gather_rows(pool, load, raw, packed, made[-1]))
    for i in range(n_reduce):
        pieces.append(
            reduce_weight(pool, extra[i], made[i], i % 2 == 0, *scratch[5 * i : 5 * i + 5])
        )
    together(pieces)


def turn(collective_id, pp, local, gather=(), reduce=(), rows=()):
    out = [shape(HALF, PACK, dtype=F32), shape(4, HALF, PACK)]
    out += [shape(4, 4, 2, *w.shape) for w in gather]
    out += [shape(ROWS, p.shape[-1], dtype=F32) for p in reduce]
    out += [shape(4, HALF, PACK) for _ in rows]
    reduce = [p.reshape(4, 4, 2, ROWS, p.shape[-1]) for p in reduce]
    scratch = [pltpu.VMEM((2, HALF // 2, PACK), BF), pltpu.VMEM((2, HALF, PACK), BF)]
    for p in reduce:
        scratch += reduce_scratch(p.shape[-1])
    for _ in rows:
        scratch += [pltpu.VMEM((SEQ, LOCAL), BF), pltpu.VMEM((HALF, PACK), BF)]
    made = comm_call(
        functools.partial(turn_body, local.ndim == 3, len(gather), len(reduce), len(rows)),
        tuple(out),
        (pp, local, *gather, *reduce, *rows),
        scratch + [DMA((96,))],
        collective_id,
        [VM, VM] + [HB] * (len(gather) + len(reduce) + len(rows)),
        tuple([VM, VM] + [HB] * len(gather) + [VM] * len(reduce) + [HB] * len(rows)),
    )
    kept = [m.reshape(D, m.shape[-1]) for m in made[2 : 2 + len(gather)]]
    return [*made[:2], *kept, *made[2 + len(gather) :]]


def gather_body(tg, gate, tw, gw, sx, rx):
    gx, gy = lax.axis_index("gx"), lax.axis_index("gy")
    greet(gy_peers(gx, gy))
    copies = []
    for k, (src, dst) in enumerate(((gate, gw), (tg, tw))):
        for d in (2, 1, 3):
            copy = remote(src, dst.at[gy], sx.at[k, d - 1], rx.at[k, d - 1], (gx, (gy + d) % 4))
            copy.start()
            copies.append(copy)
        dst[gy] = src[...]
    for copy in copies:
        copy.wait()


def gather_tokens(tg, gate):
    return comm_call(
        gather_body,
        (shape(4, HALF, PACK), shape(4, 8, SEQ, dtype=F32)),
        (tg, gate),
        [DMA((2, 3)), DMA((2, 3))],
        7,
        [VM, VM],
        (VM, VM),
    )


AHEAD = 16
LAG = 8


def to_experts_body(sent, out, own, sa, ra, sg, rg, sf, rf):
    gx, gy, y, z, core = places_of()
    there = [(gy + 1) % 4, (gy + 3) % 4]
    far = (gy + 2) % 4
    beside = [(gx, there[0]), (gx, there[1])]
    greet(beside + [((gx + k) % 32, gy) for k in range(1, 32)])
    keep = pltpu.make_async_copy(sent.at[gx], out.at[gy, gx], own)
    keep.start()

    def shift(k, sign):
        far_y, far_z, far_core = k // 8, (k // 2) % 4, k % 2
        return at((y + 4 + sign * far_y) % 4, (z + 4 + sign * far_z) % 4, (core + far_core) % 2)

    def push(k):
        peer = shift(k, 1)
        remote(sent.at[peer], out.at[gy, gx], sa, ra.at[k], (peer, gy)).start()

    def spread(k):
        block = out.at[gy, shift(k, -1)]
        for to in range(2):
            remote(block, block, sg.at[to], rg.at[to, k], beside[to]).start()

    def arrive(k):
        remote(sent.at[0], out.at[gy, shift(k, -1)], sa, ra.at[k], beside[0]).wait_recv()
        spread(k)

    def relay(k, to):
        source = shift(k, -1)
        for way in range(2):
            block = out.at[there[1 - way], source]
            remote(block, block, sg.at[way], rg.at[way, k], beside[way]).wait_recv()
        block = out.at[there[1 - to], source]
        remote(block, block, sf.at[to], rf.at[to], beside[to]).start()

    for k in range(1, AHEAD):
        push(k)
    keep.wait()
    spread(0)
    for k in range(1, LAG):
        arrive(k)

    def step(i, carry):
        for to in range(2):
            k = LAG + 2 * i + to

            @pl.when(k + AHEAD - LAG < 32)
            def _():
                push(k + AHEAD - LAG)

            arrive(k)
            relay(k - LAG, to)
        return carry

    lax.fori_loop(0, (32 - LAG) // 2, step, 0)
    for k in range(32 - LAG, 32):
        relay(k, k % 2)
    many = sent.at[pl.ds(0, 31)]
    remote(many, many, sa, ra.at[0], beside[0]).wait_send()
    for to in range(2):
        half = out.at[far, pl.ds(0, 16)]
        remote(half, half, sf.at[to], rf.at[to], beside[to]).wait()
        remote(out.at[gy], out.at[gy], sg.at[to], rg.at[to, 0], beside[to]).wait_send()


def to_experts(sent):
    return comm_call(
        to_experts_body,
        shape(4, 32, SLOT, PACK),
        (sent,),
        [
            DMA(()),
            DMA(()),
            DMA((32,)),
            DMA((2,)),
            DMA((2, 32)),
            DMA((2,)),
            DMA((2,)),
        ],
        8,
        [VM],
        VM,
        vmem=12,
    )


GROUPS = 8
BEGUN = 4


def from_experts_body(back, out, via, part, recv, total, sems, s4, r4):
    gx, gy = lax.axis_index("gx"), lax.axis_index("gy")
    there = [(gy + 1) % 4, (gy + 3) % 4]
    far = (gy + 2) % 4
    beside = [(gx, there[0]), (gx, there[1])]
    greet(beside + [((gx + k) % 32, gy) for k in range(1, 32)])
    pool = Pool(sems)
    passing, direct, summed = [], [], []

    def place(c):
        return (c + gx) % GROUPS

    def begin(c):
        to = c % 2
        passing.append(pool.send(back.at[far, :, place(c)], via.at[c], beside[to]))
        direct.append(
            pool.send(back.at[there[1 - to], :, place(c)], recv.at[1 - to, c], beside[1 - to])
        )

    def middle(c):
        to = c % 2
        passing[c].wait_recv()
        value = back[there[to], :, place(c)].astype(F32) + via[c].astype(F32)
        part[c] = value.astype(BF)
        summed.append(pool.send(part.at[c], recv.at[to, c], beside[to]))

    def end(c):
        direct[c].wait_recv()
        summed[c].wait_recv()
        value = back[gy, :, place(c)].astype(F32)
        value = value + recv[0, c].astype(F32) + recv[1, c].astype(F32)
        total[:, place(c)] = value.astype(BF)
        for i in range(4):
            peer = i * GROUPS + place(c)

            @pl.when(peer != gx)
            def _():
                remote(
                    total.at[i, place(c)],
                    out.at[gx // GROUPS, gx % GROUPS],
                    s4.at[peer],
                    r4.at[gx],
                    (peer, gy),
                ).start()

            @pl.when(peer == gx)
            def _():
                out[gx // GROUPS, gx % GROUPS] = total[i, place(c)]

    for c in range(BEGUN):
        begin(c)
    middle(0)
    middle(1)
    for c in range(GROUPS):
        if c + BEGUN < GROUPS:
            begin(c + BEGUN)
        if c + 2 < GROUPS:
            middle(c + 2)
        end(c)
    for copy in passing + direct + summed:
        copy.wait_send()

    def finish(k, carry):
        source = (gx + k) % 32
        remote(
            total.at[0, 0],
            out.at[source // GROUPS, source % GROUPS],
            s4.at[source],
            r4.at[source],
            beside[0],
        ).wait()
        return carry

    lax.fori_loop(1, 32, finish, 0)


def from_experts(back):
    full = (4, GROUPS, SLOT, PACK)
    return comm_call(
        from_experts_body,
        shape(*full),
        (back.reshape(4, *full),),
        [
            pltpu.VMEM((GROUPS, 4, SLOT, PACK), BF),
            pltpu.VMEM((GROUPS, 4, SLOT, PACK), BF),
            pltpu.VMEM((2, GROUPS, 4, SLOT, PACK), BF),
            pltpu.VMEM(full, BF),
            DMA((48,)),
            DMA((32,)),
            DMA((32,)),
        ],
        9,
        [VM],
        VM,
        vmem=16,
    ).reshape(32, SLOT, PACK)


def last_rows(pool, pp, local, grad_o, recv):
    gx, gy = lax.axis_index("gx"), lax.axis_index("gy")
    copies = [
        pool.send(pp.at[(gy + d) % 4], recv.at[d - 1], (gx, (gy + d) % 4)) for d in (2, 1, 3)
    ]
    yield
    yield
    for copy in copies:
        copy.wait_recv()
    total = local[...] + pp[gy].astype(F32)
    for d in range(3):
        total = total + recv[d].astype(F32)
    grad_o[...] = unpack(total).astype(BF)
    for copy in copies:
        copy.wait_send()


def last_small(pool, raw, loads, bias_o, gain_o, got, held):
    gx, gy, y, z, core = places_of()
    for copy in loads:
        copy.wait()
    held[0, 0:8] = raw[0] + raw[1]
    held[0, 8:16] = raw[2] + raw[3]
    groups = [
        [(at(y, z, 1 - core), gy)],
        [(at((y + d) % 4, z, core), gy) for d in (1, 2, 3)],
        [(at(y, (z + d) % 4, core), gy) for d in (1, 2, 3)],
        gy_peers(gx, gy),
    ]
    copies = []
    for stage, peers in enumerate(groups):
        now = [
            pool.send(held.at[stage], got.at[3 * stage + k], peer) for k, peer in enumerate(peers)
        ]
        copies += now
        yield
        value = held[stage]
        for k, copy in enumerate(now):
            copy.wait_recv()
            value = value + got[3 * stage + k]
        if stage < 3:
            held[stage + 1] = value
    bias_o[...] = held[3, 0:8, :128]
    for j in range(4):

        @pl.when(gy == j)
        def _():
            for k, row in enumerate((0, 8, 4, 12)):
                gain_o[k : k + 1, :] = value[row : row + 1, LOCAL * j : LOCAL * (j + 1)]

    for copy in copies:
        copy.wait_send()


def last_body(part, pp, local, a, b, c, d, out, grad_o, bias_o, gain_o, *scratch):
    pieces, (raw, recv, got, held, sems) = (scratch[:5], scratch[5:10]), scratch[10:]
    halves = [pl.ds(0, D // 2), pl.ds(D // 2, D // 2)]
    gx, gy, y, z, core = places_of()
    pool = Pool(sems)
    loads = [pool.keep(src, raw.at[k]) for k, src in enumerate((a, b, c, d))]
    greet(grid_peers(gx, gy, y, z, core) + gy_peers(gx, gy))
    together(
        [
            *[
                reduce_weight(
                    pool, part.at[:, :, :, :, half], out.at[:, half], half.start == 0, *piece
                )
                for half, piece in zip(halves, pieces)
            ],
            last_rows(pool, pp, local, grad_o, recv),
            last_small(pool, raw, loads, bias_o, gain_o, got, held),
        ]
    )


def last_sums(part, pp, local, smalls):
    out = (
        shape(ROWS, D, dtype=F32),
        shape(SEQ, LOCAL),
        shape(8, 128, dtype=F32),
        shape(4, LOCAL, dtype=F32),
    )
    scratch = reduce_scratch(D // 2) * 2 + [
        pltpu.VMEM((4, 8, D), F32),
        pltpu.VMEM((3, HALF, PACK), BF),
        pltpu.VMEM((12, 16, D), F32),
        pltpu.VMEM((4, 16, D), F32),
        DMA((96,)),
    ]
    return comm_call(
        last_body,
        out,
        (part.reshape(4, 4, 2, ROWS, D), pp, local, *smalls),
        scratch,
        6,
        [HB, VM, VM] + [HB] * 4,
        (VM,) * 4,
    )


def shards(
    block_input,
    cotangent,
    doc_ids,
    routes,
    qkv_weight,
    out_weight,
    rel_bias,
    norm_gain,
    ff_in,
    ff_out,
    router,
    expert_in,
    expert_out,
):
    picks = jnp.asarray(bucket_picks())
    doc = doc_ids.reshape(1, SEQ)
    layers = [
        jnp.concatenate([qkv_weight[l].reshape(ROWS, 576), out_weight[l]], axis=1)
        for l in range(2)
    ]
    gain_wide = jnp.pad(norm_gain.reshape(4, LOCAL), ((0, 4), (0, 64)))
    w0, xw, gains, state = start_gather(layers[0], block_input, gain_wide)
    w0 = w0.reshape(D, D)
    pp, *kept0 = attn_fwd(0, xw, "B", gains, w0, rel_bias, picks, doc)
    state, sw1, w_in, w_out, cw = turn(1, pp, state, gather=(ff_in, ff_out), rows=(cotangent,))
    pp, pre = ff_fwd(sw1, gains, w_in, w_out)
    state, sw2, w1, w_router = turn(2, pp, state, gather=(layers[1], router))
    pp, *kept1 = attn_fwd(1, sw2, "V", gains, w1, rel_bias, picks, doc)
    state, sw3 = turn(3, pp, state)
    own_gain = norm_gain[1, 1].reshape(1, LOCAL)
    sent, meta = dispatch(sw3, state, cotangent, gains, own_gain, w_router, routes)
    arrived = to_experts(sent)
    back, expert_in_grad, expert_out_grad = expert(arrived, expert_in, expert_out)
    returned = from_experts(back)
    block_output, tg, gate = combine(returned, meta, state, cotangent)
    tw, gate_all = gather_tokens(tg, gate)
    gp, grad_all, d_router, small3 = router_bwd(
        tw, gate_all, meta, routes, sw3, cw, gains, w_router
    )
    pp, d_w1, small2 = attn_bwd(1, gp, sw2, gains, w1, *kept1, picks)
    grad, gp, g1, router_grad = turn(4, pp, grad_all, reduce=(d_w1, d_router))
    pp, d_in, d_out, small1 = ff_bwd(gp, sw1, gains, w_in, w_out, pre)
    grad, gp, ff_in_grad, ff_out_grad = turn(5, pp, grad, reduce=(d_in, d_out))
    pp, d_w0, small0 = attn_bwd(0, gp, xw, gains, w0, *kept0, picks)
    g0, input_grad, bias, gain_grad = last_sums(d_w0, pp, grad, (small0, small2, small1, small3))
    both = jnp.stack([g0, g1])
    qkv_grad = both[:, :, :576].reshape(2, ROWS, 3, LOCAL)
    out_grad = both[:, :, 576:]
    bias_grad = bias.reshape(2, 4, 128)[:, 1:, :NB]
    gain_grad = gain_grad.reshape(2, 2, LOCAL)
    return (
        block_output,
        input_grad,
        qkv_grad,
        out_grad,
        bias_grad,
        gain_grad,
        ff_in_grad,
        ff_out_grad,
        router_grad,
        expert_in_grad,
        expert_out_grad,
    )


def solution(mesh):
    in_specs = (
        P("gx", "gy"),
        P("gx", "gy"),
        P("gx"),
        P("gx", None),
        P(None, "gx", None, "gy"),
        P(None, "gx", "gy"),
        P(None, "gy", None),
        P(None, None, "gy"),
        P("gx", "gy"),
        P("gx", "gy"),
        P("gx", None),
        P("gx", None, "gy"),
        P("gx", "gy", None),
    )
    out_specs = (
        P("gx", "gy"),
        P("gx", "gy"),
        P(None, "gx", None, "gy"),
        P(None, "gx", "gy"),
        P(None, "gy", None),
        P(None, None, "gy"),
        P("gx", "gy"),
        P("gx", "gy"),
        P("gx", None),
        P("gx", None, "gy"),
        P("gx", "gy", None),
    )
    return jax.shard_map(shards, mesh=mesh, in_specs=in_specs, out_specs=out_specs, check_vma=False)
```

```python
import functools
import math

import numpy as np

import jax
import jax.numpy as jnp
from jax import lax
from jax.experimental import pallas as pl
from jax.experimental.pallas import tpu as pltpu
from jax.sharding import PartitionSpec as P

NB = 32
D = 768
LOCAL = 192
SEQ = 512
HALF = 256
PACK = 384
ROWS = 24
HEADS = 3
HD = 64
MAIN = 16
SLOT = 40
SLOTS = 32 * SLOT
EXPERT_MB = 36
BF = jnp.bfloat16
F32 = jnp.float32
MESH = pl.DeviceIdType.MESH
DMA = pltpu.SemaphoreType.DMA
VM = pl.BlockSpec(memory_space=pltpu.VMEM)
HB = pl.BlockSpec(memory_space=pltpu.HBM)
epsilon = 1e-06
highest = lax.Precision.HIGHEST
bucket_edges = [int(math.ceil(16.0 * 8.0 ** (step / 16.0))) for step in range(1, 16)]


def bucket_picks():
    distance = (SEQ - np.arange(SEQ)) % SEQ
    bucket = np.minimum(distance, 16)
    for edge in bucket_edges:
        bucket = bucket + (distance >= edge)
    return (bucket[None, :] == np.arange(NB)[:, None]).astype(np.float32)


def dot(a, b, ca, cb):
    return lax.dot_general(a, b, (((ca,), (cb,)), ((), ())), preferred_element_type=F32)


def unpack(p):
    return jnp.concatenate([p[:, :LOCAL], p[:, LOCAL:]], axis=0)


def pack(a):
    half = a.shape[0] // 2
    return jnp.concatenate([a[:half], a[half:]], axis=1)


def join(ref):
    return jnp.concatenate([unpack(ref[j]) for j in range(4)], axis=1)


def split_store(ref, a):
    for j in range(4):
        ref[j] = pack(a[:, LOCAL * j : LOCAL * (j + 1)])


def gain_row(ref, k):
    return jnp.concatenate([ref[j, k : k + 1, :LOCAL] for j in range(4)], axis=1)


def normalise(whole, gain):
    scale = lax.rsqrt(jnp.mean(whole * whole, axis=-1, keepdims=True) + epsilon)
    return (whole * scale * gain).astype(BF), scale


def norm_back(normed_grad, whole, scale, gain):
    weighted = normed_grad * gain
    inner = jnp.mean(weighted * whole, axis=-1, keepdims=True)
    state_grad = weighted * scale - whole * (scale * scale * scale * inner)
    gain_part = jnp.sum(normed_grad * whole * scale, axis=0, keepdims=True)
    return state_grad, gain_part


def gelu_both(v):
    c = math.sqrt(2.0 / math.pi)
    t = jnp.tanh(c * (v + 0.044715 * (v * v * v)))
    value = 0.5 * v * (1.0 + t)
    slope = 0.5 * (1.0 + t) + 0.5 * v * (1.0 - t * t) * (c * (1.0 + 3.0 * 0.044715 * (v * v)))
    return value, slope


class Fetched:
    def __init__(self, ref, copy):
        self.ref, self.copy = ref, copy

    def __getitem__(self, index):
        if self.copy is not None:
            self.copy.wait()
            self.copy = None
        return self.ref[index]


class Kept:
    def __init__(self, ref, copy):
        self.ref, self.copy, self.sent = ref, copy, False

    def __setitem__(self, index, value):
        self.ref[index] = value

    def send(self):
        if not self.sent:
            self.copy.start()
            self.sent = True


def staged_body(body, kinds, out_kinds, *refs):
    n, m = len(kinds), len(out_kinds)
    buffers, sems = list(refs[n + m : -1]), refs[-1]
    count, held = 0, []
    for k, ref in zip(kinds, refs[:n]):
        if k == "B":
            copy = pltpu.make_async_copy(ref, buffers[count], sems.at[count])
            copy.start()
            ref, count = Fetched(buffers[count], copy), count + 1
        held.append(ref)
    results = []
    for k, ref in zip(out_kinds, refs[n : n + m]):
        if k == "B":
            copy = pltpu.make_async_copy(buffers[count], ref, sems.at[count])
            ref, count = Kept(buffers[count], copy), count + 1
        results.append(ref)
    body(*held, *results)
    for ref in held:
        if isinstance(ref, Fetched):
            ref[...]
    for ref in results:
        if isinstance(ref, Kept):
            ref.send()
    for ref in results:
        if isinstance(ref, Kept):
            ref.copy.wait()


def local_call(body, kinds, args, out_kinds, out, vmem=28):
    moved = [a for k, a in zip(kinds, args) if k == "B"]
    moved += [o for k, o in zip(out_kinds, out) if k == "B"]
    return pl.pallas_call(
        functools.partial(staged_body, body, kinds, out_kinds),
        out_shape=out,
        in_specs=[VM if k == "V" else HB for k in kinds],
        out_specs=tuple(VM if k == "V" else HB for k in out_kinds),
        scratch_shapes=[pltpu.VMEM(a.shape, a.dtype) for a in moved] + [DMA((len(moved),))],
        compiler_params=pltpu.CompilerParams(vmem_limit_bytes=vmem * 2**20),
    )(*args)


def shape(*dims, dtype=BF):
    return jax.ShapeDtypeStruct(dims, dtype)


def attn_fwd_body(layer, wp, gains, w, table, picks, doc, pp, mixed_o, ctx_o, probs_o):
    whole = join(wp).astype(F32)
    normed, _ = normalise(whole, gain_row(gains, 2 * layer))
    mixed = dot(normed, w[:, :576], 1, 0).astype(BF)
    mixed_o[...] = mixed
    mixed_o.send()
    row = lax.broadcasted_iota(jnp.int32, (SEQ, SEQ), 0)
    col = lax.broadcasted_iota(jnp.int32, (SEQ, SEQ), 1)
    doc_r = doc[...].astype(F32)
    doc_c = jnp.transpose(jnp.broadcast_to(doc_r, (128, SEQ)))[:, :1]
    allowed = (col <= row) & (doc_c == doc_r)
    few = jnp.concatenate([table[layer], jnp.zeros((8 - HEADS, NB), F32)], axis=0)
    lines = lax.dot_general(
        few, picks[...], (((1,), (0,)), ((), ())), precision=highest, preferred_element_type=F32
    )
    context = []
    for h in range(HEADS):
        q = mixed[:, HD * h : HD * (h + 1)]
        k = mixed[:, LOCAL + HD * h : LOCAL + HD * (h + 1)]
        v = mixed[:, 2 * LOCAL + HD * h : 2 * LOCAL + HD * (h + 1)]
        line = jnp.broadcast_to(lines[h : h + 1, :], (SEQ, SEQ))
        bias = pltpu.roll(line, 0, 1, stride=1, stride_axis=0)
        s = jnp.where(allowed, dot(q, k, 1, 1) * 0.125 + bias, -1000000000.0)
        e = jnp.exp(s - jnp.max(s, axis=-1, keepdims=True))
        p = (e * (1.0 / jnp.sum(e, axis=-1, keepdims=True))).astype(BF)
        probs_o[h] = p
        context.append(dot(p, v, 1, 0))
    ctx = jnp.concatenate(context, axis=1).astype(BF)
    ctx_o[...] = ctx
    ctx_o.send()
    probs_o.send()
    split_store(pp, dot(ctx, w[:, 576:], 1, 1).astype(BF))


def attn_fwd(layer, wp, kind, gains, w, table, picks, doc):
    out = (
        shape(4, HALF, PACK),
        shape(SEQ, 576),
        shape(SEQ, LOCAL),
        shape(HEADS, SEQ, SEQ),
    )
    return local_call(
        functools.partial(attn_fwd_body, layer),
        kind + "BBBBB",
        (wp, gains, w, table, picks, doc),
        "VBBB",
        out,
    )


def attn_bwd_body(layer, gp, wp, gains, w, mixed, ctx, probs, picks, pp, dw, small_o):
    whole = join(wp).astype(F32)
    gain = gain_row(gains, 2 * layer)
    normed, scale = normalise(whole, gain)
    rows = join(gp)
    cg = dot(rows, w[:, 576:], 1, 0).astype(BF)
    dw[:, 576:] = dot(rows, ctx[...], 0, 0).astype(BF)
    row = lax.broadcasted_iota(jnp.int32, (SEQ, SEQ), 0)
    col = lax.broadcasted_iota(jnp.int32, (SEQ, SEQ), 1)
    flip = jnp.where(row + col == SEQ - 1, 1.0, 0.0).astype(BF)
    dq, dk, dv = [], [], []
    cols = []
    for h in range(HEADS):
        q = mixed[:, HD * h : HD * (h + 1)]
        k = mixed[:, LOCAL + HD * h : LOCAL + HD * (h + 1)]
        v = mixed[:, 2 * LOCAL + HD * h : 2 * LOCAL + HD * (h + 1)]
        c = cg[:, HD * h : HD * (h + 1)]
        p = probs[h]
        pf = p.astype(F32)
        pg = dot(c, v, 1, 1)
        sg = (pf * (pg - jnp.sum(pf * pg, axis=-1, keepdims=True))).astype(BF)
        dq.append(dot(sg, k, 1, 0) * 0.125)
        dk.append(dot(sg, q, 0, 0) * 0.125)
        dv.append(dot(p, c, 0, 0))
        rolled = pltpu.roll(dot(flip, sg, 1, 0), 1, 1, stride=1, stride_axis=0)
        cols.append(jnp.sum(rolled, axis=0, keepdims=True))
    dmixed = jnp.concatenate(dq + dk + dv, axis=1).astype(BF)
    dw[:, :576] = dot(normed, dmixed, 0, 0).astype(BF)
    dw.send()
    ng = dot(dmixed, w[:, :576], 1, 1)
    state_grad, gain_part = norm_back(ng, whole, scale, gain)
    split_store(pp, state_grad.astype(BF))
    few = jnp.concatenate(cols + [jnp.zeros((8 - HEADS, SEQ), F32)], axis=0)
    table = lax.dot_general(
        few, picks[...], (((1,), (1,)), ((), ())), precision=highest, preferred_element_type=F32
    )
    small_o[...] = jnp.zeros((8, D), F32)
    small_o[4 * layer : 4 * layer + 1, :] = gain_part
    small_o[4 * layer + 1 : 4 * layer + 4, :NB] = table[:HEADS]


def attn_bwd(layer, gp, wp, gains, w, mixed, ctx, probs, picks):
    out = (shape(4, HALF, PACK), shape(D, D), shape(8, D, dtype=F32))
    return local_call(
        functools.partial(attn_bwd_body, layer),
        "VBBBBBBB",
        (gp, wp, gains, w, mixed, ctx, probs, picks),
        "VBB",
        out,
    )


def ff_fwd_body(wp, gains, w_in, w_out, pp, pre_o):
    whole = join(wp).astype(F32)
    normed, _ = normalise(whole, gain_row(gains, 1))
    pre = dot(normed, w_in[...], 1, 0)
    pre_o[...] = pre
    pre_o.send()
    active = gelu_both(pre)[0].astype(BF)
    split_store(pp, dot(active, w_out[...], 1, 1).astype(BF))


def ff_fwd(wp, gains, w_in, w_out):
    out = (shape(4, HALF, PACK), shape(SEQ, D, dtype=F32))
    return local_call(ff_fwd_body, "VBBB", (wp, gains, w_in, w_out), "VB", out)


def ff_bwd_body(gp, wp, gains, w_in, w_out, pre, pp, dw_in, dw_out, small_o):
    whole = join(wp).astype(F32)
    gain = gain_row(gains, 1)
    normed, scale = normalise(whole, gain)
    rows = join(gp)
    value, slope = gelu_both(pre[...])
    dw_out[...] = dot(rows, value.astype(BF), 0, 0).astype(BF)
    dw_out.send()
    hg = (slope * dot(rows, w_out[...], 1, 0)).astype(BF)
    dw_in[...] = dot(normed, hg, 0, 0).astype(BF)
    dw_in.send()
    ng = dot(hg, w_in[...], 1, 1)
    state_grad, gain_part = norm_back(ng, whole, scale, gain)
    split_store(pp, state_grad.astype(BF))
    small_o[...] = jnp.zeros((8, D), F32)
    small_o[0:1, :] = gain_part


def ff_bwd(gp, wp, gains, w_in, w_out, pre):
    out = (shape(4, HALF, PACK), shape(D, D), shape(D, D), shape(8, D, dtype=F32))
    return local_call(ff_bwd_body, "VBBBBB", (gp, wp, gains, w_in, w_out, pre), "VBBB", out)


def marks_of(routes, r):
    lane = lax.broadcasted_iota(jnp.int32, (SEQ, 64), 1)
    return lane == routes[:, r : r + 1]


def dispatch_body(wp, state, cot, gains, router, turned_routes, out, meta_o):
    whole = join(wp).astype(F32)
    normed, scale = normalise(whole, gain_row(gains, 3))
    logits = dot(normed, router[...], 1, 0)
    listed = jnp.concatenate([turned_routes[...].astype(F32), jnp.zeros((126, SEQ), F32)], axis=0)
    routes = jnp.transpose(listed).astype(jnp.int32)
    own_gain = gains[lax.axis_index("gy"), 3:4, :LOCAL]
    marks = [marks_of(routes, r) for r in range(2)]
    picked = [jnp.sum(jnp.where(m, logits, 0.0), axis=1, keepdims=True) for m in marks]
    top = jnp.maximum(picked[0], picked[1])
    weights = [jnp.exp(v - top) for v in picked]
    total = weights[0] + weights[1]
    gates = [v / total for v in weights]
    ones = (jnp.where(marks[0], 1.0, 0.0) + jnp.where(marks[1], 1.0, 0.0)).astype(BF)
    row = lax.broadcasted_iota(jnp.int32, (SEQ, SEQ), 0)
    col = lax.broadcasted_iota(jnp.int32, (SEQ, SEQ), 1)
    before = dot(jnp.where(col < row, 1.0, 0.0).astype(BF), ones, 1, 0)
    places = [jnp.sum(jnp.where(m, before, 0.0), axis=1, keepdims=True) for m in marks]
    slots = []
    for r in range(2):
        chosen = routes[:, r : r + 1]
        second = (chosen % 2).astype(F32)
        inside = jnp.where(
            places[r] < MAIN, places[r] + MAIN * second, places[r] + MAIN + 2.0 * second
        )
        slots.append(inside + SLOT * (chosen // 2).astype(F32))
    lane = lax.broadcasted_iota(jnp.int32, (SEQ, 128), 1)
    meta = jnp.zeros((SEQ, 128), F32)
    listing = [routes[:, r : r + 1].astype(F32) for r in range(2)]
    for index, value in enumerate(gates + slots + listing):
        meta = jnp.where(lane == index, value, meta)
    meta_o[...] = meta
    meta_o.send()
    turned = jnp.transpose(meta)
    own = (unpack(state[...]) * scale * own_gain).astype(BF)
    cotangent = jnp.transpose(cot[...].astype(F32))
    sent = jnp.zeros((SLOTS, PACK), F32)
    place = lax.broadcasted_iota(jnp.int32, (SLOTS, SEQ), 0)
    for r in range(2):
        chosen = place == turned[2 + r : 3 + r, :].astype(jnp.int32)
        rows = jnp.concatenate([own, (gates[r] * cotangent).astype(BF)], axis=1)
        sent = sent + dot(jnp.where(chosen, 1.0, 0.0).astype(BF), rows, 1, 0)
    out[...] = sent.reshape(32, SLOT, PACK).astype(BF)


def dispatch(wp, state, cot, gains, router, routes):
    out = (shape(32, SLOT, PACK), shape(SEQ, 128, dtype=F32))
    return local_call(
        dispatch_body, "VVBBBB", (wp, state, cot, gains, router, routes), "VB", out
    )


def expert_body(arrived, w_in, w_out, back, dw_in, dw_out, wi, wo, gi, go, sems):
    loads, stores = [], []
    for e in range(2):
        for k, (src, dst) in enumerate(((w_in.at[e], wi.at[e]), (w_out.at[e], wo.at[e]))):
            copy = pltpu.make_async_copy(src, dst, sems.at[2 * e + k])
            copy.start()
            loads.append(copy)

    def store(src, dst):
        copy = pltpu.make_async_copy(src, dst, sems.at[4 + len(stores)])
        copy.start()
        stores.append(copy)

    halves = [arrived[j].astype(F32) for j in range(4)]
    tails = [a[:, 2 * MAIN :].reshape(256, PACK).astype(BF) for a in halves]
    tail_row = lax.broadcasted_iota(jnp.int32, (256, D), 0) % 8
    held = None
    for e in range(2):
        mains = [
            a[:, MAIN * e : MAIN * (e + 1)].reshape(32 * MAIN, PACK).astype(BF) for a in halves
        ]
        both = [jnp.concatenate([m, t], axis=0) for m, t in zip(mains, tails)]
        x = jnp.concatenate([a[:, :LOCAL] for a in both], axis=1)
        own = tail_row // 2 == e
        g = jnp.concatenate([a[:, LOCAL:] for a in mains], axis=1)
        g_tail = jnp.concatenate([a[:, LOCAL:] for a in tails], axis=1)
        g_tail = jnp.where(own, g_tail.astype(F32), 0.0).astype(BF)
        g = jnp.concatenate([g, g_tail], axis=0)
        loads[2 * e].wait()
        value, slope = gelu_both(dot(x, wi[e], 1, 0))
        active = value.astype(BF)
        loads[2 * e + 1].wait()
        go[e] = dot(active, g, 0, 0)
        store(go.at[e], dw_out.at[e])
        hg = (slope * dot(g, wo[e], 1, 1)).astype(BF)
        gi[e] = dot(x, hg, 0, 0)
        store(gi.at[e], dw_in.at[e])
        result = dot(active, wo[e], 1, 0)
        sent = dot(hg, wi[e], 1, 1)
        tail = (jnp.where(own, result[32 * MAIN :], 0.0), sent[32 * MAIN :])
        if e == 1:
            tail = (tail[0] + held[0], tail[1] + held[1])
        held = tail
        for j in range(4):
            span = slice(LOCAL * j, LOCAL * (j + 1))
            pair = jnp.concatenate([result[: 32 * MAIN, span], sent[: 32 * MAIN, span]], axis=1)
            back[j, :, MAIN * e : MAIN * (e + 1)] = pair.reshape(32, MAIN, PACK).astype(BF)
            if e == 1:
                pair = jnp.concatenate([tail[0][:, span], tail[1][:, span]], axis=1)
                back[j, :, 2 * MAIN :] = pair.reshape(32, 8, PACK).astype(BF)
    for copy in stores:
        copy.wait()


def expert(arrived, w_in, w_out):
    return pl.pallas_call(
        expert_body,
        out_shape=(
            shape(4, 32, SLOT, PACK),
            shape(2, D, D, dtype=F32),
            shape(2, D, D, dtype=F32),
        ),
        in_specs=[VM, HB, HB],
        out_specs=(VM, HB, HB),
        scratch_shapes=[
            pltpu.VMEM((2, D, D), BF),
            pltpu.VMEM((2, D, D), BF),
            pltpu.VMEM((2, D, D), F32),
            pltpu.VMEM((2, D, D), F32),
            DMA((8,)),
        ],
        compiler_params=pltpu.CompilerParams(vmem_limit_bytes=EXPERT_MB * 2**20),
    )(arrived, w_in, w_out)


def combine_body(returned, meta, state, cot, out, tg_o, gate_o, cot_o):
    values = returned[...].astype(F32).reshape(SLOTS, PACK).astype(BF)
    lane = lax.broadcasted_iota(jnp.int32, (SEQ, SLOTS), 1)
    total = unpack(state[...])
    cotangent = jnp.transpose(cot[...].astype(F32))
    cot_o[...] = pack(cotangent).astype(BF)
    token_grad = jnp.zeros((SEQ, LOCAL), F32)
    spread = jnp.zeros((SEQ, 128), F32)
    place = lax.broadcasted_iota(jnp.int32, (SEQ, 128), 1)
    for r in range(2):
        chosen = lane == meta[:, 2 + r : 3 + r].astype(jnp.int32)
        found = dot(jnp.where(chosen, 1.0, 0.0).astype(BF), values, 1, 0)
        routed = found[:, :LOCAL]
        token_grad = token_grad + found[:, LOCAL:]
        total = total + meta[:, r : r + 1] * routed
        spread = jnp.where(
            place == r, jnp.sum(cotangent * routed, axis=1, keepdims=True), spread
        )
    out[...] = jnp.transpose(total).astype(BF)
    out.send()
    tg_o[...] = pack(token_grad).astype(BF)
    gate_o[...] = jnp.transpose(spread)[:8]


def combine(returned, meta, state, cot):
    out = (
        shape(LOCAL, SEQ),
        shape(HALF, PACK),
        shape(8, SEQ, dtype=F32),
        shape(HALF, PACK),
    )
    return local_call(combine_body, "VBVB", (returned, meta, state, cot), "BVVV", out)


def router_body(tg, gate, cp, meta, wp, gains, router, gp_o, grad_o, dr_o, small_o):
    whole = join(wp).astype(F32)
    gain = gain_row(gains, 3)
    normed, scale = normalise(whole, gain)
    summed = gate[0] + gate[1] + gate[2] + gate[3]
    wide = jnp.concatenate([summed, jnp.zeros((120, SEQ), F32)], axis=0)
    turned = jnp.transpose(wide)
    gates = [meta[:, r : r + 1] for r in range(2)]
    gate_grad = [turned[:, r : r + 1] for r in range(2)]
    inner = gates[0] * gate_grad[0] + gates[1] * gate_grad[1]
    routes = meta[:, 4:6].astype(jnp.int32)
    logit_grad = jnp.zeros((SEQ, 64), F32)
    for r in range(2):
        picked_grad = gates[r] * (gate_grad[r] - inner)
        logit_grad = logit_grad + jnp.where(marks_of(routes, r), picked_grad, 0.0)
    logit_grad = logit_grad.astype(BF)
    dr_o[...] = dot(normed, logit_grad, 0, 0).astype(BF)
    ng = join(tg).astype(F32) + dot(logit_grad, router[...], 1, 1)
    state_grad, gain_part = norm_back(ng, whole, scale, gain)
    small_o[...] = jnp.zeros((8, D), F32)
    small_o[4:5, :] = gain_part * 0.25
    grad = join(cp).astype(F32) + state_grad
    split_store(grad_o, grad)
    split_store(gp_o, grad.astype(BF))


def router_bwd(tg, gate, cp, meta, wp, gains, router):
    out = (
        shape(4, HALF, PACK),
        shape(4, HALF, PACK, dtype=F32),
        shape(D, 64),
        shape(8, D, dtype=F32),
    )
    return local_call(
        router_body, "VVVBBBB", (tg, gate, cp, meta, wp, gains, router), "VVBB", out, vmem=50
    )


def places_of():
    gx, gy = lax.axis_index("gx"), lax.axis_index("gy")
    return gx, gy, gx // 8, (gx // 2) % 4, gx % 2


def at(y, z, core):
    return (y * 4 + z) * 2 + core


def greet(peers):
    barrier = pltpu.get_barrier_semaphore()
    for peer in peers:
        pl.semaphore_signal(barrier, inc=1, device_id=peer, device_id_type=MESH)
    pl.semaphore_wait(barrier, len(peers))


def remote(src, dst, send, recv, peer):
    return pltpu.make_async_remote_copy(
        src_ref=src, dst_ref=dst, send_sem=send, recv_sem=recv, device_id=peer, device_id_type=MESH
    )


def gy_peers(gx, gy):
    return [(gx, (gy + d) % 4) for d in (1, 2, 3)]


def grid_peers(gx, gy, y, z, core):
    return (
        [(at((y + d) % 4, z, core), gy) for d in (1, 2, 3)]
        + [(at(y, (z + d) % 4, core), gy) for d in (1, 2, 3)]
        + [(at(y, z, 1 - core), gy)]
    )


def comm_call(body, out, args, scratch, collective_id, specs, out_specs, vmem=16):
    return pl.pallas_call(
        body,
        out_shape=out,
        in_specs=specs,
        out_specs=out_specs,
        scratch_shapes=scratch,
        compiler_params=pltpu.CompilerParams(
            collective_id=collective_id, has_side_effects=True, vmem_limit_bytes=vmem * 2**20
        ),
    )(*args)


class Pool:
    def __init__(self, sems):
        self.sems, self.count = sems, 0

    def take(self):
        self.count += 1
        return self.sems.at[self.count - 1]

    def send(self, src, dst, peer):
        copy = remote(src, dst, self.take(), self.take(), peer)
        copy.start()
        return copy

    def keep(self, src, dst):
        copy = pltpu.make_async_copy(src, dst, self.take())
        copy.start()
        return copy


def together(pieces):
    pieces = list(pieces)
    while pieces:
        pieces = [p for p in pieces if next(p, False) is None]


def gather_weight(pool, w, out, z_first):
    gx, gy, y, z, core = places_of()
    mine = y if z_first else z
    partner = (at(y, z, 1 - core), gy)

    def line(k):
        return out.at[k, :, core] if z_first else out.at[:, k, core]

    def across(d, along_z):
        return (at(y, (z + d) % 4, core) if along_z else at((y + d) % 4, z, core), gy)

    own = pool.keep(w, out.at[y, z, core])
    first = [pool.send(w, out.at[y, z, core], across(d, z_first)) for d in (1, 2, 3)]
    yield
    own.wait()
    for copy in first:
        copy.wait_recv()
    second = [pool.send(line(mine), line(mine), across(d, not z_first)) for d in (1, 2, 3)]
    third = [pool.send(line(mine), line(mine), partner)]
    yield
    for d in (1, 2, 3):
        second[d - 1].wait_recv()
        block = line((mine + 4 - d) % 4)
        third.append(pool.send(block, block, partner))
    yield
    for copy in first + second:
        copy.wait_send()
    for copy in third:
        copy.wait()


def reduce_weight(pool, part, out, y_first, got1, sum1, got2, sum2, got3):
    gx, gy, y, z, core = places_of()
    own = pool.keep(part.at[:, :, core], sum1)
    first = pool.send(part.at[:, :, 1 - core], got1, (at(y, z, 1 - core), gy))
    yield
    own.wait()
    first.wait_recv()
    sum1[...] = (sum1[...].astype(F32) + got1[...].astype(F32)).astype(BF)
    second, third = [], []
    for d in (1, 2, 3):
        if y_first:
            there = (y + d) % 4
            src, peer = sum1.at[there], (at(there, z, core), gy)
        else:
            there = (z + d) % 4
            src, peer = sum1.at[:, there], (at(y, there, core), gy)
        second.append(pool.send(src, got2.at[d - 1], peer))
    yield
    for copy in second:
        copy.wait_recv()
    value = (sum1[y] if y_first else sum1[:, z]).astype(F32)
    for d in range(3):
        value = value + got2[d].astype(F32)
    sum2[...] = value.astype(BF)
    for d in (1, 2, 3):
        there = (z + d) % 4 if y_first else (y + d) % 4
        peer = (at(y, there, core) if y_first else at(there, z, core), gy)
        third.append(pool.send(sum2.at[there], got3.at[d - 1], peer))
    yield
    for copy in third:
        copy.wait_recv()
    value = (sum2[z] if y_first else sum2[y]).astype(F32)
    for d in range(3):
        value = value + got3[d].astype(F32)
    out[...] = value
    for copy in [first] + second + third:
        copy.wait_send()


def reduce_scratch(w):
    return [
        pltpu.VMEM((4, 4, ROWS, w), BF),
        pltpu.VMEM((4, 4, ROWS, w), BF),
        pltpu.VMEM((3, 4, ROWS, w), BF),
        pltpu.VMEM((4, ROWS, w), BF),
        pltpu.VMEM((3, ROWS, w), BF),
    ]


def start_rows(pool, x, gain, xw, gw, state, raw, packed, load):
    gx, gy = lax.axis_index("gx"), lax.axis_index("gy")
    copies = []

    def spread(src, dst):
        copies.extend(pool.send(src, dst.at[gy], (gx, (gy + d) % 4)) for d in (2, 1, 3))
        copies.append(pool.keep(src, dst.at[gy]))

    load.wait()
    packed[...] = pack(raw[...])
    spread(packed, xw)
    spread(gain, gw)
    state[...] = packed[...].astype(F32)
    yield
    for copy in copies:
        copy.wait()


def start_body(w, x, gain, w_all, xw, gw, state, raw, packed, sems):
    gx, gy, y, z, core = places_of()
    pool = Pool(sems)
    halves = [pl.ds(0, D // 2), pl.ds(D // 2, D // 2)]
    load = pool.keep(x, raw)
    greet(grid_peers(gx, gy, y, z, core) + gy_peers(gx, gy))
    together(
        [
            *[
                gather_weight(
                    pool, w.at[:, half], w_all.at[:, :, :, :, half], half.start == 0
                )
                for half in halves
            ],
            start_rows(pool, x, gain, xw, gw, state, raw, packed, load),
        ]
    )


def start_gather(w, x, gain):
    out = (
        shape(4, 4, 2, *w.shape),
        shape(4, HALF, PACK),
        shape(4, 8, 256, dtype=F32),
        shape(HALF, PACK, dtype=F32),
    )
    scratch = [pltpu.VMEM((SEQ, LOCAL), BF), pltpu.VMEM((HALF, PACK), BF), DMA((96,))]
    return comm_call(start_body, out, (w, x, gain), scratch, 0, [HB] * 3, (HB, HB, HB, VM))


def turn_rows(pool, pick, pp, local, new, out, via, recv):
    gx, gy = lax.axis_index("gx"), lax.axis_index("gy")
    there, far = [(gy + 1) % 4, (gy + 3) % 4], (gy + 2) % 4
    beside = [(gx, there[0]), (gx, there[1])]
    size = HALF // 2
    rows = [pl.ds(0, size), pl.ds(size, size)]
    passed = [pool.send(pp.at[far, rows[k]], via.at[k], beside[k]) for k in range(2)]
    direct = [
        pool.send(pp.at[there[k], rows[1 - k]], recv.at[k, rows[1 - k]], beside[k])
        for k in range(2)
    ]
    yield
    for k in range(2):
        half = rows[k]
        passed[k].wait_recv()
        via[k] = (via[k].astype(F32) + pp[there[k], half].astype(F32)).astype(BF)
        direct.append(pool.send(via.at[k], recv.at[k, half], beside[k]))
    yield
    sends = [None] * 4
    for k in range(2):
        half = rows[k]
        direct[1 - k].wait_recv()
        direct[2 + k].wait_recv()
        base = local[gy, half] if pick else local[half]
        total = base + pp[gy, half].astype(F32)
        total = total + recv[0, half].astype(F32) + recv[1, half].astype(F32)
        new[half] = total
        out[gy, half] = total.astype(BF)
        for to in (k, 1 - k):
            block = out.at[gy, half]
            sends[2 * to + k] = pool.send(block, block, beside[to])
    yield
    onward = []
    for k in range(2):
        sends[2 * k + k].wait_recv()
        block = out.at[there[1 - k], rows[k]]
        onward.append(pool.send(block, block, beside[k]))
    yield
    for k in range(2):
        sends[2 * k + 1 - k].wait_recv()
    for copy in onward:
        copy.wait()
    for copy in passed + direct + sends:
        copy.wait_send()


def turn_body(pick, n_gather, n_reduce, *refs):
    n = 2 + n_gather + n_reduce
    pp, local = refs[:2]
    extra, (new, out) = refs[2:n], refs[n : n + 2]
    made = refs[n + 2 : 2 * n]
    via, recv = refs[2 * n : 2 * n + 2]
    scratch, sems = refs[2 * n + 2 : -1], refs[-1]
    gx, gy, y, z, core = places_of()
    pool = Pool(sems)
    greet(
        [(gx, (gy + 1) % 4), (gx, (gy + 3) % 4)]
        + (grid_peers(gx, gy, y, z, core) if n_gather + n_reduce else [])
    )
    pieces = [turn_rows(pool, pick, pp, local, new, out, via, recv)]
    for i in range(n_gather):
        pieces.append(gather_weight(pool, extra[i], made[i], i % 2 == 0))
    for i in range(n_reduce):
        pieces.append(
            reduce_weight(pool, extra[i], made[i], i % 2 == 0, *scratch[5 * i : 5 * i + 5])
        )
    together(pieces)


def turn(collective_id, pp, local, gather=(), reduce=()):
    out = [shape(HALF, PACK, dtype=F32), shape(4, HALF, PACK)]
    out += [shape(4, 4, 2, *w.shape) for w in gather]
    out += [shape(ROWS, p.shape[-1], dtype=F32) for p in reduce]
    reduce = [p.reshape(4, 4, 2, ROWS, p.shape[-1]) for p in reduce]
    scratch = [pltpu.VMEM((2, HALF // 2, PACK), BF), pltpu.VMEM((2, HALF, PACK), BF)]
    for p in reduce:
        scratch += reduce_scratch(p.shape[-1])
    made = comm_call(
        functools.partial(turn_body, local.ndim == 3, len(gather), len(reduce)),
        tuple(out),
        (pp, local, *gather, *reduce),
        scratch + [DMA((96,))],
        collective_id,
        [VM, VM] + [HB] * (len(gather) + len(reduce)),
        tuple([VM, VM] + [HB] * len(gather) + [VM] * len(reduce)),
    )
    kept = [m.reshape(D, m.shape[-1]) for m in made[2 : 2 + len(gather)]]
    return [*made[:2], *kept, *made[2 + len(gather) :]]


def gather_body(tg, gate, cot, tw, gw, cw, sx, rx):
    gx, gy = lax.axis_index("gx"), lax.axis_index("gy")
    greet(gy_peers(gx, gy))
    copies = []
    for k, (src, dst) in enumerate(((gate, gw), (tg, tw), (cot, cw))):
        for d in (2, 1, 3):
            copy = remote(src, dst.at[gy], sx.at[k, d - 1], rx.at[k, d - 1], (gx, (gy + d) % 4))
            copy.start()
            copies.append(copy)
        dst[gy] = src[...]
    for copy in copies:
        copy.wait()


def gather_tokens(tg, gate, cot):
    return comm_call(
        gather_body,
        (shape(4, HALF, PACK), shape(4, 8, SEQ, dtype=F32), shape(4, HALF, PACK)),
        (tg, gate, cot),
        [DMA((3, 3)), DMA((3, 3))],
        7,
        [VM] * 3,
        (VM,) * 3,
    )


AHEAD = 16
LAG = 8


def to_experts_body(sent, out, own, sa, ra, sg, rg, sf, rf):
    gx, gy, y, z, core = places_of()
    there = [(gy + 1) % 4, (gy + 3) % 4]
    far = (gy + 2) % 4
    beside = [(gx, there[0]), (gx, there[1])]
    greet(beside + [((gx + k) % 32, gy) for k in range(1, 32)])
    keep = pltpu.make_async_copy(sent.at[gx], out.at[gy, gx], own)
    keep.start()

    def shift(k, sign):
        far_y, far_z, far_core = k // 8, (k // 2) % 4, k % 2
        return at((y + 4 + sign * far_y) % 4, (z + 4 + sign * far_z) % 4, (core + far_core) % 2)

    def push(k):
        peer = shift(k, 1)
        remote(sent.at[peer], out.at[gy, gx], sa, ra.at[k], (peer, gy)).start()

    def spread(k):
        block = out.at[gy, shift(k, -1)]
        for to in range(2):
            remote(block, block, sg.at[to], rg.at[to, k], beside[to]).start()

    def arrive(k):
        remote(sent.at[0], out.at[gy, shift(k, -1)], sa, ra.at[k], beside[0]).wait_recv()
        spread(k)

    def relay(k, to):
        source = shift(k, -1)
        for way in range(2):
            block = out.at[there[1 - way], source]
            remote(block, block, sg.at[way], rg.at[way, k], beside[way]).wait_recv()
        block = out.at[there[1 - to], source]
        remote(block, block, sf.at[to], rf.at[to], beside[to]).start()

    for k in range(1, AHEAD):
        push(k)
    keep.wait()
    spread(0)
    for k in range(1, LAG):
        arrive(k)

    def step(i, carry):
        for to in range(2):
            k = LAG + 2 * i + to

            @pl.when(k + AHEAD - LAG < 32)
            def _():
                push(k + AHEAD - LAG)

            arrive(k)
            relay(k - LAG, to)
        return carry

    lax.fori_loop(0, (32 - LAG) // 2, step, 0)
    for k in range(32 - LAG, 32):
        relay(k, k % 2)
    many = sent.at[pl.ds(0, 31)]
    remote(many, many, sa, ra.at[0], beside[0]).wait_send()
    for to in range(2):
        half = out.at[far, pl.ds(0, 16)]
        remote(half, half, sf.at[to], rf.at[to], beside[to]).wait()
        remote(out.at[gy], out.at[gy], sg.at[to], rg.at[to, 0], beside[to]).wait_send()


def to_experts(sent):
    return comm_call(
        to_experts_body,
        shape(4, 32, SLOT, PACK),
        (sent,),
        [
            DMA(()),
            DMA(()),
            DMA((32,)),
            DMA((2,)),
            DMA((2, 32)),
            DMA((2,)),
            DMA((2,)),
        ],
        8,
        [VM],
        VM,
        vmem=12,
    )


GROUPS = 8
BEGUN = 4


def from_experts_body(back, out, via, part, recv, total, sems, s4, r4):
    gx, gy = lax.axis_index("gx"), lax.axis_index("gy")
    there = [(gy + 1) % 4, (gy + 3) % 4]
    far = (gy + 2) % 4
    beside = [(gx, there[0]), (gx, there[1])]
    greet(beside + [((gx + k) % 32, gy) for k in range(1, 32)])
    pool = Pool(sems)
    passing, direct, summed = [], [], []

    def place(c):
        return (c + gx) % GROUPS

    def begin(c):
        to = c % 2
        passing.append(pool.send(back.at[far, :, place(c)], via.at[c], beside[to]))
        direct.append(
            pool.send(back.at[there[1 - to], :, place(c)], recv.at[1 - to, c], beside[1 - to])
        )

    def middle(c):
        to = c % 2
        passing[c].wait_recv()
        value = back[there[to], :, place(c)].astype(F32) + via[c].astype(F32)
        part[c] = value.astype(BF)
        summed.append(pool.send(part.at[c], recv.at[to, c], beside[to]))

    def end(c):
        direct[c].wait_recv()
        summed[c].wait_recv()
        value = back[gy, :, place(c)].astype(F32)
        value = value + recv[0, c].astype(F32) + recv[1, c].astype(F32)
        total[:, place(c)] = value.astype(BF)
        for i in range(4):
            peer = i * GROUPS + place(c)

            @pl.when(peer != gx)
            def _():
                remote(
                    total.at[i, place(c)],
                    out.at[gx // GROUPS, gx % GROUPS],
                    s4.at[peer],
                    r4.at[gx],
                    (peer, gy),
                ).start()

            @pl.when(peer == gx)
            def _():
                out[gx // GROUPS, gx % GROUPS] = total[i, place(c)]

    for c in range(BEGUN):
        begin(c)
    middle(0)
    middle(1)
    for c in range(GROUPS):
        if c + BEGUN < GROUPS:
            begin(c + BEGUN)
        if c + 2 < GROUPS:
            middle(c + 2)
        end(c)
    for copy in passing + direct + summed:
        copy.wait_send()

    def finish(k, carry):
        source = (gx + k) % 32
        remote(
            total.at[0, 0],
            out.at[source // GROUPS, source % GROUPS],
            s4.at[source],
            r4.at[source],
            beside[0],
        ).wait()
        return carry

    lax.fori_loop(1, 32, finish, 0)


def from_experts(back):
    full = (4, GROUPS, SLOT, PACK)
    return comm_call(
        from_experts_body,
        shape(*full),
        (back.reshape(4, *full),),
        [
            pltpu.VMEM((GROUPS, 4, SLOT, PACK), BF),
            pltpu.VMEM((GROUPS, 4, SLOT, PACK), BF),
            pltpu.VMEM((2, GROUPS, 4, SLOT, PACK), BF),
            pltpu.VMEM(full, BF),
            DMA((48,)),
            DMA((32,)),
            DMA((32,)),
        ],
        9,
        [VM],
        VM,
        vmem=16,
    ).reshape(32, SLOT, PACK)


def last_rows(pool, pp, local, grad_o, recv):
    gx, gy = lax.axis_index("gx"), lax.axis_index("gy")
    copies = [
        pool.send(pp.at[(gy + d) % 4], recv.at[d - 1], (gx, (gy + d) % 4)) for d in (2, 1, 3)
    ]
    yield
    yield
    for copy in copies:
        copy.wait_recv()
    total = local[...] + pp[gy].astype(F32)
    for d in range(3):
        total = total + recv[d].astype(F32)
    grad_o[...] = unpack(total).astype(BF)
    for copy in copies:
        copy.wait_send()


def last_small(pool, raw, loads, bias_o, gain_o, got, held):
    gx, gy, y, z, core = places_of()
    for copy in loads:
        copy.wait()
    held[0, 0:8] = raw[0] + raw[1]
    held[0, 8:16] = raw[2] + raw[3]
    groups = [
        [(at(y, z, 1 - core), gy)],
        [(at((y + d) % 4, z, core), gy) for d in (1, 2, 3)],
        [(at(y, (z + d) % 4, core), gy) for d in (1, 2, 3)],
        gy_peers(gx, gy),
    ]
    copies = []
    for stage, peers in enumerate(groups):
        now = [
            pool.send(held.at[stage], got.at[3 * stage + k], peer) for k, peer in enumerate(peers)
        ]
        copies += now
        yield
        value = held[stage]
        for k, copy in enumerate(now):
            copy.wait_recv()
            value = value + got[3 * stage + k]
        if stage < 3:
            held[stage + 1] = value
    bias_o[...] = held[3, 0:8, :128]
    for j in range(4):

        @pl.when(gy == j)
        def _():
            for k, row in enumerate((0, 8, 4, 12)):
                gain_o[k : k + 1, :] = value[row : row + 1, LOCAL * j : LOCAL * (j + 1)]

    for copy in copies:
        copy.wait_send()


def last_body(part, pp, local, a, b, c, d, out, grad_o, bias_o, gain_o, *scratch):
    pieces, (raw, recv, got, held, sems) = (scratch[:5], scratch[5:10]), scratch[10:]
    halves = [pl.ds(0, D // 2), pl.ds(D // 2, D // 2)]
    gx, gy, y, z, core = places_of()
    pool = Pool(sems)
    loads = [pool.keep(src, raw.at[k]) for k, src in enumerate((a, b, c, d))]
    greet(grid_peers(gx, gy, y, z, core) + gy_peers(gx, gy))
    together(
        [
            *[
                reduce_weight(
                    pool, part.at[:, :, :, :, half], out.at[:, half], half.start == 0, *piece
                )
                for half, piece in zip(halves, pieces)
            ],
            last_rows(pool, pp, local, grad_o, recv),
            last_small(pool, raw, loads, bias_o, gain_o, got, held),
        ]
    )


def last_sums(part, pp, local, smalls):
    out = (
        shape(ROWS, D, dtype=F32),
        shape(SEQ, LOCAL),
        shape(8, 128, dtype=F32),
        shape(4, LOCAL, dtype=F32),
    )
    scratch = reduce_scratch(D // 2) * 2 + [
        pltpu.VMEM((4, 8, D), F32),
        pltpu.VMEM((3, HALF, PACK), BF),
        pltpu.VMEM((12, 16, D), F32),
        pltpu.VMEM((4, 16, D), F32),
        DMA((96,)),
    ]
    return comm_call(
        last_body,
        out,
        (part.reshape(4, 4, 2, ROWS, D), pp, local, *smalls),
        scratch,
        6,
        [HB, VM, VM] + [HB] * 4,
        (VM,) * 4,
    )


def shards(
    block_input,
    cotangent,
    doc_ids,
    routes,
    qkv_weight,
    out_weight,
    rel_bias,
    norm_gain,
    ff_in,
    ff_out,
    router,
    expert_in,
    expert_out,
):
    picks = jnp.asarray(bucket_picks())
    doc = doc_ids.reshape(1, SEQ)
    layers = [
        jnp.concatenate([qkv_weight[l].reshape(ROWS, 576), out_weight[l]], axis=1)
        for l in range(2)
    ]
    gain_wide = jnp.pad(norm_gain.reshape(4, LOCAL), ((0, 4), (0, 64)))
    w0, xw, gains, state = start_gather(layers[0], block_input, gain_wide)
    w0 = w0.reshape(D, D)
    pp, *kept0 = attn_fwd(0, xw, "B", gains, w0, rel_bias, picks, doc)
    state, sw1, w_in, w_out = turn(1, pp, state, gather=(ff_in, ff_out))
    pp, pre = ff_fwd(sw1, gains, w_in, w_out)
    state, sw2, w1, w_router = turn(2, pp, state, gather=(layers[1], router))
    pp, *kept1 = attn_fwd(1, sw2, "V", gains, w1, rel_bias, picks, doc)
    state, sw3 = turn(3, pp, state)
    cot = cotangent.T
    sent, meta = dispatch(sw3, state, cot, gains, w_router, routes.T)
    arrived = to_experts(sent)
    back, expert_in_grad, expert_out_grad = expert(arrived, expert_in, expert_out)
    returned = from_experts(back)
    block_output, tg, gate, cot = combine(returned, meta, state, cot)
    block_output = block_output.T
    tw, gate_all, cw = gather_tokens(tg, gate, cot)
    gp, grad_all, d_router, small3 = router_bwd(
        tw, gate_all, cw, meta, sw3, gains, w_router
    )
    pp, d_w1, small2 = attn_bwd(1, gp, sw2, gains, w1, *kept1, picks)
    grad, gp, g1, router_grad = turn(4, pp, grad_all, reduce=(d_w1, d_router))
    pp, d_in, d_out, small1 = ff_bwd(gp, sw1, gains, w_in, w_out, pre)
    grad, gp, ff_in_grad, ff_out_grad = turn(5, pp, grad, reduce=(d_in, d_out))
    pp, d_w0, small0 = attn_bwd(0, gp, xw, gains, w0, *kept0, picks)
    g0, input_grad, bias, gain_grad = last_sums(d_w0, pp, grad, (small0, small2, small1, small3))
    both = jnp.stack([g0, g1])
    qkv_grad = both[:, :, :576].reshape(2, ROWS, 3, LOCAL)
    out_grad = both[:, :, 576:]
    bias_grad = bias.reshape(2, 4, 128)[:, 1:, :NB]
    gain_grad = gain_grad.reshape(2, 2, LOCAL)
    return (
        block_output,
        input_grad,
        qkv_grad,
        out_grad,
        bias_grad,
        gain_grad,
        ff_in_grad,
        ff_out_grad,
        router_grad,
        expert_in_grad,
        expert_out_grad,
    )


def solution(mesh):
    in_specs = (
        P("gx", "gy"),
        P("gx", "gy"),
        P("gx"),
        P("gx", None),
        P(None, "gx", None, "gy"),
        P(None, "gx", "gy"),
        P(None, "gy", None),
        P(None, None, "gy"),
        P("gx", "gy"),
        P("gx", "gy"),
        P("gx", None),
        P("gx", None, "gy"),
        P("gx", "gy", None),
    )
    out_specs = (
        P("gx", "gy"),
        P("gx", "gy"),
        P(None, "gx", None, "gy"),
        P(None, "gx", "gy"),
        P(None, "gy", None),
        P(None, None, "gy"),
        P("gx", "gy"),
        P("gx", "gy"),
        P("gx", None),
        P("gx", None, "gy"),
        P("gx", "gy", None),
    )
    return jax.shard_map(shards, mesh=mesh, in_specs=in_specs, out_specs=out_specs, check_vma=False)
```

```python
import functools
import math

import numpy as np

import jax
import jax.numpy as jnp
from jax import lax
from jax.experimental import pallas as pl
from jax.experimental.pallas import tpu as pltpu
from jax.sharding import PartitionSpec as P

NB = 32
D = 768
LOCAL = 192
SEQ = 512
HALF = 256
PACK = 384
ROWS = 24
HEADS = 3
HD = 64
MAIN = 16
SLOT = 40
SLOTS = 32 * SLOT
EXPERT_MB = 36
BF = jnp.bfloat16
F32 = jnp.float32
MESH = pl.DeviceIdType.MESH
DMA = pltpu.SemaphoreType.DMA
VM = pl.BlockSpec(memory_space=pltpu.VMEM)
HB = pl.BlockSpec(memory_space=pltpu.HBM)
epsilon = 1e-06
highest = lax.Precision.HIGHEST
bucket_edges = [int(math.ceil(16.0 * 8.0 ** (step / 16.0))) for step in range(1, 16)]


def bucket_picks():
    distance = (SEQ - np.arange(SEQ)) % SEQ
    bucket = np.minimum(distance, 16)
    for edge in bucket_edges:
        bucket = bucket + (distance >= edge)
    return (bucket[None, :] == np.arange(NB)[:, None]).astype(np.float32)


def dot(a, b, ca, cb):
    return lax.dot_general(a, b, (((ca,), (cb,)), ((), ())), preferred_element_type=F32)


def unpack(p):
    return jnp.concatenate([p[:, :LOCAL], p[:, LOCAL:]], axis=0)


def pack(a):
    half = a.shape[0] // 2
    return jnp.concatenate([a[:half], a[half:]], axis=1)


def join(ref):
    return jnp.concatenate([unpack(ref[j]) for j in range(4)], axis=1)


def split_store(ref, a):
    for j in range(4):
        ref[j] = pack(a[:, LOCAL * j : LOCAL * (j + 1)])


def gain_row(ref, k):
    return jnp.concatenate([ref[j, k : k + 1, :LOCAL] for j in range(4)], axis=1)


def normalise(whole, gain):
    scale = lax.rsqrt(jnp.mean(whole * whole, axis=-1, keepdims=True) + epsilon)
    return (whole * scale * gain).astype(BF), scale


def norm_back(normed_grad, whole, scale, gain):
    weighted = normed_grad * gain
    inner = jnp.mean(weighted * whole, axis=-1, keepdims=True)
    state_grad = weighted * scale - whole * (scale * scale * scale * inner)
    gain_part = jnp.sum(normed_grad * whole * scale, axis=0, keepdims=True)
    return state_grad, gain_part


def gelu_both(v):
    c = math.sqrt(2.0 / math.pi)
    t = jnp.tanh(c * (v + 0.044715 * (v * v * v)))
    value = 0.5 * v * (1.0 + t)
    slope = 0.5 * (1.0 + t) + 0.5 * v * (1.0 - t * t) * (c * (1.0 + 3.0 * 0.044715 * (v * v)))
    return value, slope


class Fetched:
    def __init__(self, ref, copy):
        self.ref, self.copy = ref, copy

    def __getitem__(self, index):
        if self.copy is not None:
            self.copy.wait()
            self.copy = None
        return self.ref[index]


class Kept:
    def __init__(self, ref, copy):
        self.ref, self.copy, self.sent = ref, copy, False

    def __setitem__(self, index, value):
        self.ref[index] = value

    def send(self):
        if not self.sent:
            self.copy.start()
            self.sent = True


def staged_body(body, kinds, out_kinds, *refs):
    n, m = len(kinds), len(out_kinds)
    buffers, sems = list(refs[n + m : -1]), refs[-1]
    count, held = 0, []
    for k, ref in zip(kinds, refs[:n]):
        if k == "B":
            copy = pltpu.make_async_copy(ref, buffers[count], sems.at[count])
            copy.start()
            ref, count = Fetched(buffers[count], copy), count + 1
        held.append(ref)
    results = []
    for k, ref in zip(out_kinds, refs[n : n + m]):
        if k == "B":
            copy = pltpu.make_async_copy(buffers[count], ref, sems.at[count])
            ref, count = Kept(buffers[count], copy), count + 1
        results.append(ref)
    body(*held, *results)
    for ref in held:
        if isinstance(ref, Fetched):
            ref[...]
    for ref in results:
        if isinstance(ref, Kept):
            ref.send()
    for ref in results:
        if isinstance(ref, Kept):
            ref.copy.wait()


def local_call(body, kinds, args, out_kinds, out, vmem=28):
    moved = [a for k, a in zip(kinds, args) if k == "B"]
    moved += [o for k, o in zip(out_kinds, out) if k == "B"]
    return pl.pallas_call(
        functools.partial(staged_body, body, kinds, out_kinds),
        out_shape=out,
        in_specs=[VM if k == "V" else HB for k in kinds],
        out_specs=tuple(VM if k == "V" else HB for k in out_kinds),
        scratch_shapes=[pltpu.VMEM(a.shape, a.dtype) for a in moved] + [DMA((len(moved),))],
        compiler_params=pltpu.CompilerParams(vmem_limit_bytes=vmem * 2**20),
    )(*args)


def shape(*dims, dtype=BF):
    return jax.ShapeDtypeStruct(dims, dtype)


def attn_fwd_body(layer, wp, gains, w, table, picks, doc, pp, mixed_o, ctx_o, probs_o):
    whole = join(wp).astype(F32)
    normed, _ = normalise(whole, gain_row(gains, 2 * layer))
    mixed = dot(normed, w[:, :576], 1, 0).astype(BF)
    mixed_o[...] = mixed
    mixed_o.send()
    row = lax.broadcasted_iota(jnp.int32, (SEQ, SEQ), 0)
    col = lax.broadcasted_iota(jnp.int32, (SEQ, SEQ), 1)
    doc_r = doc[...].astype(F32)
    doc_c = jnp.transpose(jnp.broadcast_to(doc_r, (128, SEQ)))[:, :1]
    allowed = (col <= row) & (doc_c == doc_r)
    few = jnp.concatenate([table[layer], jnp.zeros((8 - HEADS, NB), F32)], axis=0)
    lines = lax.dot_general(
        few, picks[...], (((1,), (0,)), ((), ())), precision=highest, preferred_element_type=F32
    )
    context = []
    for h in range(HEADS):
        q = mixed[:, HD * h : HD * (h + 1)]
        k = mixed[:, LOCAL + HD * h : LOCAL + HD * (h + 1)]
        v = mixed[:, 2 * LOCAL + HD * h : 2 * LOCAL + HD * (h + 1)]
        line = jnp.broadcast_to(lines[h : h + 1, :], (SEQ, SEQ))
        bias = pltpu.roll(line, 0, 1, stride=1, stride_axis=0)
        s = jnp.where(allowed, dot(q, k, 1, 1) * 0.125 + bias, -1000000000.0)
        e = jnp.exp(s - jnp.max(s, axis=-1, keepdims=True))
        p = (e * (1.0 / jnp.sum(e, axis=-1, keepdims=True))).astype(BF)
        probs_o[h] = p
        context.append(dot(p, v, 1, 0))
    ctx = jnp.concatenate(context, axis=1).astype(BF)
    ctx_o[...] = ctx
    ctx_o.send()
    probs_o.send()
    split_store(pp, dot(ctx, w[:, 576:], 1, 1).astype(BF))


def attn_fwd(layer, wp, kind, gains, w, table, picks, doc):
    out = (
        shape(4, HALF, PACK),
        shape(SEQ, 576),
        shape(SEQ, LOCAL),
        shape(HEADS, SEQ, SEQ),
    )
    return local_call(
        functools.partial(attn_fwd_body, layer),
        kind + "BBBBB",
        (wp, gains, w, table, picks, doc),
        "VBBB",
        out,
    )


def attn_bwd_body(layer, gp, wp, gains, w, mixed, ctx, probs, picks, pp, dw, small_o):
    whole = join(wp).astype(F32)
    gain = gain_row(gains, 2 * layer)
    normed, scale = normalise(whole, gain)
    rows = join(gp)
    cg = dot(rows, w[:, 576:], 1, 0).astype(BF)
    dw[:, 576:] = dot(rows, ctx[...], 0, 0).astype(BF)
    row = lax.broadcasted_iota(jnp.int32, (SEQ, SEQ), 0)
    col = lax.broadcasted_iota(jnp.int32, (SEQ, SEQ), 1)
    flip = jnp.where(row + col == SEQ - 1, 1.0, 0.0).astype(BF)
    dq, dk, dv = [], [], []
    cols = []
    for h in range(HEADS):
        q = mixed[:, HD * h : HD * (h + 1)]
        k = mixed[:, LOCAL + HD * h : LOCAL + HD * (h + 1)]
        v = mixed[:, 2 * LOCAL + HD * h : 2 * LOCAL + HD * (h + 1)]
        c = cg[:, HD * h : HD * (h + 1)]
        p = probs[h]
        pf = p.astype(F32)
        pg = dot(c, v, 1, 1)
        sg = (pf * (pg - jnp.sum(pf * pg, axis=-1, keepdims=True))).astype(BF)
        dq.append(dot(sg, k, 1, 0) * 0.125)
        dk.append(dot(sg, q, 0, 0) * 0.125)
        dv.append(dot(p, c, 0, 0))
        rolled = pltpu.roll(dot(flip, sg, 1, 0), 1, 1, stride=1, stride_axis=0)
        cols.append(jnp.sum(rolled, axis=0, keepdims=True))
    dmixed = jnp.concatenate(dq + dk + dv, axis=1).astype(BF)
    dw[:, :576] = dot(normed, dmixed, 0, 0).astype(BF)
    dw.send()
    ng = dot(dmixed, w[:, :576], 1, 1)
    state_grad, gain_part = norm_back(ng, whole, scale, gain)
    split_store(pp, state_grad.astype(BF))
    few = jnp.concatenate(cols + [jnp.zeros((8 - HEADS, SEQ), F32)], axis=0)
    table = lax.dot_general(
        few, picks[...], (((1,), (1,)), ((), ())), precision=highest, preferred_element_type=F32
    )
    small_o[...] = jnp.zeros((8, D), F32)
    small_o[4 * layer : 4 * layer + 1, :] = gain_part
    small_o[4 * layer + 1 : 4 * layer + 4, :NB] = table[:HEADS]


def attn_bwd(layer, gp, wp, gains, w, mixed, ctx, probs, picks):
    out = (shape(4, HALF, PACK), shape(D, D), shape(8, D, dtype=F32))
    return local_call(
        functools.partial(attn_bwd_body, layer),
        "VBBBBBBB",
        (gp, wp, gains, w, mixed, ctx, probs, picks),
        "VBB",
        out,
    )


def ff_fwd_body(wp, gains, w_in, w_out, pp, pre_o):
    whole = join(wp).astype(F32)
    normed, _ = normalise(whole, gain_row(gains, 1))
    pre = dot(normed, w_in[...], 1, 0)
    pre_o[...] = pre
    pre_o.send()
    active = gelu_both(pre)[0].astype(BF)
    split_store(pp, dot(active, w_out[...], 1, 1).astype(BF))


def ff_fwd(wp, gains, w_in, w_out):
    out = (shape(4, HALF, PACK), shape(SEQ, D, dtype=F32))
    return local_call(ff_fwd_body, "VBBB", (wp, gains, w_in, w_out), "VB", out)


def ff_bwd_body(gp, wp, gains, w_in, w_out, pre, pp, dw_in, dw_out, small_o):
    whole = join(wp).astype(F32)
    gain = gain_row(gains, 1)
    normed, scale = normalise(whole, gain)
    rows = join(gp)
    value, slope = gelu_both(pre[...])
    dw_out[...] = dot(rows, value.astype(BF), 0, 0).astype(BF)
    dw_out.send()
    hg = (slope * dot(rows, w_out[...], 1, 0)).astype(BF)
    dw_in[...] = dot(normed, hg, 0, 0).astype(BF)
    dw_in.send()
    ng = dot(hg, w_in[...], 1, 1)
    state_grad, gain_part = norm_back(ng, whole, scale, gain)
    split_store(pp, state_grad.astype(BF))
    small_o[...] = jnp.zeros((8, D), F32)
    small_o[0:1, :] = gain_part


def ff_bwd(gp, wp, gains, w_in, w_out, pre):
    out = (shape(4, HALF, PACK), shape(D, D), shape(D, D), shape(8, D, dtype=F32))
    return local_call(ff_bwd_body, "VBBBBB", (gp, wp, gains, w_in, w_out, pre), "VBBB", out)


def marks_of(routes, r):
    lane = lax.broadcasted_iota(jnp.int32, (SEQ, 64), 1)
    return lane == routes[:, r : r + 1]


def dispatch_body(wp, state, cot, gains, router, turned_routes, out, meta_o):
    whole = join(wp).astype(F32)
    normed, scale = normalise(whole, gain_row(gains, 3))
    logits = dot(normed, router[...], 1, 0)
    listed = jnp.concatenate([turned_routes[...].astype(F32), jnp.zeros((126, SEQ), F32)], axis=0)
    routes = jnp.transpose(listed).astype(jnp.int32)
    own_gain = gains[lax.axis_index("gy"), 3:4, :LOCAL]
    marks = [marks_of(routes, r) for r in range(2)]
    picked = [jnp.sum(jnp.where(m, logits, 0.0), axis=1, keepdims=True) for m in marks]
    top = jnp.maximum(picked[0], picked[1])
    weights = [jnp.exp(v - top) for v in picked]
    total = weights[0] + weights[1]
    gates = [v / total for v in weights]
    ones = (jnp.where(marks[0], 1.0, 0.0) + jnp.where(marks[1], 1.0, 0.0)).astype(BF)
    row = lax.broadcasted_iota(jnp.int32, (SEQ, SEQ), 0)
    col = lax.broadcasted_iota(jnp.int32, (SEQ, SEQ), 1)
    before = dot(jnp.where(col < row, 1.0, 0.0).astype(BF), ones, 1, 0)
    places = [jnp.sum(jnp.where(m, before, 0.0), axis=1, keepdims=True) for m in marks]
    slots = []
    for r in range(2):
        chosen = routes[:, r : r + 1]
        second = (chosen % 2).astype(F32)
        inside = jnp.where(
            places[r] < MAIN, places[r] + MAIN * second, places[r] + MAIN + 2.0 * second
        )
        slots.append(inside + SLOT * (chosen // 2).astype(F32))
    lane = lax.broadcasted_iota(jnp.int32, (SEQ, 128), 1)
    meta = jnp.zeros((SEQ, 128), F32)
    listing = [routes[:, r : r + 1].astype(F32) for r in range(2)]
    for index, value in enumerate(gates + slots + listing):
        meta = jnp.where(lane == index, value, meta)
    meta_o[...] = meta
    meta_o.send()
    turned = jnp.transpose(meta)
    own = (unpack(state[...]) * scale * own_gain).astype(BF)
    cotangent = jnp.transpose(cot[...].astype(F32))
    sent = jnp.zeros((SLOTS, PACK), F32)
    place = lax.broadcasted_iota(jnp.int32, (SLOTS, SEQ), 0)
    for r in range(2):
        chosen = place == turned[2 + r : 3 + r, :].astype(jnp.int32)
        rows = jnp.concatenate([own, (gates[r] * cotangent).astype(BF)], axis=1)
        sent = sent + dot(jnp.where(chosen, 1.0, 0.0).astype(BF), rows, 1, 0)
    out[...] = sent.reshape(32, SLOT, PACK).astype(BF)


def dispatch(wp, state, cot, gains, router, routes):
    out = (shape(32, SLOT, PACK), shape(SEQ, 128, dtype=F32))
    return local_call(
        dispatch_body, "VVBBBB", (wp, state, cot, gains, router, routes), "VB", out
    )


def expert_body(arrived, w_in, w_out, back, dw_in, dw_out, wi, wo, gi, go, sems):
    loads, stores = [], []
    for e in range(2):
        for k, (src, dst) in enumerate(((w_in.at[e], wi.at[e]), (w_out.at[e], wo.at[e]))):
            copy = pltpu.make_async_copy(src, dst, sems.at[2 * e + k])
            copy.start()
            loads.append(copy)

    def store(src, dst):
        copy = pltpu.make_async_copy(src, dst, sems.at[4 + len(stores)])
        copy.start()
        stores.append(copy)

    halves = [arrived[j].astype(F32) for j in range(4)]
    tails = [a[:, 2 * MAIN :].reshape(256, PACK).astype(BF) for a in halves]
    tail_row = lax.broadcasted_iota(jnp.int32, (256, D), 0) % 8
    held = None
    for e in range(2):
        mains = [
            a[:, MAIN * e : MAIN * (e + 1)].reshape(32 * MAIN, PACK).astype(BF) for a in halves
        ]
        both = [jnp.concatenate([m, t], axis=0) for m, t in zip(mains, tails)]
        x = jnp.concatenate([a[:, :LOCAL] for a in both], axis=1)
        own = tail_row // 2 == e
        g = jnp.concatenate([a[:, LOCAL:] for a in mains], axis=1)
        g_tail = jnp.concatenate([a[:, LOCAL:] for a in tails], axis=1)
        g_tail = jnp.where(own, g_tail.astype(F32), 0.0).astype(BF)
        g = jnp.concatenate([g, g_tail], axis=0)
        loads[2 * e].wait()
        value, slope = gelu_both(dot(x, wi[e], 1, 0))
        active = value.astype(BF)
        loads[2 * e + 1].wait()
        go[e] = dot(active, g, 0, 0)
        store(go.at[e], dw_out.at[e])
        hg = (slope * dot(g, wo[e], 1, 1)).astype(BF)
        gi[e] = dot(x, hg, 0, 0)
        store(gi.at[e], dw_in.at[e])
        result = dot(active, wo[e], 1, 0)
        sent = dot(hg, wi[e], 1, 1)
        tail = (jnp.where(own, result[32 * MAIN :], 0.0), sent[32 * MAIN :])
        if e == 1:
            tail = (tail[0] + held[0], tail[1] + held[1])
        held = tail
        for j in range(4):
            span = slice(LOCAL * j, LOCAL * (j + 1))
            pair = jnp.concatenate([result[: 32 * MAIN, span], sent[: 32 * MAIN, span]], axis=1)
            back[j, :, MAIN * e : MAIN * (e + 1)] = pair.reshape(32, MAIN, PACK).astype(BF)
            if e == 1:
                pair = jnp.concatenate([tail[0][:, span], tail[1][:, span]], axis=1)
                back[j, :, 2 * MAIN :] = pair.reshape(32, 8, PACK).astype(BF)
    for copy in stores:
        copy.wait()


def expert(arrived, w_in, w_out):
    return pl.pallas_call(
        expert_body,
        out_shape=(
            shape(4, 32, SLOT, PACK),
            shape(2, D, D, dtype=F32),
            shape(2, D, D, dtype=F32),
        ),
        in_specs=[VM, HB, HB],
        out_specs=(VM, HB, HB),
        scratch_shapes=[
            pltpu.VMEM((2, D, D), BF),
            pltpu.VMEM((2, D, D), BF),
            pltpu.VMEM((2, D, D), F32),
            pltpu.VMEM((2, D, D), F32),
            DMA((8,)),
        ],
        compiler_params=pltpu.CompilerParams(vmem_limit_bytes=EXPERT_MB * 2**20),
    )(arrived, w_in, w_out)


def combine_body(returned, meta, state, cot, gains, out, tg_o, gate_o):
    values = returned[...].astype(F32).reshape(SLOTS, PACK).astype(BF)
    lane = lax.broadcasted_iota(jnp.int32, (SEQ, SLOTS), 1)
    total = unpack(state[...])
    cotangent = jnp.transpose(cot[...].astype(F32))
    token_grad = jnp.zeros((SEQ, LOCAL), F32)
    spread = jnp.zeros((SEQ, 128), F32)
    place = lax.broadcasted_iota(jnp.int32, (SEQ, 128), 1)
    for r in range(2):
        chosen = lane == meta[:, 2 + r : 3 + r].astype(jnp.int32)
        found = dot(jnp.where(chosen, 1.0, 0.0).astype(BF), values, 1, 0)
        routed = found[:, :LOCAL]
        token_grad = token_grad + found[:, LOCAL:]
        total = total + meta[:, r : r + 1] * routed
        spread = jnp.where(
            place == r, jnp.sum(cotangent * routed, axis=1, keepdims=True), spread
        )
    out[...] = jnp.transpose(total).astype(BF)
    out.send()
    tg_o[...] = token_grad
    own_gain = gains[lax.axis_index("gy"), 3:4, :LOCAL]
    inner = jnp.sum(token_grad * own_gain * unpack(state[...]), axis=1, keepdims=True)
    spread = jnp.where(place == 2, inner, spread)
    gate_o[...] = jnp.transpose(spread)[:8]


def combine(returned, meta, state, cot, gains):
    out = (
        shape(LOCAL, SEQ),
        shape(SEQ, LOCAL, dtype=F32),
        shape(8, SEQ, dtype=F32),
    )
    return local_call(combine_body, "VBVBB", (returned, meta, state, cot, gains), "BVV", out)


def router_body(gate, tg, state, cot, meta, wp, gains, router, gp_o, grad_o, dr_o, small_o):
    whole = join(wp).astype(F32)
    gain = gain_row(gains, 3)
    normed, scale = normalise(whole, gain)
    summed = gate[0] + gate[1] + gate[2] + gate[3]
    wide = jnp.concatenate([summed, jnp.zeros((120, SEQ), F32)], axis=0)
    turned = jnp.transpose(wide)
    gates = [meta[:, r : r + 1] for r in range(2)]
    gate_grad = [turned[:, r : r + 1] for r in range(2)]
    inner = gates[0] * gate_grad[0] + gates[1] * gate_grad[1]
    routes = meta[:, 4:6].astype(jnp.int32)
    logit_grad = jnp.zeros((SEQ, 64), F32)
    for r in range(2):
        picked_grad = gates[r] * (gate_grad[r] - inner)
        logit_grad = logit_grad + jnp.where(marks_of(routes, r), picked_grad, 0.0)
    logit_grad = logit_grad.astype(BF)
    dr_o[...] = dot(normed, logit_grad, 0, 0).astype(BF)
    gy = lax.axis_index("gy")
    term = dot(logit_grad, router[...], 1, 1)
    inner = turned[:, 2:3] + jnp.sum(term * gain * whole, axis=1, keepdims=True)
    own_router = router[pl.ds(pl.multiple_of(gy * LOCAL, LOCAL), LOCAL), :]
    ng = tg[...] + dot(logit_grad, own_router, 1, 1)
    own_gain = gains[gy, 3:4, :LOCAL]
    entered = unpack(state[...])
    state_grad = ng * own_gain * scale - entered * (scale * scale * scale * inner * (1.0 / D))
    gain_part = jnp.sum(ng * entered * scale, axis=0, keepdims=True)
    small_o[...] = jnp.zeros((8, D), F32)
    small_o[4:5, :] = jnp.concatenate(
        [jnp.where(gy == j, gain_part, 0.0) for j in range(4)], axis=1
    )
    grad = pack(jnp.transpose(cot[...].astype(F32)) + state_grad)
    grad_o[...] = grad
    gp_o[...] = grad.astype(BF)


def router_bwd(gate, tg, state, cot, meta, wp, gains, router):
    out = (
        shape(HALF, PACK),
        shape(HALF, PACK, dtype=F32),
        shape(D, 64),
        shape(8, D, dtype=F32),
    )
    return local_call(
        router_body, "VVVBBBBB", (gate, tg, state, cot, meta, wp, gains, router), "VVBB", out, vmem=50
    )


def places_of():
    gx, gy = lax.axis_index("gx"), lax.axis_index("gy")
    return gx, gy, gx // 8, (gx // 2) % 4, gx % 2


def at(y, z, core):
    return (y * 4 + z) * 2 + core


def greet(peers):
    barrier = pltpu.get_barrier_semaphore()
    for peer in peers:
        pl.semaphore_signal(barrier, inc=1, device_id=peer, device_id_type=MESH)
    pl.semaphore_wait(barrier, len(peers))


def remote(src, dst, send, recv, peer):
    return pltpu.make_async_remote_copy(
        src_ref=src, dst_ref=dst, send_sem=send, recv_sem=recv, device_id=peer, device_id_type=MESH
    )


def gy_peers(gx, gy):
    return [(gx, (gy + d) % 4) for d in (1, 2, 3)]


def grid_peers(gx, gy, y, z, core):
    return (
        [(at((y + d) % 4, z, core), gy) for d in (1, 2, 3)]
        + [(at(y, (z + d) % 4, core), gy) for d in (1, 2, 3)]
        + [(at(y, z, 1 - core), gy)]
    )


def comm_call(body, out, args, scratch, collective_id, specs, out_specs, vmem=16):
    return pl.pallas_call(
        body,
        out_shape=out,
        in_specs=specs,
        out_specs=out_specs,
        scratch_shapes=scratch,
        compiler_params=pltpu.CompilerParams(
            collective_id=collective_id, has_side_effects=True, vmem_limit_bytes=vmem * 2**20
        ),
    )(*args)


class Pool:
    def __init__(self, sems):
        self.sems, self.count = sems, 0

    def take(self):
        self.count += 1
        return self.sems.at[self.count - 1]

    def send(self, src, dst, peer):
        copy = remote(src, dst, self.take(), self.take(), peer)
        copy.start()
        return copy

    def keep(self, src, dst):
        copy = pltpu.make_async_copy(src, dst, self.take())
        copy.start()
        return copy


def together(pieces):
    pieces = list(pieces)
    while pieces:
        pieces = [p for p in pieces if next(p, False) is None]


def gather_weight(pool, w, out, z_first):
    gx, gy, y, z, core = places_of()
    mine = y if z_first else z
    partner = (at(y, z, 1 - core), gy)

    def line(k):
        return out.at[k, :, core] if z_first else out.at[:, k, core]

    def across(d, along_z):
        return (at(y, (z + d) % 4, core) if along_z else at((y + d) % 4, z, core), gy)

    own = pool.keep(w, out.at[y, z, core])
    first = [pool.send(w, out.at[y, z, core], across(d, z_first)) for d in (1, 2, 3)]
    yield
    own.wait()
    for copy in first:
        copy.wait_recv()
    second = [pool.send(line(mine), line(mine), across(d, not z_first)) for d in (1, 2, 3)]
    third = [pool.send(line(mine), line(mine), partner)]
    yield
    for d in (1, 2, 3):
        second[d - 1].wait_recv()
        block = line((mine + 4 - d) % 4)
        third.append(pool.send(block, block, partner))
    yield
    for copy in first + second:
        copy.wait_send()
    for copy in third:
        copy.wait()


def reduce_weight(pool, part, out, y_first, got1, sum1, got2, sum2, got3):
    gx, gy, y, z, core = places_of()
    own = pool.keep(part.at[:, :, core], sum1)
    first = pool.send(part.at[:, :, 1 - core], got1, (at(y, z, 1 - core), gy))
    yield
    own.wait()
    first.wait_recv()
    sum1[...] = (sum1[...].astype(F32) + got1[...].astype(F32)).astype(BF)
    second, third = [], []
    for d in (1, 2, 3):
        if y_first:
            there = (y + d) % 4
            src, peer = sum1.at[there], (at(there, z, core), gy)
        else:
            there = (z + d) % 4
            src, peer = sum1.at[:, there], (at(y, there, core), gy)
        second.append(pool.send(src, got2.at[d - 1], peer))
    yield
    for copy in second:
        copy.wait_recv()
    value = (sum1[y] if y_first else sum1[:, z]).astype(F32)
    for d in range(3):
        value = value + got2[d].astype(F32)
    sum2[...] = value.astype(BF)
    for d in (1, 2, 3):
        there = (z + d) % 4 if y_first else (y + d) % 4
        peer = (at(y, there, core) if y_first else at(there, z, core), gy)
        third.append(pool.send(sum2.at[there], got3.at[d - 1], peer))
    yield
    for copy in third:
        copy.wait_recv()
    value = (sum2[z] if y_first else sum2[y]).astype(F32)
    for d in range(3):
        value = value + got3[d].astype(F32)
    out[...] = value
    for copy in [first] + second + third:
        copy.wait_send()


def reduce_scratch(w):
    return [
        pltpu.VMEM((4, 4, ROWS, w), BF),
        pltpu.VMEM((4, 4, ROWS, w), BF),
        pltpu.VMEM((3, 4, ROWS, w), BF),
        pltpu.VMEM((4, ROWS, w), BF),
        pltpu.VMEM((3, ROWS, w), BF),
    ]


def start_rows(pool, x, gain, xw, gw, state, raw, packed, load):
    gx, gy = lax.axis_index("gx"), lax.axis_index("gy")
    copies = []

    def spread(src, dst):
        copies.extend(pool.send(src, dst.at[gy], (gx, (gy + d) % 4)) for d in (2, 1, 3))
        copies.append(pool.keep(src, dst.at[gy]))

    load.wait()
    packed[...] = pack(raw[...])
    spread(packed, xw)
    spread(gain, gw)
    state[...] = packed[...].astype(F32)
    yield
    for copy in copies:
        copy.wait()


def start_body(w, x, gain, w_all, xw, gw, state, raw, packed, sems):
    gx, gy, y, z, core = places_of()
    pool = Pool(sems)
    halves = [pl.ds(0, D // 2), pl.ds(D // 2, D // 2)]
    load = pool.keep(x, raw)
    greet(grid_peers(gx, gy, y, z, core) + gy_peers(gx, gy))
    together(
        [
            *[
                gather_weight(
                    pool, w.at[:, half], w_all.at[:, :, :, :, half], half.start == 0
                )
                for half in halves
            ],
            start_rows(pool, x, gain, xw, gw, state, raw, packed, load),
        ]
    )


def start_gather(w, x, gain):
    out = (
        shape(4, 4, 2, *w.shape),
        shape(4, HALF, PACK),
        shape(4, 8, 256, dtype=F32),
        shape(HALF, PACK, dtype=F32),
    )
    scratch = [pltpu.VMEM((SEQ, LOCAL), BF), pltpu.VMEM((HALF, PACK), BF), DMA((96,))]
    return comm_call(start_body, out, (w, x, gain), scratch, 0, [HB] * 3, (HB, HB, HB, VM))


def turn_rows(pool, pick, pp, local, new, out, via, recv):
    gx, gy = lax.axis_index("gx"), lax.axis_index("gy")
    there, far = [(gy + 1) % 4, (gy + 3) % 4], (gy + 2) % 4
    beside = [(gx, there[0]), (gx, there[1])]
    size = HALF // 2
    rows = [pl.ds(0, size), pl.ds(size, size)]
    passed = [pool.send(pp.at[far, rows[k]], via.at[k], beside[k]) for k in range(2)]
    direct = [
        pool.send(pp.at[there[k], rows[1 - k]], recv.at[k, rows[1 - k]], beside[k])
        for k in range(2)
    ]
    yield
    for k in range(2):
        half = rows[k]
        passed[k].wait_recv()
        via[k] = (via[k].astype(F32) + pp[there[k], half].astype(F32)).astype(BF)
        direct.append(pool.send(via.at[k], recv.at[k, half], beside[k]))
    yield
    sends = [None] * 4
    for k in range(2):
        half = rows[k]
        direct[1 - k].wait_recv()
        direct[2 + k].wait_recv()
        base = local[gy, half] if pick else local[half]
        total = base + pp[gy, half].astype(F32)
        total = total + recv[0, half].astype(F32) + recv[1, half].astype(F32)
        new[half] = total
        out[gy, half] = total.astype(BF)
        for to in (k, 1 - k):
            block = out.at[gy, half]
            sends[2 * to + k] = pool.send(block, block, beside[to])
    yield
    onward = []
    for k in range(2):
        sends[2 * k + k].wait_recv()
        block = out.at[there[1 - k], rows[k]]
        onward.append(pool.send(block, block, beside[k]))
    yield
    for k in range(2):
        sends[2 * k + 1 - k].wait_recv()
    for copy in onward:
        copy.wait()
    for copy in passed + direct + sends:
        copy.wait_send()


def turn_body(pick, n_gather, n_reduce, *refs):
    n = 2 + n_gather + n_reduce
    pp, local = refs[:2]
    extra, (new, out) = refs[2:n], refs[n : n + 2]
    made = refs[n + 2 : 2 * n]
    via, recv = refs[2 * n : 2 * n + 2]
    scratch, sems = refs[2 * n + 2 : -1], refs[-1]
    gx, gy, y, z, core = places_of()
    pool = Pool(sems)
    greet(
        [(gx, (gy + 1) % 4), (gx, (gy + 3) % 4)]
        + (grid_peers(gx, gy, y, z, core) if n_gather + n_reduce else [])
    )
    pieces = [turn_rows(pool, pick, pp, local, new, out, via, recv)]
    for i in range(n_gather):
        pieces.append(gather_weight(pool, extra[i], made[i], i % 2 == 0))
    for i in range(n_reduce):
        pieces.append(
            reduce_weight(pool, extra[i], made[i], i % 2 == 0, *scratch[5 * i : 5 * i + 5])
        )
    together(pieces)


def turn(collective_id, pp, local, gather=(), reduce=()):
    out = [shape(HALF, PACK, dtype=F32), shape(4, HALF, PACK)]
    out += [shape(4, 4, 2, *w.shape) for w in gather]
    out += [shape(ROWS, p.shape[-1], dtype=F32) for p in reduce]
    reduce = [p.reshape(4, 4, 2, ROWS, p.shape[-1]) for p in reduce]
    scratch = [pltpu.VMEM((2, HALF // 2, PACK), BF), pltpu.VMEM((2, HALF, PACK), BF)]
    for p in reduce:
        scratch += reduce_scratch(p.shape[-1])
    made = comm_call(
        functools.partial(turn_body, local.ndim == 3, len(gather), len(reduce)),
        tuple(out),
        (pp, local, *gather, *reduce),
        scratch + [DMA((96,))],
        collective_id,
        [VM, VM] + [HB] * (len(gather) + len(reduce)),
        tuple([VM, VM] + [HB] * len(gather) + [VM] * len(reduce)),
    )
    kept = [m.reshape(D, m.shape[-1]) for m in made[2 : 2 + len(gather)]]
    return [*made[:2], *kept, *made[2 + len(gather) :]]


def gather_body(src, dst, sx, rx):
    gx, gy = lax.axis_index("gx"), lax.axis_index("gy")
    greet(gy_peers(gx, gy))
    copies = []
    for d in (2, 1, 3):
        copy = remote(src, dst.at[gy], sx.at[d - 1], rx.at[d - 1], (gx, (gy + d) % 4))
        copy.start()
        copies.append(copy)
    dst[gy] = src[...]
    for copy in copies:
        copy.wait()


def gather(collective_id, a):
    return comm_call(
        gather_body,
        shape(4, *a.shape, dtype=a.dtype),
        (a,),
        [DMA((3,)), DMA((3,))],
        collective_id,
        [VM],
        VM,
    )


AHEAD = 16
LAG = 8


def to_experts_body(sent, out, own, sa, ra, sg, rg, sf, rf):
    gx, gy, y, z, core = places_of()
    there = [(gy + 1) % 4, (gy + 3) % 4]
    far = (gy + 2) % 4
    beside = [(gx, there[0]), (gx, there[1])]
    greet(beside + [((gx + k) % 32, gy) for k in range(1, 32)])
    keep = pltpu.make_async_copy(sent.at[gx], out.at[gy, gx], own)
    keep.start()

    def shift(k, sign):
        far_y, far_z, far_core = k // 8, (k // 2) % 4, k % 2
        return at((y + 4 + sign * far_y) % 4, (z + 4 + sign * far_z) % 4, (core + far_core) % 2)

    def push(k):
        peer = shift(k, 1)
        remote(sent.at[peer], out.at[gy, gx], sa, ra.at[k], (peer, gy)).start()

    def spread(k):
        block = out.at[gy, shift(k, -1)]
        for to in range(2):
            remote(block, block, sg.at[to], rg.at[to, k], beside[to]).start()

    def arrive(k):
        remote(sent.at[0], out.at[gy, shift(k, -1)], sa, ra.at[k], beside[0]).wait_recv()
        spread(k)

    def relay(k, to):
        source = shift(k, -1)
        for way in range(2):
            block = out.at[there[1 - way], source]
            remote(block, block, sg.at[way], rg.at[way, k], beside[way]).wait_recv()
        block = out.at[there[1 - to], source]
        remote(block, block, sf.at[to], rf.at[to], beside[to]).start()

    for k in range(1, AHEAD):
        push(k)
    keep.wait()
    spread(0)
    for k in range(1, LAG):
        arrive(k)

    def step(i, carry):
        for to in range(2):
            k = LAG + 2 * i + to

            @pl.when(k + AHEAD - LAG < 32)
            def _():
                push(k + AHEAD - LAG)

            arrive(k)
            relay(k - LAG, to)
        return carry

    lax.fori_loop(0, (32 - LAG) // 2, step, 0)
    for k in range(32 - LAG, 32):
        relay(k, k % 2)
    many = sent.at[pl.ds(0, 31)]
    remote(many, many, sa, ra.at[0], beside[0]).wait_send()
    for to in range(2):
        half = out.at[far, pl.ds(0, 16)]
        remote(half, half, sf.at[to], rf.at[to], beside[to]).wait()
        remote(out.at[gy], out.at[gy], sg.at[to], rg.at[to, 0], beside[to]).wait_send()


def to_experts(sent):
    return comm_call(
        to_experts_body,
        shape(4, 32, SLOT, PACK),
        (sent,),
        [
            DMA(()),
            DMA(()),
            DMA((32,)),
            DMA((2,)),
            DMA((2, 32)),
            DMA((2,)),
            DMA((2,)),
        ],
        8,
        [VM],
        VM,
        vmem=12,
    )


GROUPS = 8
BEGUN = 4


def from_experts_body(back, out, via, part, recv, total, sems, s4, r4):
    gx, gy = lax.axis_index("gx"), lax.axis_index("gy")
    there = [(gy + 1) % 4, (gy + 3) % 4]
    far = (gy + 2) % 4
    beside = [(gx, there[0]), (gx, there[1])]
    greet(beside + [((gx + k) % 32, gy) for k in range(1, 32)])
    pool = Pool(sems)
    passing, direct, summed = [], [], []

    def place(c):
        return (c + gx) % GROUPS

    def begin(c):
        to = c % 2
        passing.append(pool.send(back.at[far, :, place(c)], via.at[c], beside[to]))
        direct.append(
            pool.send(back.at[there[1 - to], :, place(c)], recv.at[1 - to, c], beside[1 - to])
        )

    def middle(c):
        to = c % 2
        passing[c].wait_recv()
        value = back[there[to], :, place(c)].astype(F32) + via[c].astype(F32)
        part[c] = value.astype(BF)
        summed.append(pool.send(part.at[c], recv.at[to, c], beside[to]))

    def end(c):
        direct[c].wait_recv()
        summed[c].wait_recv()
        value = back[gy, :, place(c)].astype(F32)
        value = value + recv[0, c].astype(F32) + recv[1, c].astype(F32)
        total[:, place(c)] = value.astype(BF)
        for i in range(4):
            peer = i * GROUPS + place(c)

            @pl.when(peer != gx)
            def _():
                remote(
                    total.at[i, place(c)],
                    out.at[gx // GROUPS, gx % GROUPS],
                    s4.at[peer],
                    r4.at[gx],
                    (peer, gy),
                ).start()

            @pl.when(peer == gx)
            def _():
                out[gx // GROUPS, gx % GROUPS] = total[i, place(c)]

    for c in range(BEGUN):
        begin(c)
    middle(0)
    middle(1)
    for c in range(GROUPS):
        if c + BEGUN < GROUPS:
            begin(c + BEGUN)
        if c + 2 < GROUPS:
            middle(c + 2)
        end(c)
    for copy in passing + direct + summed:
        copy.wait_send()

    def finish(k, carry):
        source = (gx + k) % 32
        remote(
            total.at[0, 0],
            out.at[source // GROUPS, source % GROUPS],
            s4.at[source],
            r4.at[source],
            beside[0],
        ).wait()
        return carry

    lax.fori_loop(1, 32, finish, 0)


def from_experts(back):
    full = (4, GROUPS, SLOT, PACK)
    return comm_call(
        from_experts_body,
        shape(*full),
        (back.reshape(4, *full),),
        [
            pltpu.VMEM((GROUPS, 4, SLOT, PACK), BF),
            pltpu.VMEM((GROUPS, 4, SLOT, PACK), BF),
            pltpu.VMEM((2, GROUPS, 4, SLOT, PACK), BF),
            pltpu.VMEM(full, BF),
            DMA((48,)),
            DMA((32,)),
            DMA((32,)),
        ],
        9,
        [VM],
        VM,
        vmem=16,
    ).reshape(32, SLOT, PACK)


def last_rows(pool, pp, local, grad_o, recv):
    gx, gy = lax.axis_index("gx"), lax.axis_index("gy")
    copies = [
        pool.send(pp.at[(gy + d) % 4], recv.at[d - 1], (gx, (gy + d) % 4)) for d in (2, 1, 3)
    ]
    yield
    yield
    for copy in copies:
        copy.wait_recv()
    total = local[...] + pp[gy].astype(F32)
    for d in range(3):
        total = total + recv[d].astype(F32)
    grad_o[...] = unpack(total).astype(BF)
    for copy in copies:
        copy.wait_send()


def last_small(pool, raw, loads, bias_o, gain_o, got, held):
    gx, gy, y, z, core = places_of()
    for copy in loads:
        copy.wait()
    held[0, 0:8] = raw[0] + raw[1]
    held[0, 8:16] = raw[2] + raw[3]
    groups = [
        [(at(y, z, 1 - core), gy)],
        [(at((y + d) % 4, z, core), gy) for d in (1, 2, 3)],
        [(at(y, (z + d) % 4, core), gy) for d in (1, 2, 3)],
        gy_peers(gx, gy),
    ]
    copies = []
    for stage, peers in enumerate(groups):
        now = [
            pool.send(held.at[stage], got.at[3 * stage + k], peer) for k, peer in enumerate(peers)
        ]
        copies += now
        yield
        value = held[stage]
        for k, copy in enumerate(now):
            copy.wait_recv()
            value = value + got[3 * stage + k]
        if stage < 3:
            held[stage + 1] = value
    bias_o[...] = held[3, 0:8, :128]
    for j in range(4):

        @pl.when(gy == j)
        def _():
            for k, row in enumerate((0, 8, 4, 12)):
                gain_o[k : k + 1, :] = value[row : row + 1, LOCAL * j : LOCAL * (j + 1)]

    for copy in copies:
        copy.wait_send()


def last_body(part, pp, local, a, b, c, d, out, grad_o, bias_o, gain_o, *scratch):
    pieces, (raw, recv, got, held, sems) = (scratch[:5], scratch[5:10]), scratch[10:]
    halves = [pl.ds(0, D // 2), pl.ds(D // 2, D // 2)]
    gx, gy, y, z, core = places_of()
    pool = Pool(sems)
    loads = [pool.keep(src, raw.at[k]) for k, src in enumerate((a, b, c, d))]
    greet(grid_peers(gx, gy, y, z, core) + gy_peers(gx, gy))
    together(
        [
            *[
                reduce_weight(
                    pool, part.at[:, :, :, :, half], out.at[:, half], half.start == 0, *piece
                )
                for half, piece in zip(halves, pieces)
            ],
            last_rows(pool, pp, local, grad_o, recv),
            last_small(pool, raw, loads, bias_o, gain_o, got, held),
        ]
    )


def last_sums(part, pp, local, smalls):
    out = (
        shape(ROWS, D, dtype=F32),
        shape(SEQ, LOCAL),
        shape(8, 128, dtype=F32),
        shape(4, LOCAL, dtype=F32),
    )
    scratch = reduce_scratch(D // 2) * 2 + [
        pltpu.VMEM((4, 8, D), F32),
        pltpu.VMEM((3, HALF, PACK), BF),
        pltpu.VMEM((12, 16, D), F32),
        pltpu.VMEM((4, 16, D), F32),
        DMA((96,)),
    ]
    return comm_call(
        last_body,
        out,
        (part.reshape(4, 4, 2, ROWS, D), pp, local, *smalls),
        scratch,
        6,
        [HB, VM, VM] + [HB] * 4,
        (VM,) * 4,
    )


def shards(
    block_input,
    cotangent,
    doc_ids,
    routes,
    qkv_weight,
    out_weight,
    rel_bias,
    norm_gain,
    ff_in,
    ff_out,
    router,
    expert_in,
    expert_out,
):
    picks = jnp.asarray(bucket_picks())
    doc = doc_ids.reshape(1, SEQ)
    layers = [
        jnp.concatenate([qkv_weight[l].reshape(ROWS, 576), out_weight[l]], axis=1)
        for l in range(2)
    ]
    gain_wide = jnp.pad(norm_gain.reshape(4, LOCAL), ((0, 4), (0, 64)))
    w0, xw, gains, state = start_gather(layers[0], block_input, gain_wide)
    w0 = w0.reshape(D, D)
    pp, *kept0 = attn_fwd(0, xw, "B", gains, w0, rel_bias, picks, doc)
    state, sw1, w_in, w_out = turn(1, pp, state, gather=(ff_in, ff_out))
    pp, pre = ff_fwd(sw1, gains, w_in, w_out)
    state, sw2, w1, w_router = turn(2, pp, state, gather=(layers[1], router))
    pp, *kept1 = attn_fwd(1, sw2, "V", gains, w1, rel_bias, picks, doc)
    state, sw3 = turn(3, pp, state)
    cot = cotangent.T
    sent, meta = dispatch(sw3, state, cot, gains, w_router, routes.T)
    arrived = to_experts(sent)
    back, expert_in_grad, expert_out_grad = expert(arrived, expert_in, expert_out)
    returned = from_experts(back)
    block_output, tg, gate = combine(returned, meta, state, cot, gains)
    block_output = block_output.T
    gp, grad, d_router, small3 = router_bwd(
        gather(7, gate), tg, state, cot, meta, sw3, gains, w_router
    )
    gp = gather(10, gp)
    pp, d_w1, small2 = attn_bwd(1, gp, sw2, gains, w1, *kept1, picks)
    grad, gp, g1, router_grad = turn(4, pp, grad, reduce=(d_w1, d_router))
    pp, d_in, d_out, small1 = ff_bwd(gp, sw1, gains, w_in, w_out, pre)
    grad, gp, ff_in_grad, ff_out_grad = turn(5, pp, grad, reduce=(d_in, d_out))
    pp, d_w0, small0 = attn_bwd(0, gp, xw, gains, w0, *kept0, picks)
    g0, input_grad, bias, gain_grad = last_sums(d_w0, pp, grad, (small0, small2, small1, small3))
    both = jnp.stack([g0, g1])
    qkv_grad = both[:, :, :576].reshape(2, ROWS, 3, LOCAL)
    out_grad = both[:, :, 576:]
    bias_grad = bias.reshape(2, 4, 128)[:, 1:, :NB]
    gain_grad = gain_grad.reshape(2, 2, LOCAL)
    return (
        block_output,
        input_grad,
        qkv_grad,
        out_grad,
        bias_grad,
        gain_grad,
        ff_in_grad,
        ff_out_grad,
        router_grad,
        expert_in_grad,
        expert_out_grad,
    )


def solution(mesh):
    in_specs = (
        P("gx", "gy"),
        P("gx", "gy"),
        P("gx"),
        P("gx", None),
        P(None, "gx", None, "gy"),
        P(None, "gx", "gy"),
        P(None, "gy", None),
        P(None, None, "gy"),
        P("gx", "gy"),
        P("gx", "gy"),
        P("gx", None),
        P("gx", None, "gy"),
        P("gx", "gy", None),
    )
    out_specs = (
        P("gx", "gy"),
        P("gx", "gy"),
        P(None, "gx", None, "gy"),
        P(None, "gx", "gy"),
        P(None, "gy", None),
        P(None, None, "gy"),
        P("gx", "gy"),
        P("gx", "gy"),
        P("gx", None),
        P("gx", None, "gy"),
        P("gx", "gy", None),
    )
    return jax.shard_map(shards, mesh=mesh, in_specs=in_specs, out_specs=out_specs, check_vma=False)
```
